512 devices in a mesh: sec: 16 (over z), slab: 32 (over y, x, core).
Axes of the slice: x: 4, y: 4, z: 16, core: 2. Of those that a mesh axis runs over, the one named last changes fastest.
Arguments:
- heat_level: float32 [16, 128, 64, 128], P('sec', 'slab'), may hold values from -6 to 6
- material_factor: float32 [16, 128, 64, 128], P('sec', 'slab'), may hold values from 0.4 to 1.2
- dual_sensitivity: float32 [16, 128, 64, 128], P('sec', 'slab'), may hold values from -6 to 6
- source_liquid_part: int32 [4, 48, 1], replicated, may hold values from 0 to 11; in each aligned block of 48 rows (0 to 47, 48 to 95, ..., all dimensions but the last counted through in order) at most 8 rows name the same one
- source_liquid_line: int32 [4, 48], replicated, may hold values from 0 to 63
- solid_touch_flag: int32 [4, 48], replicated, may hold values 0 or 1
- archived_instant: int32 [1], replicated, may hold values from 0 to 63
Outputs:
- state_field: float32 [16, 128, 64, 128], P('sec', 'slab')
- adjoint_field: float32 [16, 128, 64, 128], P('sec', 'slab')
The draws below stay inside these ranges and needn't reach their ends.
Inputs may be any that keep to these rules, and one draw needn't show every extreme that they name: `source_liquid_part`: among the 48 rows of one ingot section no melt section is named more than 8 times, and in some ingot section one melt section is named exactly 8 times.
All inputs are finite; a program needn't handle non-finite values.
Results may differ from the reference program's by a relative error of at most 0.0002.
Values sent between devices are 32-bit elements; how exact they have to be, the bound alone decides.
A program may use at most 64 MiB of HBM per device.

```python
import math
import jax
import jax.numpy as jnp
import numpy as np

PART_HEIGHT = 64
PART_WIDTH = 128
STEPS = 4
ITERS = 4
PAIRCAP = 8
LIQUID_PARTS = 12
NI = 4
TOUCHING_LINES = 48
PART_DEPTH = 128
N_SEC = 16


def touch_ends(entries, stream_key, low, top_value):
    spot = [jax.random.randint(jax.random.fold_in(stream_key, axis), (), 0, length) for axis, length in enumerate(entries.shape)]
    main_axis = entries.shape.index(max(entries.shape))
    neighbour = spot[:main_axis] + [(spot[main_axis] + 1) % entries.shape[main_axis]] + spot[main_axis + 1:]
    return entries.at[tuple(spot)].set(low).at[tuple(neighbour)].set(top_value)


def level_of(own_key, shape, pieces, low, top_value):
    def one(dim, shards_of):
        heights = jax.random.uniform(jax.random.fold_in(jax.random.fold_in(own_key, 6), dim), (shards_of,), jnp.float32, low / len(pieces), top_value / len(pieces))
        return jnp.repeat(jnp.exp(heights), shape[dim] // shards_of).reshape((-1,) + (1,) * (len(shape) - dim - 1))

    loudness = one(*pieces[0])
    for cut in pieces[1:]:
        loudness = loudness * one(*cut)
    return loudness


def routed_block(rng, own, number, rows, number_of, top, limit, lean):
    order = jax.random.permutation(rng, number_of)
    heavy_load, common = load_shares(number_of, rows * top, limit, lean, True), load_shares(number_of, rows * top, limit, lean, False)
    places = jnp.arange(number_of)

    def named(sizes, offset_by):
        used = int((sizes > 0).sum())
        fixed = max(1, used // 4)
        shifted = fixed + (places - fixed + offset_by * (used - fixed)) % max(1, number_of - fixed)
        return jnp.zeros((number_of,), jnp.int32).at[order[jnp.where(places < fixed, places, shifted)]].set(jnp.asarray(sizes, jnp.int32))

    sizes = jnp.where(number % 4 == 0, named(heavy_load, number // 4), named(common, number - number // 4 - 1))
    mixed = jax.random.permutation(jax.random.fold_in(own, 3), number_of)
    donor, receiver = mixed[0:number_of // 2 * 2:2], mixed[1:number_of // 2 * 2:2]
    slack = jnp.minimum(sizes[donor] - 1, limit - sizes[receiver]) // 2
    slack = jnp.where((donor == order[0]) | (receiver == order[0]) | (sizes[receiver] == 0), 0, jnp.maximum(slack, 0))
    shifted = jax.random.randint(jax.random.fold_in(own, 4), (number_of // 2,), 0, 1 << 20) % (slack + 1)
    sizes = sizes.at[donor].add(-shifted).at[receiver].add(shifted)
    members = jnp.searchsorted(jnp.cumsum(sizes), jnp.arange(rows * top), side="right").astype(jnp.int32)
    listing = members.reshape(top, rows).T
    listing = listing[jax.random.permutation(jax.random.fold_in(own, 1), rows)]
    offset_by = jax.random.randint(jax.random.fold_in(own, 2), (rows, 1), 0, top)
    return jnp.take_along_axis(listing, (jnp.arange(top)[None, :] + offset_by) % top, axis=1)


def load_shares(count, total, most, skew, full):
    loads = [(1 << 20) // math.isqrt(rank ** skew) + 1 for rank in range(1, count + 1)]
    largest = most if full else min(most, max(-(-total // count), total * loads[0] // sum(loads)))
    least = 1 if total - largest >= count - 1 else 0
    counts, rest = [largest] + [least] * (count - 1), total - largest - least * (count - 1)
    while rest > 0:
        movable = [i for i in range(1, count) if counts[i] < largest] or [i for i in range(1, count) if counts[i] < most]
        whole, remaining = sum([loads[i] for i in movable]), rest
        for i in movable:
            more = min(most - counts[i], max(1, remaining * loads[i] // whole), rest)
            counts[i] = counts[i] + more
            rest = rest - more
    return np.array(counts)


def gaussian(own_key, shape, deviation, reach, pieces=(), held_as=jnp.bfloat16):
    entries = deviation * jax.random.normal(own_key, shape, jnp.float32)
    if pieces:
        entries = entries * level_of(own_key, shape, pieces, -0.22, 0.18)
    return jnp.clip(entries, -reach, reach).astype(held_as)


def setup_inputs(seed: int = 0) -> dict:
    keys = jax.random.split(jax.random.key(seed), 8)
    heat_level = gaussian(keys[0], (N_SEC, PART_DEPTH, PART_HEIGHT, PART_WIDTH), 1.0, 6.0, ((0, 16), (1, 32)), jnp.float32)
    material_factor = jnp.clip(0.4 + 0.800000042 * jax.random.uniform(keys[1], (N_SEC, PART_DEPTH, PART_HEIGHT, PART_WIDTH), jnp.float32) ** level_of(keys[1], (N_SEC, PART_DEPTH, PART_HEIGHT, PART_WIDTH), ((0, 16), (1, 32)), -0.2, 0.2), 0.4, 1.2)
    dual_sensitivity = gaussian(keys[2], (N_SEC, PART_DEPTH, PART_HEIGHT, PART_WIDTH), 1.0, 6.0, ((0, 16), (1, 32)), jnp.float32)
    source_liquid_part_keys = jax.random.split(jax.random.fold_in(keys[3], 1), NI * TOUCHING_LINES // TOUCHING_LINES)
    source_liquid_part_turns = jax.random.permutation(jax.random.fold_in(keys[3], 3), NI * TOUCHING_LINES // TOUCHING_LINES)
    source_liquid_part = jax.vmap(lambda own, number: routed_block(jax.random.fold_in(keys[3], 2), own, number, TOUCHING_LINES, LIQUID_PARTS, 1, PAIRCAP, 2))(source_liquid_part_keys, source_liquid_part_turns).reshape((NI, TOUCHING_LINES, 1))
    source_liquid_line = touch_ends(jax.random.randint(keys[4], (NI, TOUCHING_LINES), 0, PART_HEIGHT), jax.random.fold_in(keys[4], 1), 0, PART_HEIGHT - 1).astype(jnp.int32)
    solid_touch_flag = touch_ends((jax.random.randint(keys[5], (NI, TOUCHING_LINES), 0, 4) < 3).astype(jnp.int32), jax.random.fold_in(keys[5], 1), 0, 1)
    archived_instant = jax.random.randint(keys[6], (1,), 0, 64).astype(jnp.int32)
    return dict(heat_level=heat_level, material_factor=material_factor, dual_sensitivity=dual_sensitivity, source_liquid_part=source_liquid_part, source_liquid_line=source_liquid_line, solid_touch_flag=solid_touch_flag, archived_instant=archived_instant)


time_step = 0.1
sink_rate = 0.5
period_steps = 16.0


def pad_planes(values):
    widths = [(0, 0)] * (values.ndim - 3) + [(1, 1), (0, 0), (0, 0)]
    return jnp.pad(values, widths)


def neighbor_sum(padded):
    center = padded[..., 1:-1, :, :]
    widths = [(0, 0)] * (center.ndim - 2) + [(1, 1), (1, 1)]
    plane_cycle = jnp.pad(center, widths)
    total = padded[..., 2:, :, :] + padded[..., :-2, :, :]
    total = total + plane_cycle[..., 2:, 1:-1] + plane_cycle[..., :-2, 1:-1]
    return total + plane_cycle[..., 1:-1, 2:] + plane_cycle[..., 1:-1, :-2]


def pull_speed(archived_instant, substep):
    phase = archived_instant[0].astype(jnp.float32) + substep
    return 1.0 + 0.5 * jnp.sin(2.0 * math.pi * phase / period_steps)


def melt_advance(padded, factor, velocity):
    center = padded[..., 1:-1, :, :]
    neighbors = neighbor_sum(padded)
    change = factor * (neighbors - 6.0 * center) - velocity * (center - padded[..., :-2, :, :])
    return center + time_step * change - time_step * sink_rate * jnp.tanh(center)


def melt_reverse(weighted_pad, adjoint_pad, melt_adjoint, earlier, velocity):
    weighted = weighted_pad[..., 1:-1, :, :]
    neighbors = neighbor_sum(weighted_pad)
    change = neighbors - 6.0 * weighted - velocity * (melt_adjoint - adjoint_pad[..., 2:, :, :])
    slope = 1.0 - jnp.tanh(earlier) ** 2
    return melt_adjoint + time_step * change - time_step * sink_rate * slope * melt_adjoint


def apply_operator(padded, factor):
    center = padded[..., 1:-1, :, :]
    return (6.0 + factor) * center - neighbor_sum(padded)


def conjugate(right_side, factor):
    def section_sum(values):
        return jnp.sum(values, axis=(1, 2, 3), keepdims=True)

    solution = jnp.zeros_like(right_side)
    residual = right_side
    direction = right_side
    norm_now = section_sum(residual * residual)
    for iteration in range(ITERS):
        applied = apply_operator(pad_planes(direction), factor)
        step_size = norm_now / section_sum(direction * applied)
        solution = solution + step_size * direction
        residual = residual - step_size * applied
        norm_next = section_sum(residual * residual)
        direction = residual + (norm_next / norm_now) * direction
        norm_now = norm_next
    return solution


def reference(heat_level, material_factor, dual_sensitivity, source_liquid_part, source_liquid_line, solid_touch_flag, archived_instant):
    melt_coef = material_factor[:LIQUID_PARTS]
    states = []
    current_entry = heat_level[:LIQUID_PARTS]
    for substep in range(STEPS):
        states.append(current_entry)
        current_entry = melt_advance(pad_planes(current_entry), melt_coef, pull_speed(archived_instant, substep))
    sections = source_liquid_part[:, :, 0]
    weight = solid_touch_flag.astype(jnp.float32)[:, :, None, None]
    picked = current_entry[sections, :, source_liquid_line, :]
    solid_interface = jnp.transpose(weight * picked, (0, 2, 1, 3))
    heat_strain_source = heat_level[LIQUID_PARTS:] + jnp.pad(solid_interface, ((0, 0), (0, 0), (0, PART_HEIGHT - TOUCHING_LINES), (0, 0)))
    ingot_coef = material_factor[LIQUID_PARTS:]
    displacement = conjugate(heat_strain_source, ingot_coef)
    adjoint_ingot = conjugate(dual_sensitivity[LIQUID_PARTS:], ingot_coef)
    sensitivity = weight * jnp.transpose(adjoint_ingot[:, :, :TOUCHING_LINES, :], (0, 2, 1, 3))
    returned = jnp.zeros_like(current_entry).at[sections, :, source_liquid_line, :].add(sensitivity)
    melt_adjoint = dual_sensitivity[:LIQUID_PARTS] + returned
    for substep in reversed(range(STEPS)):
        weighted = melt_coef * melt_adjoint
        melt_adjoint = melt_reverse(pad_planes(weighted), pad_planes(melt_adjoint), melt_adjoint, states[substep], pull_speed(archived_instant, substep))
    state_field = jnp.concatenate([current_entry, displacement], axis=0)
    adjoint_field = jnp.concatenate([melt_adjoint, adjoint_ingot], axis=0)
    return state_field, adjoint_field
```

```python
import functools
import math

import jax
import jax.numpy as jnp
from jax import lax
from jax.experimental import pallas as pl
from jax.experimental.pallas import tpu as pltpu
from jax.sharding import PartitionSpec as P

STEPS = 4
PAIRCAP = 8
BASIS = 4

time_step = 0.1
sink_rate = 0.5
period_steps = 16.0

CENTRE = 6.8
RADIUS = 6.4

MESH = pl.DeviceIdType.MESH
HIGHEST = lax.Precision.HIGHEST


def in_plane(c):
    rows, cols = c.shape
    row = lax.broadcasted_iota(jnp.int32, c.shape, 0)
    col = lax.broadcasted_iota(jnp.int32, c.shape, 1)
    up = jnp.where(row == 0, 0.0, pltpu.roll(c, 1, 0))
    down = jnp.where(row == rows - 1, 0.0, pltpu.roll(c, rows - 1, 0))
    left = jnp.where(col == 0, 0.0, pltpu.roll(c, 1, 1))
    right = jnp.where(col == cols - 1, 0.0, pltpu.roll(c, cols - 1, 1))
    return (up + down) + (left + right)


def fold(values):
    rows, cols = values.shape
    return jnp.sum(values.reshape(rows // 8, 8, cols), axis=0)


def coefficients(sums):
    total = jnp.broadcast_to(jnp.sum(sums, axis=1, keepdims=True), sums.shape)
    s = [total[k : k + 1, :] for k in range(8)]
    nu = [s[0], s[1], 2.0 * s[2] - s[0], 2.0 * s[3] - s[1], 2.0 * s[4] - s[0], 2.0 * s[5] - s[1], 2.0 * s[6] - s[0]]
    nu.append(4.0 * s[7] - 2.0 * s[5] - s[1])
    shift = 2.0 * CENTRE / RADIUS
    u = [shift * nu[k] + nu[k + 1] + nu[abs(k - 1)] for k in range(7)]
    mat = [[u[i + j] + u[abs(i - j)] for j in range(BASIS)] for i in range(BASIS)]
    diag = [mat[i][i] for i in range(BASIS)]
    rhs = [(4.0 / RADIUS) * nu[i] for i in range(BASIS)]
    inverse = []
    for k in range(BASIS):
        good = mat[k][k] > 1e-8 * diag[k]
        inv = jnp.where(good, 1.0 / jnp.where(good, mat[k][k], 1.0), 0.0)
        inverse.append(inv)
        for i in range(k + 1, BASIS):
            factor = mat[k][i] * inv
            for j in range(i, BASIS):
                mat[i][j] = mat[i][j] - factor * mat[k][j]
            rhs[i] = rhs[i] - factor * rhs[k]
    out = [None] * BASIS
    for i in reversed(range(BASIS)):
        value = rhs[i]
        for j in range(i + 1, BASIS):
            value = value - mat[i][j] * out[j]
        out[i] = value * inverse[i]
    return out


def kernel(
    n_sec,
    n_slab,
    group,
    part_ref,
    line_ref,
    flag_ref,
    instant_ref,
    heat_ref,
    factor_ref,
    dual_ref,
    state_ref,
    adjoint_ref,
    heat,
    coef,
    dual,
    a1,
    a2,
    a3,
    own,
    keep,
    mu_a,
    mu_b,
    w_a,
    w_b,
    pick,
    offered,
    slots,
    placed,
    back,
    returned,
    tile_a,
    tile_b,
    gather_a,
    gather_b,
    result,
    local_sem,
    out_sem,
    halo_send,
    halo_recv,
    row_send,
    row_recv,
    side_send,
    side_recv,
    sum_send_a,
    sum_send_b,
    sum_recv,
):
    ingots, contact = part_ref.shape
    melts = n_sec - ingots
    depth, height, width = heat_ref.shape
    first, last = depth, 2 * depth
    second = n_slab // group
    sec, slab = lax.axis_index("sec"), lax.axis_index("slab")
    is_melt = sec < melts
    has_left, has_right = slab > 0, slab < n_slab - 1
    low = jnp.where(has_left, 0, first)
    high = jnp.where(has_right, 3 * depth, last)

    loads = [
        pltpu.make_async_copy(src, dst.at[pl.ds(first, depth)], local_sem.at[i])
        for i, (src, dst) in enumerate(((heat_ref, heat), (factor_ref, coef), (dual_ref, dual)))
    ]
    for load in loads:
        load.start()

    barrier = pltpu.get_barrier_semaphore()

    def greet(to_sec, to_slab):
        pl.semaphore_signal(barrier, inc=1, device_id=(to_sec, to_slab), device_id_type=MESH)

    pl.when(has_left)(lambda: greet(sec, slab - 1))
    pl.when(has_right)(lambda: greet(sec, slab + 1))
    base = (slab // group) * group

    def peer_a(offset):
        return base + lax.rem(slab - base + offset, group)

    def peer_b(offset):
        return lax.rem(slab + offset * group, n_slab)

    beside = has_left.astype(jnp.int32) + has_right.astype(jnp.int32)

    @pl.when(is_melt)
    def _():
        for j in range(ingots):
            greet(melts + j, slab)

    @pl.when(jnp.logical_not(is_melt))
    def _():
        for m in range(melts):
            greet(m, slab)
        for offset in range(1, group):
            greet(sec, peer_a(offset))
        for offset in range(1, second):
            greet(sec, peer_b(offset))

    pl.semaphore_wait(barrier, beside + jnp.where(is_melt, ingots, melts + group - 1 + second - 1))

    def halo(src, dst, send, recv, lefts, rights):
        (left_src, left_dst), (right_src, right_dst) = lefts, rights
        to_left = pltpu.make_async_remote_copy(
            src_ref=src.at[left_src], dst_ref=dst.at[left_dst], send_sem=send.at[0], recv_sem=recv.at[1],
            device_id=(sec, slab - 1), device_id_type=MESH,
        )
        to_right = pltpu.make_async_remote_copy(
            src_ref=src.at[right_src], dst_ref=dst.at[right_dst], send_sem=send.at[1], recv_sem=recv.at[0],
            device_id=(sec, slab + 1), device_id_type=MESH,
        )
        return to_left, to_right

    def start(pair):
        pl.when(has_left)(lambda: pair[0].start())
        pl.when(has_right)(lambda: pair[1].start())

    def wait_recv(pair):
        pl.when(has_right)(lambda: pair[0].wait_recv())
        pl.when(has_left)(lambda: pair[1].wait_recv())

    def wait_send(pair):
        pl.when(has_left)(lambda: pair[0].wait_send())
        pl.when(has_right)(lambda: pair[1].wait_send())

    whole = (pl.ds(0, depth), pl.ds(last, depth)), (pl.ds(0, depth), pl.ds(0, depth))
    heat_halo = halo(heat_ref, heat, halo_send.at[0], halo_recv.at[0], *whole)
    coef_halo = halo(factor_ref, coef, halo_send.at[1], halo_recv.at[1], *whole)
    dual_halo = halo(dual_ref, dual, halo_send.at[2], halo_recv.at[2], *whole)

    zero = jnp.zeros((height, width), jnp.float32)

    def clear(bufs):
        @pl.when(jnp.logical_not(has_left))
        def _():
            for buf in bufs:
                buf[first - 1] = zero

        @pl.when(jnp.logical_not(has_right))
        def _():
            for buf in bufs:
                buf[last] = zero

    row_i = lax.broadcasted_iota(jnp.int32, (contact, contact), 0)
    lane_i = lax.broadcasted_iota(jnp.int32, (contact, contact), 1)

    def column(row):
        return jnp.sum(jnp.where(row_i == lane_i, row, 0.0), axis=1, keepdims=True)

    @pl.when(is_melt)
    def _():
        start(heat_halo)
        start(coef_halo)
        clear((heat, a1, a2, a3, dual, mu_a, mu_b, w_a, w_b))

        for j in range(ingots):
            named = part_ref[j : j + 1, :].astype(jnp.float32) == sec.astype(jnp.float32)
            lines = line_ref[j : j + 1, :].astype(jnp.float32)
            before = column(jnp.where(named, 1.0, 0.0))
            rank = jnp.sum(jnp.where(row_i < lane_i, before, 0.0), axis=0, keepdims=True)
            slot = lax.broadcasted_iota(jnp.int32, (PAIRCAP, contact), 0).astype(jnp.float32)
            chosen = jnp.where(named, 1.0, 0.0) * jnp.where(rank == slot, 1.0, 0.0)
            slot_line = jnp.sum(chosen * lines, axis=1, keepdims=True)
            live = jnp.sum(chosen, axis=1, keepdims=True)
            q = lax.broadcasted_iota(jnp.int32, (PAIRCAP, height), 1).astype(jnp.float32)
            pick[pl.ds(j * PAIRCAP, PAIRCAP), :] = jnp.where(q == slot_line, live, 0.0)

        archived = instant_ref[0].astype(jnp.float32)
        speeds = []
        for k in range(STEPS):
            phase = jnp.full((1, width), archived + k)
            speeds.append(1.0 + 0.5 * jnp.sin(2.0 * math.pi * phase / period_steps))

        for load in loads:
            load.wait()
        wait_recv(heat_halo)
        wait_recv(coef_halo)
        start(dual_halo)

        states = (heat, a1, a2, a3, own)
        for k in range(STEPS):
            src, dst = states[k], states[k + 1]
            shift = first if k == STEPS - 1 else 0

            def forward(z, carry, k=k, src=src, dst=dst, shift=shift):
                c = src[z]
                below = src[z - 1]
                total = (below + src[z + 1]) + in_plane(c)
                change = coef[z] * (total - 6.0 * c) - speeds[k] * (c - below)
                bent = jnp.tanh(c)
                dst[z - shift] = c + time_step * change - time_step * sink_rate * bent
                keep[k, z] = 1.0 - time_step * sink_rate * (1.0 - bent * bent)
                return carry

            lax.fori_loop(jnp.maximum(low, 1 + k), jnp.minimum(high, 3 * depth - 1 - k), forward, 0)

        keep3 = keep.at[3]
        keep_halo = halo(
            keep3, keep3, side_send.at[0], side_recv.at[0],
            (pl.ds(first, depth - 1), pl.ds(last, depth - 1)), (pl.ds(first + 1, depth - 1), pl.ds(1, depth - 1)),
        )
        start(keep_halo)
        for z in range(depth):
            offered[z] = jnp.dot(pick[...], own[z], precision=HIGHEST, preferred_element_type=jnp.float32)
        sends = []
        for j in range(ingots):
            send = pltpu.make_async_remote_copy(
                src_ref=offered.at[:, pl.ds(j * PAIRCAP, PAIRCAP), :],
                dst_ref=slots.at[:, pl.ds(pl.multiple_of(sec * PAIRCAP, PAIRCAP), PAIRCAP), :],
                send_sem=row_send.at[j], recv_sem=row_recv, device_id=(melts + j, slab), device_id_type=MESH,
            )
            send.start()
            sends.append(send)
        state_out = pltpu.make_async_copy(own, state_ref, out_sem.at[0])
        state_out.start()

        for z in (first - 2, last + 1):
            bent = jnp.tanh(a2[z])
            keep[2, z] = 1.0 - time_step * sink_rate * (1.0 - bent * bent)
        wait_recv(dual_halo)
        wait_recv(keep_halo)

        here = returned.at[pl.ds(first, depth)]
        pltpu.make_async_copy(here, here, row_recv).wait()
        back_halo = halo(
            returned, returned, side_send.at[1], side_recv.at[1],
            (pl.ds(first, depth), pl.ds(last, depth)), (pl.ds(first, depth), pl.ds(0, depth)),
        )
        start(back_halo)

        def add_returned(z, carry):
            rows = lax.dot_general(
                pick[...], returned[z], (((0,), (0,)), ((), ())), precision=HIGHEST, preferred_element_type=jnp.float32
            )
            value = dual[z] + rows
            dual[z] = value
            w_a[z] = coef[z] * value
            return carry

        lax.fori_loop(first, last, add_returned, 0)
        wait_recv(back_halo)
        lax.fori_loop(low, first, add_returned, 0)
        lax.fori_loop(last, high, add_returned, 0)

        mus = (result, mu_b, mu_a, mu_b, dual)
        ws = (None, w_b, w_a, w_b, w_a)
        for k in reversed(range(STEPS)):
            src, dst, wsrc, wdst = mus[k + 1], mus[k], ws[k + 1], ws[k]
            shift = first if k == 0 else 0

            def backward(z, carry, k=k, src=src, dst=dst, wsrc=wsrc, wdst=wdst, shift=shift):
                c, w = src[z], wsrc[z]
                total = (wsrc[z - 1] + wsrc[z + 1]) + in_plane(w)
                change = total - 6.0 * w - speeds[k] * (c - src[z + 1])
                value = keep[k, z] * c + time_step * change
                dst[z - shift] = value
                if wdst is not None:
                    wdst[z] = coef[z] * value
                return carry

            lax.fori_loop(jnp.maximum(low, first - k), jnp.minimum(high, last + k), backward, 0)

        adjoint_out = pltpu.make_async_copy(result, adjoint_ref, out_sem.at[1])
        adjoint_out.start()
        for pair in (heat_halo, coef_halo, dual_halo, keep_halo, back_halo):
            wait_send(pair)
        for send in sends:
            send.wait_send()
        state_out.wait()
        adjoint_out.wait()

    @pl.when(jnp.logical_not(is_melt))
    def _():
        start(dual_halo)
        start(coef_halo)
        clear((heat, dual, a1, a2, a3))

        mine = sec - melts
        names = part_ref[pl.ds(mine, 1), :].astype(jnp.float32)
        flags = flag_ref[pl.ds(mine, 1), :].astype(jnp.float32)
        names_col, flags_col = column(names), column(flags)
        same = jnp.where(names_col == names, 1.0, 0.0)
        rank_col = jnp.sum(jnp.where(lane_i < row_i, same, 0.0), axis=1, keepdims=True)
        rank_row = jnp.sum(jnp.where(row_i < lane_i, same, 0.0), axis=0, keepdims=True)
        count = melts * PAIRCAP
        slot_lane = lax.broadcasted_iota(jnp.int32, (contact, count), 1).astype(jnp.float32)
        slot_row = lax.broadcasted_iota(jnp.int32, (count, contact), 0).astype(jnp.float32)
        place = jnp.where(slot_lane == names_col * PAIRCAP + rank_col, flags_col, 0.0)
        give = jnp.where(slot_row == names * PAIRCAP + rank_row, flags, 0.0)

        for load in loads:
            load.wait()
        wait_recv(dual_halo)
        wait_recv(coef_halo)
        start(heat_halo)

        pending = []

        def solve(which, t0, out):
            ts = (t0, a1, a2, a3)

            def image(t, z):
                c = t[z]
                return (coef[z] - (CENTRE - 6.0)) * c - ((t[z - 1] + t[z + 1]) + in_plane(c))

            for k in range(1, BASIS):

                def grow(z, carry, k=k):
                    value = image(ts[k - 1], z)
                    if k == 1:
                        ts[k][z] = value * (1.0 / RADIUS)
                    else:
                        ts[k][z] = value * (2.0 / RADIUS) - ts[k - 2][z]
                    return carry

                reach = BASIS - 1 - k
                lax.fori_loop(jnp.maximum(low, first - reach), jnp.minimum(high, last + 1 + reach), grow, 0)

            def dots(z, sums):
                t = [ref[z] for ref in ts]
                image3 = (coef[z] - (CENTRE - 6.0)) * t[3] - 2.0 * a3[z + 1] - in_plane(t[3])
                terms = (
                    t[0] * t[0], t[0] * t[1], t[1] * t[1], t[1] * t[2],
                    t[2] * t[2], t[2] * t[3], t[3] * t[3], t[3] * image3 * (1.0 / RADIUS),
                )
                return tuple(s + fold(term) for s, term in zip(sums, terms))

            sums = lax.fori_loop(first, last, dots, (jnp.zeros((8, width), jnp.float32),) * 8)
            for k in range(8):
                tile_a[which, pl.ds(k, 1), :] = jnp.sum(sums[k], axis=0, keepdims=True)

            def exchange(tile, gather, send_sem, recv_sem, size, peer):
                for offset in range(1, size):
                    copy = pltpu.make_async_remote_copy(
                        src_ref=tile.at[which], dst_ref=gather.at[which, offset - 1],
                        send_sem=send_sem.at[which, offset - 1], recv_sem=recv_sem,
                        device_id=(sec, peer(offset)), device_id_type=MESH,
                    )
                    copy.start()
                    pending.append(copy)
                if size > 1:
                    pltpu.make_async_copy(gather.at[which], gather.at[which], recv_sem).wait()
                total = tile[which]
                for offset in range(1, size):
                    total = total + gather[which, offset - 1]
                return total

            tile_b[which] = exchange(tile_a, gather_a, sum_send_a, sum_recv.at[which, 0], group, peer_a)
            total = exchange(tile_b, gather_b, sum_send_b, sum_recv.at[which, 1], second, peer_b)
            c = coefficients(total)

            def combine(z, carry):
                out[z - first] = (c[0] * ts[0][z] + c[1] * ts[1][z]) + (c[2] * ts[2][z] + c[3] * ts[3][z])
                return carry

            lax.fori_loop(first, last, combine, 0)

        solve(0, dual, own)
        for z in range(depth):
            back[z] = jnp.dot(give, own[z, :contact, :], precision=HIGHEST, preferred_element_type=jnp.float32)
        sends = []
        for m in range(melts):
            send = pltpu.make_async_remote_copy(
                src_ref=back.at[:, pl.ds(m * PAIRCAP, PAIRCAP), :],
                dst_ref=returned.at[pl.ds(first, depth), pl.ds(pl.multiple_of(mine * PAIRCAP, PAIRCAP), PAIRCAP), :],
                send_sem=row_send.at[m], recv_sem=row_recv, device_id=(m, slab), device_id_type=MESH,
            )
            send.start()
            sends.append(send)
        adjoint_out = pltpu.make_async_copy(own, adjoint_ref, out_sem.at[1])
        adjoint_out.start()

        pltpu.make_async_copy(slots, slots, row_recv).wait()
        for z in range(depth):
            placed[first + z] = jnp.dot(place, slots[z], precision=HIGHEST, preferred_element_type=jnp.float32)
        placed_halo = halo(
            placed, placed, side_send.at[0], side_recv.at[0],
            (pl.ds(first, depth), pl.ds(last, depth)), (pl.ds(first, depth), pl.ds(0, depth)),
        )
        start(placed_halo)
        wait_recv(heat_halo)
        wait_recv(placed_halo)

        def load_up(z, carry):
            heat[z, pl.ds(0, contact), :] = heat[z, pl.ds(0, contact), :] + placed[z]
            return carry

        lax.fori_loop(low, high, load_up, 0)
        solve(1, heat, result)
        state_out = pltpu.make_async_copy(result, state_ref, out_sem.at[0])
        state_out.start()

        for pair in (heat_halo, coef_halo, dual_halo, placed_halo):
            wait_send(pair)
        for copy in sends + pending:
            copy.wait_send()
        state_out.wait()
        adjoint_out.wait()


def body(n_sec, n_slab, group, heat_level, material_factor, dual_sensitivity, part, line, flag, instant):
    ingots, contact = line.shape
    melts = n_sec - ingots
    _, depth, height, width = heat_level.shape
    second = n_slab // group
    f32 = jnp.float32
    wide = pltpu.VMEM((3 * depth, height, width), f32)
    slab_buf = pltpu.VMEM((depth, height, width), f32)
    dma = pltpu.SemaphoreType.DMA
    scratch = [
        wide, wide, wide, wide, wide, wide, slab_buf,
        pltpu.VMEM((STEPS, 3 * depth, height, width), f32),
        wide, wide, wide, wide,
        pltpu.VMEM((ingots * PAIRCAP, height), f32),
        pltpu.VMEM((depth, ingots * PAIRCAP, width), f32),
        pltpu.VMEM((depth, melts * PAIRCAP, width), f32),
        pltpu.VMEM((3 * depth, contact, width), f32),
        pltpu.VMEM((depth, melts * PAIRCAP, width), f32),
        pltpu.VMEM((3 * depth, ingots * PAIRCAP, width), f32),
        pltpu.VMEM((2, 8, width), f32),
        pltpu.VMEM((2, 8, width), f32),
        pltpu.VMEM((2, max(group - 1, 1), 8, width), f32),
        pltpu.VMEM((2, max(second - 1, 1), 8, width), f32),
        slab_buf,
        dma((3,)), dma((2,)), dma((3, 2)), dma((3, 2)),
        dma((max(melts, ingots),)), dma, dma((2, 2)), dma((2, 2)),
        dma((2, max(group - 1, 1))), dma((2, max(second - 1, 1))), dma((2, 2)),
    ]
    vmem, smem, anywhere = (pl.BlockSpec(memory_space=s) for s in (pltpu.VMEM, pltpu.SMEM, pl.ANY))
    shape = jax.ShapeDtypeStruct((depth, height, width), f32)
    state, adjoint = pl.pallas_call(
        functools.partial(kernel, n_sec, n_slab, group),
        out_shape=(shape, shape),
        in_specs=[vmem, vmem, vmem, smem, anywhere, anywhere, anywhere],
        out_specs=(anywhere, anywhere),
        scratch_shapes=scratch,
        compiler_params=pltpu.CompilerParams(
            collective_id=0, has_side_effects=True, vmem_limit_bytes=32 * 1024 * 1024
        ),
    )(part[:, :, 0], line, flag, instant, heat_level[0], material_factor[0], dual_sensitivity[0])
    return state[None], adjoint[None]


def solution(mesh):
    n_sec, n_slab = mesh.shape["sec"], mesh.shape["slab"]
    group = min(8, max(1, n_slab // 2))
    fields = P("sec", "slab", None, None)
    return jax.shard_map(
        functools.partial(body, n_sec, n_slab, group),
        mesh=mesh,
        in_specs=(fields, fields, fields, P(), P(), P(), P()),
        out_specs=(fields, fields),
        check_vma=False,
    )
```

```python
import functools
import math

import jax
import jax.numpy as jnp
from jax import lax
from jax.experimental import pallas as pl
from jax.experimental.pallas import tpu as pltpu
from jax.sharding import PartitionSpec as P

STEPS = 4
PAIRCAP = 8
BASIS = 4

time_step = 0.1
sink_rate = 0.5
period_steps = 16.0

CENTRE = 6.8
RADIUS = 6.4

MESH = pl.DeviceIdType.MESH
HIGHEST = lax.Precision.HIGHEST


def in_plane(c):
    rows, cols = c.shape
    row = lax.broadcasted_iota(jnp.int32, c.shape, 0)
    col = lax.broadcasted_iota(jnp.int32, c.shape, 1)
    up = jnp.where(row == 0, 0.0, pltpu.roll(c, 1, 0))
    down = jnp.where(row == rows - 1, 0.0, pltpu.roll(c, rows - 1, 0))
    left = jnp.where(col == 0, 0.0, pltpu.roll(c, 1, 1))
    right = jnp.where(col == cols - 1, 0.0, pltpu.roll(c, cols - 1, 1))
    return (up + down) + (left + right)


def fold(values):
    rows, cols = values.shape
    return jnp.sum(values.reshape(rows // 8, 8, cols), axis=0)


def coefficients(sums):
    total = jnp.broadcast_to(jnp.sum(sums, axis=1, keepdims=True), sums.shape)
    s = [total[k : k + 1, :] for k in range(8)]
    nu = [s[0], s[1], 2.0 * s[2] - s[0], 2.0 * s[3] - s[1], 2.0 * s[4] - s[0], 2.0 * s[5] - s[1], 2.0 * s[6] - s[0]]
    nu.append(4.0 * s[7] - 2.0 * s[5] - s[1])
    shift = 2.0 * CENTRE / RADIUS
    u = [shift * nu[k] + nu[k + 1] + nu[abs(k - 1)] for k in range(7)]
    mat = [[u[i + j] + u[abs(i - j)] for j in range(BASIS)] for i in range(BASIS)]
    diag = [mat[i][i] for i in range(BASIS)]
    rhs = [(4.0 / RADIUS) * nu[i] for i in range(BASIS)]
    inverse = []
    for k in range(BASIS):
        good = mat[k][k] > 1e-8 * diag[k]
        inv = jnp.where(good, 1.0 / jnp.where(good, mat[k][k], 1.0), 0.0)
        inverse.append(inv)
        for i in range(k + 1, BASIS):
            factor = mat[k][i] * inv
            for j in range(i, BASIS):
                mat[i][j] = mat[i][j] - factor * mat[k][j]
            rhs[i] = rhs[i] - factor * rhs[k]
    out = [None] * BASIS
    for i in reversed(range(BASIS)):
        value = rhs[i]
        for j in range(i + 1, BASIS):
            value = value - mat[i][j] * out[j]
        out[i] = value * inverse[i]
    return out


def kernel(
    n_sec,
    n_slab,
    group,
    part_hbm,
    line_hbm,
    flag_hbm,
    instant_hbm,
    heat_ref,
    factor_ref,
    dual_ref,
    state_ref,
    adjoint_ref,
    part_ref,
    line_ref,
    flag_ref,
    instant_ref,
    heat,
    coef,
    dual,
    a1,
    a2,
    a3,
    own,
    keep,
    mu_a,
    mu_b,
    w_a,
    w_b,
    pick,
    offered,
    slots,
    placed,
    back,
    returned,
    tile_a,
    tile_b,
    gather_a,
    gather_b,
    result,
    local_sem,
    out_sem,
    halo_send,
    halo_recv,
    row_send,
    row_recv,
    side_send,
    side_recv,
    sum_send_a,
    sum_send_b,
    sum_recv,
):
    ingots, contact = part_hbm.shape
    melts = n_sec - ingots
    depth, height, width = heat_ref.shape
    first, last = depth, 2 * depth
    second = n_slab // group
    sec, slab = lax.axis_index("sec"), lax.axis_index("slab")
    is_melt = sec < melts
    has_left, has_right = slab > 0, slab < n_slab - 1
    low = jnp.where(has_left, 0, first)
    high = jnp.where(has_right, 3 * depth, last)

    loads = [
        pltpu.make_async_copy(src, dst.at[pl.ds(first, depth)], local_sem.at[i])
        for i, (src, dst) in enumerate(((heat_ref, heat), (factor_ref, coef), (dual_ref, dual)))
    ]
    tables = [
        pltpu.make_async_copy(src, dst, local_sem.at[3 + i])
        for i, (src, dst) in enumerate(
            ((part_hbm, part_ref), (line_hbm, line_ref), (flag_hbm, flag_ref), (instant_hbm, instant_ref))
        )
    ]
    for load in tables + loads:
        load.start()

    barrier = pltpu.get_barrier_semaphore()

    def greet(to_sec, to_slab):
        pl.semaphore_signal(barrier, inc=1, device_id=(to_sec, to_slab), device_id_type=MESH)

    pl.when(has_left)(lambda: greet(sec, slab - 1))
    pl.when(has_right)(lambda: greet(sec, slab + 1))
    base = (slab // group) * group

    def peer_a(offset):
        return base + lax.rem(slab - base + offset, group)

    def peer_b(offset):
        return lax.rem(slab + offset * group, n_slab)

    beside = has_left.astype(jnp.int32) + has_right.astype(jnp.int32)

    @pl.when(is_melt)
    def _():
        for j in range(ingots):
            greet(melts + j, slab)

    @pl.when(jnp.logical_not(is_melt))
    def _():
        for m in range(melts):
            greet(m, slab)
        for offset in range(1, group):
            greet(sec, peer_a(offset))
        for offset in range(1, second):
            greet(sec, peer_b(offset))

    pl.semaphore_wait(barrier, beside + jnp.where(is_melt, ingots, melts + group - 1 + second - 1))

    def halo(src, dst, send, recv, lefts, rights):
        (left_src, left_dst), (right_src, right_dst) = lefts, rights
        to_left = pltpu.make_async_remote_copy(
            src_ref=src.at[left_src], dst_ref=dst.at[left_dst], send_sem=send.at[0], recv_sem=recv.at[1],
            device_id=(sec, slab - 1), device_id_type=MESH,
        )
        to_right = pltpu.make_async_remote_copy(
            src_ref=src.at[right_src], dst_ref=dst.at[right_dst], send_sem=send.at[1], recv_sem=recv.at[0],
            device_id=(sec, slab + 1), device_id_type=MESH,
        )
        return to_left, to_right

    def start(pair):
        pl.when(has_left)(lambda: pair[0].start())
        pl.when(has_right)(lambda: pair[1].start())

    def wait_recv(pair):
        pl.when(has_right)(lambda: pair[0].wait_recv())
        pl.when(has_left)(lambda: pair[1].wait_recv())

    def wait_send(pair):
        pl.when(has_left)(lambda: pair[0].wait_send())
        pl.when(has_right)(lambda: pair[1].wait_send())

    whole = (pl.ds(0, depth), pl.ds(last, depth)), (pl.ds(0, depth), pl.ds(0, depth))
    heat_halo = halo(heat_ref, heat, halo_send.at[0], halo_recv.at[0], *whole)
    coef_halo = halo(factor_ref, coef, halo_send.at[1], halo_recv.at[1], *whole)
    dual_halo = halo(dual_ref, dual, halo_send.at[2], halo_recv.at[2], *whole)

    zero = jnp.zeros((height, width), jnp.float32)

    def clear(bufs):
        @pl.when(jnp.logical_not(has_left))
        def _():
            for buf in bufs:
                buf[first - 1] = zero

        @pl.when(jnp.logical_not(has_right))
        def _():
            for buf in bufs:
                buf[last] = zero

    for load in tables:
        load.wait()
    row_i = lax.broadcasted_iota(jnp.int32, (contact, contact), 0)
    lane_i = lax.broadcasted_iota(jnp.int32, (contact, contact), 1)

    def column(row):
        return jnp.sum(jnp.where(row_i == lane_i, row, 0.0), axis=1, keepdims=True)

    @pl.when(is_melt)
    def _():
        start(heat_halo)
        start(coef_halo)
        clear((heat, a1, a2, a3, dual, mu_a, mu_b, w_a, w_b))

        for j in range(ingots):
            named = part_ref[j : j + 1, :].astype(jnp.float32) == sec.astype(jnp.float32)
            lines = line_ref[j : j + 1, :].astype(jnp.float32)
            before = column(jnp.where(named, 1.0, 0.0))
            rank = jnp.sum(jnp.where(row_i < lane_i, before, 0.0), axis=0, keepdims=True)
            slot = lax.broadcasted_iota(jnp.int32, (PAIRCAP, contact), 0).astype(jnp.float32)
            chosen = jnp.where(named, 1.0, 0.0) * jnp.where(rank == slot, 1.0, 0.0)
            slot_line = jnp.sum(chosen * lines, axis=1, keepdims=True)
            live = jnp.sum(chosen, axis=1, keepdims=True)
            q = lax.broadcasted_iota(jnp.int32, (PAIRCAP, height), 1).astype(jnp.float32)
            pick[pl.ds(j * PAIRCAP, PAIRCAP), :] = jnp.where(q == slot_line, live, 0.0)

        archived = instant_ref[0].astype(jnp.float32)
        speeds = []
        for k in range(STEPS):
            phase = jnp.full((1, width), archived + k)
            speeds.append(1.0 + 0.5 * jnp.sin(2.0 * math.pi * phase / period_steps))

        for load in loads:
            load.wait()
        wait_recv(heat_halo)
        wait_recv(coef_halo)
        start(dual_halo)

        states = (heat, a1, a2, a3, own)
        for k in range(STEPS):
            src, dst = states[k], states[k + 1]
            shift = first if k == STEPS - 1 else 0

            def forward(z, carry, k=k, src=src, dst=dst, shift=shift):
                c = src[z]
                below = src[z - 1]
                total = (below + src[z + 1]) + in_plane(c)
                change = coef[z] * (total - 6.0 * c) - speeds[k] * (c - below)
                bent = jnp.tanh(c)
                dst[z - shift] = c + time_step * change - time_step * sink_rate * bent
                keep[k, z] = 1.0 - time_step * sink_rate * (1.0 - bent * bent)
                return carry

            lax.fori_loop(jnp.maximum(low, 1 + k), jnp.minimum(high, 3 * depth - 1 - k), forward, 0)

        keep3 = keep.at[3]
        keep_halo = halo(
            keep3, keep3, side_send.at[0], side_recv.at[0],
            (pl.ds(first, depth - 1), pl.ds(last, depth - 1)), (pl.ds(first + 1, depth - 1), pl.ds(1, depth - 1)),
        )
        start(keep_halo)
        for z in range(depth):
            offered[z] = jnp.dot(pick[...], own[z], precision=HIGHEST, preferred_element_type=jnp.float32)
        sends = []
        for j in range(ingots):
            send = pltpu.make_async_remote_copy(
                src_ref=offered.at[:, pl.ds(j * PAIRCAP, PAIRCAP), :],
                dst_ref=slots.at[:, pl.ds(pl.multiple_of(sec * PAIRCAP, PAIRCAP), PAIRCAP), :],
                send_sem=row_send.at[j], recv_sem=row_recv, device_id=(melts + j, slab), device_id_type=MESH,
            )
            send.start()
            sends.append(send)
        state_out = pltpu.make_async_copy(own, state_ref, out_sem.at[0])
        state_out.start()

        for z in (first - 2, last + 1):
            bent = jnp.tanh(a2[z])
            keep[2, z] = 1.0 - time_step * sink_rate * (1.0 - bent * bent)
        wait_recv(dual_halo)
        wait_recv(keep_halo)

        here = returned.at[pl.ds(first, depth)]
        pltpu.make_async_copy(here, here, row_recv).wait()
        back_halo = halo(
            returned, returned, side_send.at[1], side_recv.at[1],
            (pl.ds(first, depth), pl.ds(last, depth)), (pl.ds(first, depth), pl.ds(0, depth)),
        )
        start(back_halo)

        def add_returned(z, carry):
            rows = lax.dot_general(
                pick[...], returned[z], (((0,), (0,)), ((), ())), precision=HIGHEST, preferred_element_type=jnp.float32
            )
            value = dual[z] + rows
            dual[z] = value
            w_a[z] = coef[z] * value
            return carry

        lax.fori_loop(first, last, add_returned, 0)
        wait_recv(back_halo)
        lax.fori_loop(low, first, add_returned, 0)
        lax.fori_loop(last, high, add_returned, 0)

        mus = (result, mu_b, mu_a, mu_b, dual)
        ws = (None, w_b, w_a, w_b, w_a)
        for k in reversed(range(STEPS)):
            src, dst, wsrc, wdst = mus[k + 1], mus[k], ws[k + 1], ws[k]
            shift = first if k == 0 else 0

            def backward(z, carry, k=k, src=src, dst=dst, wsrc=wsrc, wdst=wdst, shift=shift):
                c, w = src[z], wsrc[z]
                total = (wsrc[z - 1] + wsrc[z + 1]) + in_plane(w)
                change = total - 6.0 * w - speeds[k] * (c - src[z + 1])
                value = keep[k, z] * c + time_step * change
                dst[z - shift] = value
                if wdst is not None:
                    wdst[z] = coef[z] * value
                return carry

            lax.fori_loop(jnp.maximum(low, first - k), jnp.minimum(high, last + k), backward, 0)

        adjoint_out = pltpu.make_async_copy(result, adjoint_ref, out_sem.at[1])
        adjoint_out.start()
        for pair in (heat_halo, coef_halo, dual_halo, keep_halo, back_halo):
            wait_send(pair)
        for send in sends:
            send.wait_send()
        state_out.wait()
        adjoint_out.wait()

    @pl.when(jnp.logical_not(is_melt))
    def _():
        start(dual_halo)
        start(coef_halo)
        clear((heat, dual, a1, a2, a3))

        mine = sec - melts
        names = part_ref[pl.ds(mine, 1), :].astype(jnp.float32)
        flags = flag_ref[pl.ds(mine, 1), :].astype(jnp.float32)
        names_col, flags_col = column(names), column(flags)
        same = jnp.where(names_col == names, 1.0, 0.0)
        rank_col = jnp.sum(jnp.where(lane_i < row_i, same, 0.0), axis=1, keepdims=True)
        rank_row = jnp.sum(jnp.where(row_i < lane_i, same, 0.0), axis=0, keepdims=True)
        count = melts * PAIRCAP
        slot_lane = lax.broadcasted_iota(jnp.int32, (contact, count), 1).astype(jnp.float32)
        slot_row = lax.broadcasted_iota(jnp.int32, (count, contact), 0).astype(jnp.float32)
        place = jnp.where(slot_lane == names_col * PAIRCAP + rank_col, flags_col, 0.0)
        give = jnp.where(slot_row == names * PAIRCAP + rank_row, flags, 0.0)

        for load in loads:
            load.wait()
        wait_recv(dual_halo)
        wait_recv(coef_halo)
        start(heat_halo)

        pending = []

        def solve(which, t0, out):
            ts = (t0, a1, a2, a3)

            def image(t, z):
                c = t[z]
                return (coef[z] - (CENTRE - 6.0)) * c - ((t[z - 1] + t[z + 1]) + in_plane(c))

            for k in range(1, BASIS):

                def grow(z, carry, k=k):
                    value = image(ts[k - 1], z)
                    if k == 1:
                        ts[k][z] = value * (1.0 / RADIUS)
                    else:
                        ts[k][z] = value * (2.0 / RADIUS) - ts[k - 2][z]
                    return carry

                reach = BASIS - 1 - k
                lax.fori_loop(jnp.maximum(low, first - reach), jnp.minimum(high, last + 1 + reach), grow, 0)

            def dots(z, sums):
                t = [ref[z] for ref in ts]
                image3 = (coef[z] - (CENTRE - 6.0)) * t[3] - 2.0 * a3[z + 1] - in_plane(t[3])
                terms = (
                    t[0] * t[0], t[0] * t[1], t[1] * t[1], t[1] * t[2],
                    t[2] * t[2], t[2] * t[3], t[3] * t[3], t[3] * image3 * (1.0 / RADIUS),
                )
                return tuple(s + fold(term) for s, term in zip(sums, terms))

            sums = lax.fori_loop(first, last, dots, (jnp.zeros((8, width), jnp.float32),) * 8)
            for k in range(8):
                tile_a[which, pl.ds(k, 1), :] = jnp.sum(sums[k], axis=0, keepdims=True)

            def exchange(tile, gather, send_sem, recv_sem, size, peer):
                for offset in range(1, size):
                    copy = pltpu.make_async_remote_copy(
                        src_ref=tile.at[which], dst_ref=gather.at[which, offset - 1],
                        send_sem=send_sem.at[which, offset - 1], recv_sem=recv_sem,
                        device_id=(sec, peer(offset)), device_id_type=MESH,
                    )
                    copy.start()
                    pending.append(copy)
                if size > 1:
                    pltpu.make_async_copy(gather.at[which], gather.at[which], recv_sem).wait()
                total = tile[which]
                for offset in range(1, size):
                    total = total + gather[which, offset - 1]
                return total

            tile_b[which] = exchange(tile_a, gather_a, sum_send_a, sum_recv.at[which, 0], group, peer_a)
            total = exchange(tile_b, gather_b, sum_send_b, sum_recv.at[which, 1], second, peer_b)
            c = coefficients(total)

            def combine(z, carry):
                out[z - first] = (c[0] * ts[0][z] + c[1] * ts[1][z]) + (c[2] * ts[2][z] + c[3] * ts[3][z])
                return carry

            lax.fori_loop(first, last, combine, 0)

        solve(0, dual, own)
        for z in range(depth):
            back[z] = jnp.dot(give, own[z, :contact, :], precision=HIGHEST, preferred_element_type=jnp.float32)
        sends = []
        for m in range(melts):
            send = pltpu.make_async_remote_copy(
                src_ref=back.at[:, pl.ds(m * PAIRCAP, PAIRCAP), :],
                dst_ref=returned.at[pl.ds(first, depth), pl.ds(pl.multiple_of(mine * PAIRCAP, PAIRCAP), PAIRCAP), :],
                send_sem=row_send.at[m], recv_sem=row_recv, device_id=(m, slab), device_id_type=MESH,
            )
            send.start()
            sends.append(send)
        adjoint_out = pltpu.make_async_copy(own, adjoint_ref, out_sem.at[1])
        adjoint_out.start()

        pltpu.make_async_copy(slots, slots, row_recv).wait()
        for z in range(depth):
            placed[first + z] = jnp.dot(place, slots[z], precision=HIGHEST, preferred_element_type=jnp.float32)
        placed_halo = halo(
            placed, placed, side_send.at[0], side_recv.at[0],
            (pl.ds(first, depth), pl.ds(last, depth)), (pl.ds(first, depth), pl.ds(0, depth)),
        )
        start(placed_halo)
        wait_recv(heat_halo)
        wait_recv(placed_halo)

        def load_up(z, carry):
            heat[z, pl.ds(0, contact), :] = heat[z, pl.ds(0, contact), :] + placed[z]
            return carry

        lax.fori_loop(low, high, load_up, 0)
        solve(1, heat, result)
        state_out = pltpu.make_async_copy(result, state_ref, out_sem.at[0])
        state_out.start()

        for pair in (heat_halo, coef_halo, dual_halo, placed_halo):
            wait_send(pair)
        for copy in sends + pending:
            copy.wait_send()
        state_out.wait()
        adjoint_out.wait()


def body(n_sec, n_slab, group, heat_level, material_factor, dual_sensitivity, part, line, flag, instant):
    ingots, contact = line.shape
    melts = n_sec - ingots
    _, depth, height, width = heat_level.shape
    second = n_slab // group
    f32 = jnp.float32
    wide = pltpu.VMEM((3 * depth, height, width), f32)
    slab_buf = pltpu.VMEM((depth, height, width), f32)
    dma = pltpu.SemaphoreType.DMA
    scratch = [
        pltpu.VMEM((ingots, contact), jnp.int32), pltpu.VMEM((ingots, contact), jnp.int32),
        pltpu.VMEM((ingots, contact), jnp.int32), pltpu.SMEM((1,), jnp.int32),
        wide, wide, wide, wide, wide, wide, slab_buf,
        pltpu.VMEM((STEPS, 3 * depth, height, width), f32),
        wide, wide, wide, wide,
        pltpu.VMEM((ingots * PAIRCAP, height), f32),
        pltpu.VMEM((depth, ingots * PAIRCAP, width), f32),
        pltpu.VMEM((depth, melts * PAIRCAP, width), f32),
        pltpu.VMEM((3 * depth, contact, width), f32),
        pltpu.VMEM((depth, melts * PAIRCAP, width), f32),
        pltpu.VMEM((3 * depth, ingots * PAIRCAP, width), f32),
        pltpu.VMEM((2, 8, width), f32),
        pltpu.VMEM((2, 8, width), f32),
        pltpu.VMEM((2, max(group - 1, 1), 8, width), f32),
        pltpu.VMEM((2, max(second - 1, 1), 8, width), f32),
        slab_buf,
        dma((7,)), dma((2,)), dma((3, 2)), dma((3, 2)),
        dma((max(melts, ingots),)), dma, dma((2, 2)), dma((2, 2)),
        dma((2, max(group - 1, 1))), dma((2, max(second - 1, 1))), dma((2, 2)),
    ]
    hbm = pl.BlockSpec(memory_space=pltpu.HBM)
    shape = jax.ShapeDtypeStruct((depth, height, width), f32)
    state, adjoint = pl.pallas_call(
        functools.partial(kernel, n_sec, n_slab, group),
        out_shape=(shape, shape),
        in_specs=[hbm] * 7,
        out_specs=(hbm, hbm),
        scratch_shapes=scratch,
        compiler_params=pltpu.CompilerParams(
            collective_id=0, has_side_effects=True, vmem_limit_bytes=60 * 1024 * 1024
        ),
    )(part[:, :, 0], line, flag, instant, heat_level[0], material_factor[0], dual_sensitivity[0])
    return state[None], adjoint[None]


def solution(mesh):
    n_sec, n_slab = mesh.shape["sec"], mesh.shape["slab"]
    group = min(8, max(1, n_slab // 2))
    fields = P("sec", "slab", None, None)
    return jax.shard_map(
        functools.partial(body, n_sec, n_slab, group),
        mesh=mesh,
        in_specs=(fields, fields, fields, P(), P(), P(), P()),
        out_specs=(fields, fields),
        check_vma=False,
    )
```

```python
import functools
import math

import jax
import jax.numpy as jnp
from jax import lax
from jax.experimental import pallas as pl
from jax.experimental.pallas import tpu as pltpu
from jax.sharding import PartitionSpec as P

STEPS = 4
PAIRCAP = 8
BASIS = 4

time_step = 0.1
sink_rate = 0.5
period_steps = 16.0

CENTRE = 6.8
RADIUS = 6.4

MESH = pl.DeviceIdType.MESH
HIGHEST = lax.Precision.HIGHEST


def in_plane(c):
    rows, cols = c.shape
    row = lax.broadcasted_iota(jnp.int32, c.shape, 0)
    col = lax.broadcasted_iota(jnp.int32, c.shape, 1)
    up = jnp.where(row == 0, 0.0, pltpu.roll(c, 1, 0))
    down = jnp.where(row == rows - 1, 0.0, pltpu.roll(c, rows - 1, 0))
    left = jnp.where(col == 0, 0.0, pltpu.roll(c, 1, 1))
    right = jnp.where(col == cols - 1, 0.0, pltpu.roll(c, cols - 1, 1))
    return (up + down) + (left + right)


def fold(values):
    rows, cols = values.shape
    return jnp.sum(values.reshape(rows // 8, 8, cols), axis=0)


def own_lanes(values):
    row = lax.broadcasted_iota(jnp.int32, values.shape, 0)
    lane = lax.broadcasted_iota(jnp.int32, values.shape, 1)
    each = values.shape[1] // values.shape[0]
    return jnp.where((lane >= row * each) & (lane < (row + 1) * each), values, 0.0)


def pack(values):
    lanes = values.shape[1]
    for distance in (lanes // 2, lanes // 4, lanes // 8):
        values = values + pltpu.roll(values, distance, 1)
    return jnp.sum(own_lanes(values), axis=0, keepdims=True)


def coefficients(packed):
    spread = own_lanes(jnp.broadcast_to(packed, (8, packed.shape[1])))
    total = jnp.broadcast_to(jnp.sum(spread, axis=1, keepdims=True), spread.shape)
    s = [total[k : k + 1, :] for k in range(8)]
    nu = [s[0], s[1], 2.0 * s[2] - s[0], 2.0 * s[3] - s[1], 2.0 * s[4] - s[0], 2.0 * s[5] - s[1], 2.0 * s[6] - s[0]]
    nu.append(4.0 * s[7] - 2.0 * s[5] - s[1])
    shift = 2.0 * CENTRE / RADIUS
    u = [shift * nu[k] + nu[k + 1] + nu[abs(k - 1)] for k in range(7)]
    mat = [[u[i + j] + u[abs(i - j)] for j in range(BASIS)] for i in range(BASIS)]
    diag = [mat[i][i] for i in range(BASIS)]
    rhs = [(4.0 / RADIUS) * nu[i] for i in range(BASIS)]
    inverse = []
    for k in range(BASIS):
        good = mat[k][k] > 1e-8 * diag[k]
        inv = jnp.where(good, 1.0 / jnp.where(good, mat[k][k], 1.0), 0.0)
        inverse.append(inv)
        for i in range(k + 1, BASIS):
            factor = mat[k][i] * inv
            for j in range(i, BASIS):
                mat[i][j] = mat[i][j] - factor * mat[k][j]
            rhs[i] = rhs[i] - factor * rhs[k]
    out = [None] * BASIS
    for i in reversed(range(BASIS)):
        value = rhs[i]
        for j in range(i + 1, BASIS):
            value = value - mat[i][j] * out[j]
        out[i] = value * inverse[i]
    return out


def kernel(
    n_sec,
    n_slab,
    part_hbm,
    line_hbm,
    flag_hbm,
    instant_ref,
    heat_ref,
    factor_ref,
    dual_ref,
    both_ref,
    part_ref,
    line_ref,
    flag_ref,
    heat,
    coef,
    dual,
    a1,
    a2,
    a3,
    keep,
    mu_a,
    mu_b,
    w_a,
    w_b,
    pick,
    pick_t,
    offered,
    slots,
    back,
    returned,
    sums_ref,
    packed_ref,
    gather,
    local_sem,
    halo_send,
    halo_recv,
    row_send,
    row_recv,
    side_send,
    side_recv,
    sum_send,
    sum_recv,
    ready,
):
    ingots, contact = part_hbm.shape
    melts = n_sec - ingots
    early = 2 * melts // 3
    depth, height, width = heat_ref.shape
    first, last = depth, 2 * depth
    sec, slab = lax.axis_index("sec"), lax.axis_index("slab")
    is_melt = sec < melts
    is_early = sec < early
    has_left, has_right = slab > 0, slab < n_slab - 1
    state_ref, adjoint_ref = both_ref.at[0], both_ref.at[1]

    loads = [
        pltpu.make_async_copy(src, dst.at[pl.ds(first, depth)], local_sem.at[i])
        for i, (src, dst) in enumerate(((heat_ref, heat), (factor_ref, coef), (dual_ref, dual)))
    ]
    tables = [
        pltpu.make_async_copy(src, dst, local_sem.at[3 + i])
        for i, (src, dst) in enumerate(((part_hbm, part_ref), (line_hbm, line_ref), (flag_hbm, flag_ref)))
    ]
    for load in tables + loads:
        load.start()

    barrier = pltpu.get_barrier_semaphore()

    def greet(to_sec, to_slab, sem=barrier):
        pl.semaphore_signal(sem, inc=1, device_id=(to_sec, to_slab), device_id_type=MESH)

    def peer(offset):
        return lax.rem(slab + offset, n_slab)

    @pl.when(is_melt)
    def _():
        pl.when(has_left)(lambda: greet(sec, slab - 1))
        pl.when(has_right)(lambda: greet(sec, slab + 1))

        @pl.when(is_early)
        def _():
            for j in range(ingots):
                greet(melts + j, slab)

    @pl.when(jnp.logical_not(is_melt))
    def _():
        for offset in range(1, n_slab):
            greet(sec, peer(offset))
        for m in range(early, melts):
            greet(m, slab)

    beside = has_left.astype(jnp.int32) + has_right.astype(jnp.int32)
    heard = jnp.where(is_melt, beside + jnp.where(is_early, 0, ingots), n_slab - 1 + early)
    pl.semaphore_wait(barrier, heard)

    def halo(index, src, dst, to_left, to_right):
        (left_src, left_dst), (right_src, right_dst) = to_left, to_right
        send, recv = halo_send.at[index], halo_recv.at[index]
        return (
            pltpu.make_async_remote_copy(
                src_ref=src.at[left_src], dst_ref=dst.at[left_dst], send_sem=send.at[0], recv_sem=recv.at[1],
                device_id=(sec, slab - 1), device_id_type=MESH,
            ),
            pltpu.make_async_remote_copy(
                src_ref=src.at[right_src], dst_ref=dst.at[right_dst], send_sem=send.at[1], recv_sem=recv.at[0],
                device_id=(sec, slab + 1), device_id_type=MESH,
            ),
        )

    def start(pair):
        pl.when(has_left)(lambda: pair[0].start())
        pl.when(has_right)(lambda: pair[1].start())

    def wait_recv(pair):
        pl.when(has_right)(lambda: pair[0].wait_recv())
        pl.when(has_left)(lambda: pair[1].wait_recv())

    def wait_send(pair):
        pl.when(has_left)(lambda: pair[0].wait_send())
        pl.when(has_right)(lambda: pair[1].wait_send())

    def lower(planes, offset=0):
        return pl.ds(offset, planes), pl.ds(last + offset, planes)

    def upper(planes, offset=0):
        at = depth - planes - offset
        return pl.ds(at, planes), pl.ds(at, planes)

    def pass_on(buf, rows, index):
        here = buf.at[pl.ds(first, depth), rows]
        pair = []
        for side, there, to in ((0, last, slab - 1), (1, 0, slab + 1)):
            pair.append(
                pltpu.make_async_remote_copy(
                    src_ref=here, dst_ref=buf.at[pl.ds(there, depth), rows], send_sem=side_send.at[side, index],
                    recv_sem=side_recv.at[1 - side], device_id=(sec, to), device_id_type=MESH,
                )
            )
        start(pair)
        return pair

    def take(buf, side):
        region = buf.at[pl.ds(2 * depth * side, depth)]
        pltpu.make_async_copy(region, region, side_recv.at[side]).wait()

    zero = jnp.zeros((height, width), jnp.float32)

    def clear(*bufs):
        @pl.when(jnp.logical_not(has_left))
        def _():
            for buf in bufs:
                buf[first - 1] = zero

        @pl.when(jnp.logical_not(has_right))
        def _():
            for buf in bufs:
                buf[last] = zero

    row_i = lax.broadcasted_iota(jnp.int32, (contact, contact), 0)
    lane_i = lax.broadcasted_iota(jnp.int32, (contact, contact), 1)

    def column(row):
        return jnp.sum(jnp.where(row_i == lane_i, row, 0.0), axis=1, keepdims=True)

    def slot_rows(index):
        return pl.ds(index * PAIRCAP, PAIRCAP)

    @pl.when(is_melt)
    def _():
        heat_halo = halo(0, heat_ref, heat, lower(depth), upper(depth))
        coef_halo = halo(1, factor_ref, coef, lower(depth - 1), upper(depth - 1))
        edge_halo = halo(2, factor_ref, coef, lower(1, depth - 1), upper(1, depth - 1))
        dual_halo = halo(3, dual_ref, dual, lower(depth), upper(depth))
        start(heat_halo)
        start(coef_halo)

        @pl.when(jnp.logical_not(is_early))
        def _():
            for j in range(ingots):
                greet(melts + j, slab, ready)

        clear(heat, dual, w_a)
        for load in tables:
            load.wait()

        for j in range(ingots):
            named = part_ref[j : j + 1, :].astype(jnp.float32) == sec.astype(jnp.float32)
            lines = line_ref[j : j + 1, :].astype(jnp.float32)
            before = column(jnp.where(named, 1.0, 0.0))
            rank = jnp.sum(jnp.where(row_i < lane_i, before, 0.0), axis=0, keepdims=True)
            slot = lax.broadcasted_iota(jnp.int32, (PAIRCAP, contact), 0).astype(jnp.float32)
            chosen = jnp.where(named, 1.0, 0.0) * jnp.where(rank == slot, 1.0, 0.0)
            slot_line = jnp.sum(chosen * lines, axis=1, keepdims=True)
            live = jnp.sum(chosen, axis=1, keepdims=True)
            q = lax.broadcasted_iota(jnp.int32, (PAIRCAP, height), 1).astype(jnp.float32)
            pick[slot_rows(j), :] = jnp.where(q == slot_line, live, 0.0)
        eye = jnp.where(
            lax.broadcasted_iota(jnp.int32, (height, height), 0) == lax.broadcasted_iota(jnp.int32, (height, height), 1),
            1.0, 0.0,
        )
        pick_t[...] = lax.dot_general(
            eye, pick[...], (((1,), (1,)), ((), ())), precision=HIGHEST, preferred_element_type=jnp.float32
        )

        archived = instant_ref[0].astype(jnp.float32)
        speeds = []
        for k in range(STEPS):
            phase = jnp.full((1, width), archived + k)
            speeds.append(1.0 + 0.5 * jnp.sin(2.0 * math.pi * phase / period_steps))

        for load in loads:
            load.wait()
        wait_recv(heat_halo)
        wait_recv(coef_halo)
        start(edge_halo)
        start(dual_halo)

        states = (heat, a1, a2, a3, state_ref)
        for k in range(STEPS):
            src, dst = states[k], states[k + 1]
            final = k == STEPS - 1
            shift = first if final else 0

            def forward(z, carry, k=k, src=src, dst=dst, shift=shift):
                c = src[z]
                below = src[z - 1]
                total = (below + src[z + 1]) + in_plane(c)
                change = coef[z] * (total - 6.0 * c) - speeds[k] * (c - below)
                bent = jnp.tanh(c)
                dst[z - shift] = c + time_step * change - time_step * sink_rate * bent
                keep[k, z] = 1.0 - time_step * sink_rate * (1.0 - bent * bent)
                return carry

            lax.fori_loop(1 + k, 3 * depth - 1 - k, forward, 0, unroll=2)
            if not final:
                clear(dst)

        for z in range(depth):
            offered[z] = jnp.dot(pick[...], state_ref[z], precision=HIGHEST, preferred_element_type=jnp.float32)
        pl.when(is_early)(lambda: pl.semaphore_wait(ready, ingots))
        sends = []
        for j in range(ingots):
            send = pltpu.make_async_remote_copy(
                src_ref=offered.at[:, slot_rows(j), :],
                dst_ref=slots.at[pl.ds(first, depth), pl.ds(pl.multiple_of(sec * PAIRCAP, PAIRCAP), PAIRCAP), :],
                send_sem=row_send.at[j], recv_sem=row_recv.at[sec], device_id=(melts + j, slab), device_id_type=MESH,
            )
            send.start()
            sends.append(send)
        keep3 = keep.at[3]
        keep_halo = halo(
            4, keep3, keep3, (pl.ds(first, depth - 1), pl.ds(last, depth - 1)), (pl.ds(first + 1, depth - 1), pl.ds(1, depth - 1))
        )
        start(keep_halo)

        for z in (first - 2, last + 1):
            bent = jnp.tanh(a2[z])
            keep[2, z] = 1.0 - time_step * sink_rate * (1.0 - bent * bent)
        wait_recv(edge_halo)
        wait_recv(dual_halo)
        wait_recv(keep_halo)

        passed = []
        for j in reversed(range(ingots)):
            region = returned.at[pl.ds(first, depth), slot_rows(j)]
            pltpu.make_async_copy(region, region, row_recv.at[j]).wait()
            passed.append(pass_on(returned, slot_rows(j), j))

        def add_returned(at):
            for z in range(at, at + depth):
                rows = jnp.dot(pick_t[...], returned[z], precision=HIGHEST, preferred_element_type=jnp.float32)
                value = dual[z] + rows
                dual[z] = value
                w_a[z] = coef[z] * value

        add_returned(first)

        @pl.when(has_left)
        def _():
            take(returned, 0)
            add_returned(0)

        @pl.when(has_right)
        def _():
            take(returned, 1)
            add_returned(last)

        mus = (adjoint_ref, mu_b, mu_a, mu_b, dual)
        ws = (None, w_b, w_a, w_b, w_a)
        for k in reversed(range(STEPS)):
            src, dst, wsrc, wdst = mus[k + 1], mus[k], ws[k + 1], ws[k]
            shift = first if k == 0 else 0

            def backward(z, carry, k=k, src=src, dst=dst, wsrc=wsrc, wdst=wdst, shift=shift):
                c, w = src[z], wsrc[z]
                total = (wsrc[z - 1] + wsrc[z + 1]) + in_plane(w)
                change = total - 6.0 * w - speeds[k] * (c - src[z + 1])
                value = keep[k, z] * c + time_step * change
                dst[z - shift] = value
                if wdst is not None:
                    wdst[z] = coef[z] * value
                return carry

            lax.fori_loop(first - k, last + k, backward, 0, unroll=2)
            if wdst is not None:
                clear(dst, wdst)

        for pair in [heat_halo, coef_halo, edge_halo, dual_halo, keep_halo] + passed:
            wait_send(pair)
        for send in sends:
            send.wait_send()

    @pl.when(jnp.logical_not(is_melt))
    def _():
        dual_halo = halo(3, dual_ref, dual, lower(depth), upper(depth - 1))
        coef_halo = halo(1, factor_ref, coef, lower(depth - 1), upper(depth - 2))
        heat_halo = halo(0, heat_ref, heat, lower(depth), upper(depth - 1))
        start(dual_halo)
        start(coef_halo)
        for m in range(early):
            greet(m, slab, ready)
        clear(heat, dual)

        for load in tables:
            load.wait()
        mine = sec - melts
        names = part_ref[pl.ds(mine, 1), :].astype(jnp.float32)
        flags = flag_ref[pl.ds(mine, 1), :].astype(jnp.float32)
        names_col, flags_col = column(names), column(flags)
        same = jnp.where(names_col == names, 1.0, 0.0)
        rank_col = jnp.sum(jnp.where(lane_i < row_i, same, 0.0), axis=1, keepdims=True)
        rank_row = jnp.sum(jnp.where(row_i < lane_i, same, 0.0), axis=0, keepdims=True)
        count = melts * PAIRCAP
        slot_lane = lax.broadcasted_iota(jnp.int32, (contact, count), 1).astype(jnp.float32)
        slot_row = lax.broadcasted_iota(jnp.int32, (count, contact), 0).astype(jnp.float32)
        place = jnp.where(slot_lane == names_col * PAIRCAP + rank_col, flags_col, 0.0)
        give = jnp.where(slot_row == names * PAIRCAP + rank_row, flags, 0.0)

        for load in loads:
            load.wait()
        wait_recv(dual_halo)
        wait_recv(coef_halo)
        start(heat_halo)

        def solve(which, t0, out):
            ts = (t0, a1, a2, a3)

            def image(t, z):
                c = t[z]
                return (coef[z] - (CENTRE - 6.0)) * c - ((t[z - 1] + t[z + 1]) + in_plane(c))

            for k in range(1, BASIS):

                def grow(z, carry, k=k):
                    value = image(ts[k - 1], z)
                    if k == 1:
                        ts[k][z] = value * (1.0 / RADIUS)
                    else:
                        ts[k][z] = value * (2.0 / RADIUS) - ts[k - 2][z]
                    return carry

                reach = BASIS - 1 - k
                lax.fori_loop(first - reach, last + 1 + reach, grow, 0, unroll=2)
                clear(ts[k])

            def dots(z, sums):
                t = [ref[z] for ref in ts]
                image3 = (coef[z] - (CENTRE - 6.0)) * t[3] - 2.0 * a3[z + 1] - in_plane(t[3])
                terms = (
                    t[0] * t[0], t[0] * t[1], t[1] * t[1], t[1] * t[2],
                    t[2] * t[2], t[2] * t[3], t[3] * t[3], t[3] * image3 * (1.0 / RADIUS),
                )
                return tuple(s + fold(term) for s, term in zip(sums, terms))

            sums = lax.fori_loop(first, last, dots, (jnp.zeros((8, width), jnp.float32),) * 8, unroll=2)
            for k in range(8):
                sums_ref[pl.ds(k, 1), :] = jnp.sum(sums[k], axis=0, keepdims=True)
            packed = pack(sums_ref[...])
            packed_ref[which] = packed
            for offset in range(1, n_slab):
                pltpu.make_async_remote_copy(
                    src_ref=packed_ref.at[which], dst_ref=gather.at[which, pl.ds(offset - 1, 1)],
                    send_sem=sum_send.at[which], recv_sem=sum_recv.at[which],
                    device_id=(sec, peer(offset)), device_id_type=MESH,
                ).start()
            others = gather.at[which, pl.ds(0, n_slab - 1)]
            pltpu.make_async_copy(others, others, sum_recv.at[which]).wait()
            c = coefficients(packed + jnp.sum(gather[which, : n_slab - 1, :], axis=0, keepdims=True))

            def combine(z, carry):
                out[z - first] = (c[0] * ts[0][z] + c[1] * ts[1][z]) + (c[2] * ts[2][z] + c[3] * ts[3][z])
                return carry

            lax.fori_loop(first, last, combine, 0, unroll=2)

        solve(0, dual, adjoint_ref)
        for z in range(depth):
            back[z] = jnp.dot(give, adjoint_ref[z, :contact, :], precision=HIGHEST, preferred_element_type=jnp.float32)
        sends = []
        for m in range(melts):
            if m == early:
                pl.semaphore_wait(ready, melts - early)
            send = pltpu.make_async_remote_copy(
                src_ref=back.at[:, slot_rows(m), :],
                dst_ref=returned.at[pl.ds(first, depth), pl.ds(pl.multiple_of(mine * PAIRCAP, PAIRCAP), PAIRCAP), :],
                send_sem=row_send.at[m], recv_sem=row_recv.at[mine], device_id=(m, slab), device_id_type=MESH,
            )
            send.start()
            sends.append(send)

        passed = []
        for m in range(melts):
            region = slots.at[pl.ds(first, depth), slot_rows(m)]
            pltpu.make_async_copy(region, region, row_recv.at[m]).wait()
            passed.append(pass_on(slots, slot_rows(m), m))

        def load_up(at):
            for z in range(at, at + depth):
                rows = jnp.dot(place, slots[z], precision=HIGHEST, preferred_element_type=jnp.float32)
                heat[z, pl.ds(0, contact), :] = heat[z, pl.ds(0, contact), :] + rows

        wait_recv(heat_halo)
        load_up(first)

        @pl.when(has_left)
        def _():
            take(slots, 0)
            load_up(0)

        @pl.when(has_right)
        def _():
            take(slots, 1)
            load_up(last)

        solve(1, heat, state_ref)

        for pair in [dual_halo, coef_halo, heat_halo] + passed:
            wait_send(pair)
        for send in sends:
            send.wait_send()
        for which in range(2):
            others = gather.at[which, pl.ds(0, n_slab - 1)]
            pltpu.make_async_copy(others, others, sum_send.at[which]).wait()


def body(n_sec, n_slab, heat_level, material_factor, dual_sensitivity, part, line, flag, instant):
    ingots, contact = line.shape
    melts = n_sec - ingots
    _, depth, height, width = heat_level.shape
    f32 = jnp.float32
    wide = pltpu.VMEM((3 * depth, height, width), f32)
    table = pltpu.VMEM((ingots, contact), jnp.int32)
    dma = pltpu.SemaphoreType.DMA
    most = max(melts, ingots)
    scratch = [
        table, table, table,
        wide, wide, wide, wide, wide, wide,
        pltpu.VMEM((STEPS, 3 * depth, height, width), f32),
        wide, wide, wide, wide,
        pltpu.VMEM((ingots * PAIRCAP, height), f32),
        pltpu.VMEM((height, ingots * PAIRCAP), f32),
        pltpu.VMEM((depth, ingots * PAIRCAP, width), f32),
        pltpu.VMEM((3 * depth, melts * PAIRCAP, width), f32),
        pltpu.VMEM((depth, melts * PAIRCAP, width), f32),
        pltpu.VMEM((3 * depth, ingots * PAIRCAP, width), f32),
        pltpu.VMEM((8, width), f32),
        pltpu.VMEM((2, 1, width), f32),
        pltpu.VMEM((2, n_slab, width), f32),
        dma((6,)), dma((5, 2)), dma((5, 2)),
        dma((most,)), dma((most,)), dma((2, most)), dma((2,)),
        dma((2,)), dma((2,)), pltpu.SemaphoreType.REGULAR,
    ]
    hbm, vmem, smem = (pl.BlockSpec(memory_space=s) for s in (pltpu.HBM, pltpu.VMEM, pltpu.SMEM))
    fields = (part[:, :, 0], line, flag, heat_level[0], material_factor[0], dual_sensitivity[0])
    fields = [pltpu.with_memory_space_constraint(field, pltpu.HBM) for field in fields]
    both = pl.pallas_call(
        functools.partial(kernel, n_sec, n_slab),
        out_shape=jax.ShapeDtypeStruct((2, depth, height, width), f32),
        in_specs=[hbm, hbm, hbm, smem, hbm, hbm, hbm],
        out_specs=vmem,
        scratch_shapes=scratch,
        compiler_params=pltpu.CompilerParams(
            collective_id=0, has_side_effects=True, vmem_limit_bytes=32 * 1024 * 1024
        ),
    )(*fields[:3], instant, *fields[3:])
    return both[0:1], both[1:2]


def solution(mesh):
    n_sec, n_slab = mesh.shape["sec"], mesh.shape["slab"]
    fields = P("sec", "slab", None, None)
    return jax.shard_map(
        functools.partial(body, n_sec, n_slab),
        mesh=mesh,
        in_specs=(fields, fields, fields, P(), P(), P(), P()),
        out_specs=(fields, fields),
        check_vma=False,
    )
```

```python
import functools
import math

import jax
import jax.numpy as jnp
from jax import lax
from jax.experimental import pallas as pl
from jax.experimental.pallas import tpu as pltpu
from jax.sharding import PartitionSpec as P

STEPS = 4
PAIRCAP = 8
BASIS = 4
CLOSE = 4

time_step = 0.1
sink_rate = 0.5
period_steps = 16.0

CENTRE = 6.8
RADIUS = 6.4

MESH = pl.DeviceIdType.MESH
HIGHEST = lax.Precision.HIGHEST


def in_plane(c):
    rows, cols = c.shape
    row = lax.broadcasted_iota(jnp.int32, c.shape, 0)
    col = lax.broadcasted_iota(jnp.int32, c.shape, 1)
    up = jnp.where(row == 0, 0.0, pltpu.roll(c, 1, 0))
    down = jnp.where(row == rows - 1, 0.0, pltpu.roll(c, rows - 1, 0))
    left = jnp.where(col == 0, 0.0, pltpu.roll(c, 1, 1))
    right = jnp.where(col == cols - 1, 0.0, pltpu.roll(c, cols - 1, 1))
    return (up + down) + (left + right)


def fold(values):
    rows, cols = values.shape
    return jnp.sum(values.reshape(rows // 8, 8, cols), axis=0)


def own_lanes(values):
    row = lax.broadcasted_iota(jnp.int32, values.shape, 0)
    lane = lax.broadcasted_iota(jnp.int32, values.shape, 1)
    each = values.shape[1] // values.shape[0]
    return jnp.where((lane >= row * each) & (lane < (row + 1) * each), values, 0.0)


def pack(values):
    lanes = values.shape[1]
    for distance in (lanes // 2, lanes // 4, lanes // 8):
        values = values + pltpu.roll(values, distance, 1)
    return jnp.sum(own_lanes(values), axis=0, keepdims=True)


def coefficients(packed):
    spread = own_lanes(jnp.broadcast_to(packed, (8, packed.shape[1])))
    total = jnp.broadcast_to(jnp.sum(spread, axis=1, keepdims=True), spread.shape)
    s = [total[k : k + 1, :] for k in range(8)]
    nu = [s[0], s[1], 2.0 * s[2] - s[0], 2.0 * s[3] - s[1], 2.0 * s[4] - s[0], 2.0 * s[5] - s[1], 2.0 * s[6] - s[0]]
    nu.append(4.0 * s[7] - 2.0 * s[5] - s[1])
    shift = 2.0 * CENTRE / RADIUS
    u = [shift * nu[k] + nu[k + 1] + nu[abs(k - 1)] for k in range(7)]
    mat = [[u[i + j] + u[abs(i - j)] for j in range(BASIS)] for i in range(BASIS)]
    diag = [mat[i][i] for i in range(BASIS)]
    rhs = [(4.0 / RADIUS) * nu[i] for i in range(BASIS)]
    inverse = []
    for k in range(BASIS):
        good = mat[k][k] > 1e-8 * diag[k]
        inv = jnp.where(good, 1.0 / jnp.where(good, mat[k][k], 1.0), 0.0)
        inverse.append(inv)
        for i in range(k + 1, BASIS):
            factor = mat[k][i] * inv
            for j in range(i, BASIS):
                mat[i][j] = mat[i][j] - factor * mat[k][j]
            rhs[i] = rhs[i] - factor * rhs[k]
    out = [None] * BASIS
    for i in reversed(range(BASIS)):
        value = rhs[i]
        for j in range(i + 1, BASIS):
            value = value - mat[i][j] * out[j]
        out[i] = value * inverse[i]
    return out


def kernel(
    n_sec,
    n_slab,
    part_hbm,
    line_hbm,
    flag_hbm,
    instant_ref,
    heat_ref,
    factor_ref,
    dual_ref,
    both_ref,
    part_ref,
    line_ref,
    flag_ref,
    heat,
    coef,
    dual,
    a1,
    a2,
    a3,
    keep,
    mu_a,
    mu_b,
    w_a,
    w_b,
    pick,
    pick_t,
    offered,
    slots,
    back,
    basis_rows,
    returned,
    sums_ref,
    packed_ref,
    gather,
    local_sem,
    halo_send,
    halo_recv,
    row_send,
    row_recv,
    side_send,
    side_recv,
    sum_send,
    sum_recv,
    ready,
    known,
):
    ingots, contact = part_hbm.shape
    melts = n_sec - ingots
    early = 2 * melts // 3
    depth, height, width = heat_ref.shape
    first, last = depth, 2 * depth
    sec, slab = lax.axis_index("sec"), lax.axis_index("slab")
    is_melt = sec < melts
    is_early = sec < early
    has_left, has_right = slab > 0, slab < n_slab - 1
    state_ref, adjoint_ref = both_ref.at[0], both_ref.at[1]

    loads = [
        pltpu.make_async_copy(src, dst.at[pl.ds(first, depth)], local_sem.at[i])
        for i, (src, dst) in enumerate(((heat_ref, heat), (factor_ref, coef), (dual_ref, dual)))
    ]
    tables = [
        pltpu.make_async_copy(src, dst, local_sem.at[3 + i])
        for i, (src, dst) in enumerate(((part_hbm, part_ref), (line_hbm, line_ref), (flag_hbm, flag_ref)))
    ]
    barrier = pltpu.get_barrier_semaphore()

    def greet(to_sec, to_slab, sem=barrier):
        pl.semaphore_signal(sem, inc=1, device_id=(to_sec, to_slab), device_id_type=MESH)

    def along(offset):
        return lax.rem(slab + offset % n_slab, n_slab)

    sizes = (4, 4, 2) if n_slab == 32 else (n_slab,)
    partners = []
    for flat in range(1, n_slab):
        shift, rest = [], flat
        for size in reversed(sizes):
            shift.insert(0, rest % size)
            rest //= size
        partners.append((sum(min(step, size - step) for step, size in zip(shift, sizes)), tuple(shift)))
    partners.sort(key=lambda entry: (-entry[0], entry[1]))

    def partner(shift):
        index, stride, rest = 0, 1, slab
        for step, size in zip(reversed(shift), reversed(sizes)):
            index = index + lax.rem(lax.rem(rest, size) + step, size) * stride
            rest, stride = rest // size, stride * size
        return index

    near = sorted({offset % n_slab for offset in range(-CLOSE, CLOSE + 1)} - {0})

    @pl.when(is_melt)
    def _():
        pl.when(has_left)(lambda: greet(sec, slab - 1))
        pl.when(has_right)(lambda: greet(sec, slab + 1))

        @pl.when(is_early)
        def _():
            for j in range(ingots):
                greet(melts + j, slab)

    @pl.when(jnp.logical_not(is_melt))
    def _():
        for offset in near:
            greet(sec, along(offset))
        for m in range(early, melts):
            greet(m, slab)

    beside = has_left.astype(jnp.int32) + has_right.astype(jnp.int32)
    heard = jnp.where(is_melt, beside + jnp.where(is_early, 0, ingots), len(near) + early)
    for load in tables + loads:
        load.start()
    pl.semaphore_wait(barrier, heard)

    def halo(index, src, dst, to_left, to_right):
        (left_src, left_dst), (right_src, right_dst) = to_left, to_right
        send, recv = halo_send.at[index], halo_recv.at[index]
        return (
            pltpu.make_async_remote_copy(
                src_ref=src.at[left_src], dst_ref=dst.at[left_dst], send_sem=send.at[0], recv_sem=recv.at[1],
                device_id=(sec, slab - 1), device_id_type=MESH,
            ),
            pltpu.make_async_remote_copy(
                src_ref=src.at[right_src], dst_ref=dst.at[right_dst], send_sem=send.at[1], recv_sem=recv.at[0],
                device_id=(sec, slab + 1), device_id_type=MESH,
            ),
        )

    def start(pair):
        pl.when(has_left)(lambda: pair[0].start())
        pl.when(has_right)(lambda: pair[1].start())

    def wait_recv(pair):
        pl.when(has_right)(lambda: pair[0].wait_recv())
        pl.when(has_left)(lambda: pair[1].wait_recv())

    def wait_send(pair):
        pl.when(has_left)(lambda: pair[0].wait_send())
        pl.when(has_right)(lambda: pair[1].wait_send())

    def lower(planes, offset=0):
        return pl.ds(offset, planes), pl.ds(last + offset, planes)

    def upper(planes, offset=0):
        at = depth - planes - offset
        return pl.ds(at, planes), pl.ds(at, planes)

    def pass_on(buf, rows, index):
        here = buf.at[pl.ds(first, depth), rows]
        pair = []
        for side, there, to in ((0, last, slab - 1), (1, 0, slab + 1)):
            pair.append(
                pltpu.make_async_remote_copy(
                    src_ref=here, dst_ref=buf.at[pl.ds(there, depth), rows], send_sem=side_send.at[side, index],
                    recv_sem=side_recv.at[1 - side], device_id=(sec, to), device_id_type=MESH,
                )
            )
        start(pair)
        return pair

    def take(buf, side):
        region = buf.at[pl.ds(2 * depth * side, depth)]
        pltpu.make_async_copy(region, region, side_recv.at[side]).wait()

    zero = jnp.zeros((height, width), jnp.float32)

    def clear(*bufs):
        @pl.when(jnp.logical_not(has_left))
        def _():
            for buf in bufs:
                buf[first - 1] = zero

        @pl.when(jnp.logical_not(has_right))
        def _():
            for buf in bufs:
                buf[last] = zero

    row_i = lax.broadcasted_iota(jnp.int32, (contact, contact), 0)
    lane_i = lax.broadcasted_iota(jnp.int32, (contact, contact), 1)

    def column(row):
        return jnp.sum(jnp.where(row_i == lane_i, row, 0.0), axis=1, keepdims=True)

    def slot_rows(index):
        return pl.ds(index * PAIRCAP, PAIRCAP)

    @pl.when(is_melt)
    def _():
        heat_halo = halo(0, heat_ref, heat, lower(depth), upper(depth))
        coef_halo = halo(1, factor_ref, coef, lower(depth - 1), upper(depth - 1))
        edge_halo = halo(2, factor_ref, coef, lower(1, depth - 1), upper(1, depth - 1))
        dual_halo = halo(3, dual_ref, dual, lower(depth), upper(depth))
        start(heat_halo)
        start(coef_halo)

        @pl.when(jnp.logical_not(is_early))
        def _():
            for j in range(ingots):
                greet(melts + j, slab, ready)

        clear(heat, dual, w_a)
        for load in tables:
            load.wait()

        for j in range(ingots):
            named = part_ref[j : j + 1, :].astype(jnp.float32) == sec.astype(jnp.float32)
            lines = line_ref[j : j + 1, :].astype(jnp.float32)
            before = column(jnp.where(named, 1.0, 0.0))
            rank = jnp.sum(jnp.where(row_i < lane_i, before, 0.0), axis=0, keepdims=True)
            slot = lax.broadcasted_iota(jnp.int32, (PAIRCAP, contact), 0).astype(jnp.float32)
            chosen = jnp.where(named, 1.0, 0.0) * jnp.where(rank == slot, 1.0, 0.0)
            slot_line = jnp.sum(chosen * lines, axis=1, keepdims=True)
            live = jnp.sum(chosen, axis=1, keepdims=True)
            q = lax.broadcasted_iota(jnp.int32, (PAIRCAP, height), 1).astype(jnp.float32)
            pick[slot_rows(j), :] = jnp.where(q == slot_line, live, 0.0)
        eye = jnp.where(
            lax.broadcasted_iota(jnp.int32, (height, height), 0) == lax.broadcasted_iota(jnp.int32, (height, height), 1),
            1.0, 0.0,
        )
        pick_t[...] = lax.dot_general(
            eye, pick[...], (((1,), (1,)), ((), ())), precision=HIGHEST, preferred_element_type=jnp.float32
        )

        archived = instant_ref[0].astype(jnp.float32)
        speeds = []
        for k in range(STEPS):
            phase = jnp.full((1, width), archived + k)
            speeds.append(1.0 + 0.5 * jnp.sin(2.0 * math.pi * phase / period_steps))

        for load in loads:
            load.wait()
        wait_recv(heat_halo)
        wait_recv(coef_halo)
        start(edge_halo)
        start(dual_halo)

        states = (heat, a1, a2, a3, state_ref)
        for k in range(STEPS):
            src, dst = states[k], states[k + 1]
            final = k == STEPS - 1
            shift = first if final else 0

            def forward(z, carry, k=k, src=src, dst=dst, shift=shift):
                c = src[z]
                below = src[z - 1]
                total = (below + src[z + 1]) + in_plane(c)
                change = coef[z] * (total - 6.0 * c) - speeds[k] * (c - below)
                bent = jnp.tanh(c)
                dst[z - shift] = c + time_step * change - time_step * sink_rate * bent
                keep[k, z] = 1.0 - time_step * sink_rate * (1.0 - bent * bent)
                return carry

            lax.fori_loop(1 + k, 3 * depth - 1 - k, forward, 0, unroll=2)
            if not final:
                clear(dst)

        for z in range(depth):
            offered[z] = jnp.dot(pick[...], state_ref[z], precision=HIGHEST, preferred_element_type=jnp.float32)
        pl.when(is_early)(lambda: pl.semaphore_wait(ready, ingots))
        sends = []
        for j in range(ingots):
            send = pltpu.make_async_remote_copy(
                src_ref=offered.at[:, slot_rows(j), :],
                dst_ref=slots.at[pl.ds(first, depth), pl.ds(pl.multiple_of(sec * PAIRCAP, PAIRCAP), PAIRCAP), :],
                send_sem=row_send.at[j], recv_sem=row_recv.at[sec], device_id=(melts + j, slab), device_id_type=MESH,
            )
            send.start()
            sends.append(send)
        keep3 = keep.at[3]
        keep_halo = halo(
            4, keep3, keep3, (pl.ds(first, depth - 1), pl.ds(last, depth - 1)), (pl.ds(first + 1, depth - 1), pl.ds(1, depth - 1))
        )
        start(keep_halo)

        for z in (first - 2, last + 1):
            bent = jnp.tanh(a2[z])
            keep[2, z] = 1.0 - time_step * sink_rate * (1.0 - bent * bent)
        wait_recv(edge_halo)
        wait_recv(dual_halo)
        wait_recv(keep_halo)

        passed = []
        for j in reversed(range(ingots)):
            region = returned.at[pl.ds(first, depth), slot_rows(j)]
            pltpu.make_async_copy(region, region, row_recv.at[j]).wait()
            passed.append(pass_on(returned, slot_rows(j), j))

        def add_returned(at):
            for z in range(at, at + depth):
                rows = jnp.dot(pick_t[...], returned[z], precision=HIGHEST, preferred_element_type=jnp.float32)
                value = dual[z] + rows
                dual[z] = value
                w_a[z] = coef[z] * value

        add_returned(first)

        @pl.when(has_left)
        def _():
            take(returned, 0)
            add_returned(0)

        @pl.when(has_right)
        def _():
            take(returned, 1)
            add_returned(last)

        mus = (adjoint_ref, mu_b, mu_a, mu_b, dual)
        ws = (None, w_b, w_a, w_b, w_a)
        for k in reversed(range(STEPS)):
            src, dst, wsrc, wdst = mus[k + 1], mus[k], ws[k + 1], ws[k]
            shift = first if k == 0 else 0

            def backward(z, carry, k=k, src=src, dst=dst, wsrc=wsrc, wdst=wdst, shift=shift):
                c, w = src[z], wsrc[z]
                total = (wsrc[z - 1] + wsrc[z + 1]) + in_plane(w)
                change = total - 6.0 * w - speeds[k] * (c - src[z + 1])
                value = keep[k, z] * c + time_step * change
                dst[z - shift] = value
                if wdst is not None:
                    wdst[z] = coef[z] * value
                return carry

            lax.fori_loop(first - k, last + k, backward, 0, unroll=2)
            if wdst is not None:
                clear(dst, wdst)

        for pair in [heat_halo, coef_halo, edge_halo, dual_halo, keep_halo] + passed:
            wait_send(pair)
        for send in sends:
            send.wait_send()

    @pl.when(jnp.logical_not(is_melt))
    def _():
        dual_near = halo(3, dual_ref, dual, lower(2), upper(2))
        coef_near = halo(1, factor_ref, coef, lower(1), upper(1))
        dual_far = halo(4, dual_ref, dual, lower(depth - 2, 2), upper(depth - 3, 2))
        coef_far = halo(2, factor_ref, coef, lower(depth - 2, 1), upper(depth - 3, 1))
        heat_halo = halo(0, heat_ref, heat, lower(depth), upper(depth - 1))
        start(dual_near)
        start(coef_near)
        start(coef_far)
        start(dual_far)
        for m in range(early):
            greet(m, slab, ready)
        rounds = []
        reach = CLOSE
        while reach < n_slab // 2:
            rounds.append(reach)
            reach *= 2

        def tell(index):
            for offset in (-rounds[index], rounds[index]):
                greet(sec, along(offset), known.at[index])

        if rounds:
            tell(0)
        clear(heat, dual)

        for load in tables:
            load.wait()
        mine = sec - melts
        names = part_ref[pl.ds(mine, 1), :].astype(jnp.float32)
        flags = flag_ref[pl.ds(mine, 1), :].astype(jnp.float32)
        names_col, flags_col = column(names), column(flags)
        same = jnp.where(names_col == names, 1.0, 0.0)
        rank_col = jnp.sum(jnp.where(lane_i < row_i, same, 0.0), axis=1, keepdims=True)
        rank_row = jnp.sum(jnp.where(row_i < lane_i, same, 0.0), axis=0, keepdims=True)
        count = melts * PAIRCAP
        slot_lane = lax.broadcasted_iota(jnp.int32, (contact, count), 1).astype(jnp.float32)
        slot_row = lax.broadcasted_iota(jnp.int32, (count, contact), 0).astype(jnp.float32)
        place = jnp.where(slot_lane == names_col * PAIRCAP + rank_col, flags_col, 0.0)
        give = jnp.where(slot_row == names * PAIRCAP + rank_row, flags, 0.0)

        for load in loads:
            load.wait()
        for index in range(len(rounds)):
            pl.semaphore_wait(known.at[index], 2)
            if index + 1 < len(rounds):
                tell(index + 1)

        def solve(which, t0, out, arrive_near, arrive_far, meanwhile, then):
            ts = (t0, a1, a2, a3)

            def grow(k, z):
                t = ts[k - 1]
                c = t[z]
                value = (coef[z] - (CENTRE - 6.0)) * c - ((t[z - 1] + t[z + 1]) + in_plane(c))
                if k == 1:
                    ts[k][z] = value * (1.0 / RADIUS)
                else:
                    ts[k][z] = value * (2.0 / RADIUS) - ts[k - 2][z]

            def grow_all(k, lo, hi):
                lax.fori_loop(lo, hi, lambda z, carry: grow(k, z) or carry, 0, unroll=2)

            def add_up(terms, count):
                def plane(z, sums):
                    return tuple(s + fold(term) for s, term in zip(sums, terms(z)))

                sums = lax.fori_loop(first, last, plane, (jnp.zeros((8, width), jnp.float32),) * count, unroll=2)
                return [jnp.sum(total, axis=0, keepdims=True) for total in sums]

            def near_terms(z):
                x0, x1, x2 = (ref[z] for ref in ts[:3])
                return x0 * x0, x0 * x1, x1 * x1, x1 * x2, x2 * x2

            def far_terms(z):
                x2, x3 = a2[z], a3[z]
                image = (coef[z] - (CENTRE - 6.0)) * x3 - 2.0 * a3[z + 1] - in_plane(x3)
                return x2 * x3, x3 * x3, x3 * image * (1.0 / RADIUS)

            arrive_near()
            grow_all(1, first - 1, last + 1)
            clear(a1)
            grow_all(2, first, last)
            sums = add_up(near_terms, 5)
            arrive_far()
            for z in (first - 2, last + 1, last + 2):
                grow(1, z)
            for z in (first - 1, last, last + 1):
                grow(2, z)
            clear(a2)
            grow_all(3, first, last)
            grow(3, last)
            clear(a3)
            sums += add_up(far_terms, 3)
            for k in range(8):
                sums_ref[pl.ds(k, 1), :] = sums[k]
            packed = pack(sums_ref[...])
            packed_ref[which] = packed
            for index, (_, shift) in enumerate(partners):
                pltpu.make_async_remote_copy(
                    src_ref=packed_ref.at[which], dst_ref=gather.at[which, pl.ds(index, 1)],
                    send_sem=sum_send.at[which], recv_sem=sum_recv.at[which],
                    device_id=(sec, partner(shift)), device_id_type=MESH,
                ).start()
            meanwhile()
            others = gather.at[which, pl.ds(0, n_slab - 1)]
            pltpu.make_async_copy(others, others, sum_recv.at[which]).wait()
            c = coefficients(packed + jnp.sum(gather[which, : n_slab - 1, :], axis=0, keepdims=True))
            then(c)

            def combine(z, carry):
                out[z - first] = (c[0] * ts[0][z] + c[1] * ts[1][z]) + (c[2] * ts[2][z] + c[3] * ts[3][z])
                return carry

            lax.fori_loop(first, last, combine, 0, unroll=2)

        def arrive_near():
            wait_recv(dual_near)
            wait_recv(coef_near)

        def arrive_far():
            wait_recv(coef_far)
            wait_recv(dual_far)
            start(heat_halo)

        def pick_basis():
            for i, t in enumerate((dual, a1, a2, a3)):
                for z in range(depth):
                    basis_rows[i, z] = jnp.dot(
                        give, t[first + z, :contact, :], precision=HIGHEST, preferred_element_type=jnp.float32
                    )

        sends = []

        def send_back(c):
            for z in range(depth):
                back[z] = (c[0] * basis_rows[0, z] + c[1] * basis_rows[1, z]) + (
                    c[2] * basis_rows[2, z] + c[3] * basis_rows[3, z]
                )
            for m in range(melts):
                if m == early:
                    pl.semaphore_wait(ready, melts - early)
                send = pltpu.make_async_remote_copy(
                    src_ref=back.at[:, slot_rows(m), :],
                    dst_ref=returned.at[pl.ds(first, depth), pl.ds(pl.multiple_of(mine * PAIRCAP, PAIRCAP), PAIRCAP), :],
                    send_sem=row_send.at[m], recv_sem=row_recv.at[mine], device_id=(m, slab), device_id_type=MESH,
                )
                send.start()
                sends.append(send)

        solve(0, dual, adjoint_ref, arrive_near, arrive_far, pick_basis, send_back)

        passed = []
        for m in range(melts):
            region = slots.at[pl.ds(first, depth), slot_rows(m)]
            pltpu.make_async_copy(region, region, row_recv.at[m]).wait()
            passed.append(pass_on(slots, slot_rows(m), m))

        def load_up(at):
            for z in range(at, at + depth):
                rows = jnp.dot(place, slots[z], precision=HIGHEST, preferred_element_type=jnp.float32)
                heat[z, pl.ds(0, contact), :] = heat[z, pl.ds(0, contact), :] + rows

        wait_recv(heat_halo)
        load_up(first)

        @pl.when(has_left)
        def _():
            take(slots, 0)
            load_up(0)

        @pl.when(has_right)
        def _():
            take(slots, 1)
            load_up(last)

        solve(1, heat, state_ref, lambda: None, lambda: None, lambda: None, lambda c: None)

        for pair in [dual_near, coef_near, dual_far, coef_far, heat_halo] + passed:
            wait_send(pair)
        for send in sends:
            send.wait_send()
        for which in range(2):
            others = gather.at[which, pl.ds(0, n_slab - 1)]
            pltpu.make_async_copy(others, others, sum_send.at[which]).wait()


def body(n_sec, n_slab, heat_level, material_factor, dual_sensitivity, part, line, flag, instant):
    ingots, contact = line.shape
    melts = n_sec - ingots
    _, depth, height, width = heat_level.shape
    f32 = jnp.float32
    wide = pltpu.VMEM((3 * depth, height, width), f32)
    table = pltpu.VMEM((ingots, contact), jnp.int32)
    dma = pltpu.SemaphoreType.DMA
    most = max(melts, ingots)
    scratch = [
        table, table, table,
        wide, wide, wide, wide, wide, wide,
        pltpu.VMEM((STEPS, 3 * depth, height, width), f32),
        wide, wide, wide, wide,
        pltpu.VMEM((ingots * PAIRCAP, height), f32),
        pltpu.VMEM((height, ingots * PAIRCAP), f32),
        pltpu.VMEM((depth, ingots * PAIRCAP, width), f32),
        pltpu.VMEM((3 * depth, melts * PAIRCAP, width), f32),
        pltpu.VMEM((depth, melts * PAIRCAP, width), f32),
        pltpu.VMEM((BASIS, depth, melts * PAIRCAP, width), f32),
        pltpu.VMEM((3 * depth, ingots * PAIRCAP, width), f32),
        pltpu.VMEM((8, width), f32),
        pltpu.VMEM((2, 1, width), f32),
        pltpu.VMEM((2, n_slab, width), f32),
        dma((6,)), dma((5, 2)), dma((5, 2)),
        dma((most,)), dma((most,)), dma((2, most)), dma((2,)),
        dma((2,)), dma((2,)), pltpu.SemaphoreType.REGULAR, pltpu.SemaphoreType.REGULAR((4,)),
    ]
    hbm, vmem, smem = (pl.BlockSpec(memory_space=s) for s in (pltpu.HBM, pltpu.VMEM, pltpu.SMEM))
    fields = (part[:, :, 0], line, flag, heat_level[0], material_factor[0], dual_sensitivity[0])
    fields = [pltpu.with_memory_space_constraint(field, pltpu.HBM) for field in fields]
    both = pl.pallas_call(
        functools.partial(kernel, n_sec, n_slab),
        out_shape=jax.ShapeDtypeStruct((2, depth, height, width), f32),
        in_specs=[hbm, hbm, hbm, smem, hbm, hbm, hbm],
        out_specs=vmem,
        scratch_shapes=scratch,
        compiler_params=pltpu.CompilerParams(
            collective_id=0, has_side_effects=True, vmem_limit_bytes=32 * 1024 * 1024
        ),
    )(*fields[:3], instant, *fields[3:])
    return both[0:1], both[1:2]


def solution(mesh):
    n_sec, n_slab = mesh.shape["sec"], mesh.shape["slab"]
    fields = P("sec", "slab", None, None)
    return jax.shard_map(
        functools.partial(body, n_sec, n_slab),
        mesh=mesh,
        in_specs=(fields, fields, fields, P(), P(), P(), P()),
        out_specs=(fields, fields),
        check_vma=False,
    )
```

```python
import functools
import math

import jax
import jax.numpy as jnp
from jax import lax
from jax.experimental import pallas as pl
from jax.experimental.pallas import tpu as pltpu
from jax.sharding import PartitionSpec as P

STEPS = 4
PAIRCAP = 8
BASIS = 4
CLOSE = 4

time_step = 0.1
sink_rate = 0.5
period_steps = 16.0

CENTRE = 6.8
RADIUS = 6.4

MESH = pl.DeviceIdType.MESH
HIGHEST = lax.Precision.HIGHEST


def in_plane(c):
    rows, cols = c.shape
    row = lax.broadcasted_iota(jnp.int32, c.shape, 0)
    col = lax.broadcasted_iota(jnp.int32, c.shape, 1)
    up = jnp.where(row == 0, 0.0, pltpu.roll(c, 1, 0))
    down = jnp.where(row == rows - 1, 0.0, pltpu.roll(c, rows - 1, 0))
    left = jnp.where(col == 0, 0.0, pltpu.roll(c, 1, 1))
    right = jnp.where(col == cols - 1, 0.0, pltpu.roll(c, cols - 1, 1))
    return (up + down) + (left + right)


def fold(values):
    rows, cols = values.shape
    return jnp.sum(values.reshape(rows // 8, 8, cols), axis=0)


def own_lanes(values):
    row = lax.broadcasted_iota(jnp.int32, values.shape, 0)
    lane = lax.broadcasted_iota(jnp.int32, values.shape, 1)
    each = values.shape[1] // values.shape[0]
    return jnp.where((lane >= row * each) & (lane < (row + 1) * each), values, 0.0)


def pack(values):
    lanes = values.shape[1]
    for distance in (lanes // 2, lanes // 4, lanes // 8):
        values = values + pltpu.roll(values, distance, 1)
    return jnp.sum(own_lanes(values), axis=0, keepdims=True)


def coefficients(packed):
    spread = own_lanes(jnp.broadcast_to(packed, (8, packed.shape[1])))
    total = jnp.broadcast_to(jnp.sum(spread, axis=1, keepdims=True), spread.shape)
    s = [total[k : k + 1, :] for k in range(8)]
    nu = [s[0], s[1], 2.0 * s[2] - s[0], 2.0 * s[3] - s[1], 2.0 * s[4] - s[0], 2.0 * s[5] - s[1], 2.0 * s[6] - s[0]]
    nu.append(4.0 * s[7] - 2.0 * s[5] - s[1])
    shift = 2.0 * CENTRE / RADIUS
    u = [shift * nu[k] + nu[k + 1] + nu[abs(k - 1)] for k in range(7)]
    mat = [[u[i + j] + u[abs(i - j)] for j in range(BASIS)] for i in range(BASIS)]
    diag = [mat[i][i] for i in range(BASIS)]
    rhs = [(4.0 / RADIUS) * nu[i] for i in range(BASIS)]
    inverse = []
    for k in range(BASIS):
        good = mat[k][k] > 1e-8 * diag[k]
        inv = jnp.where(good, 1.0 / jnp.where(good, mat[k][k], 1.0), 0.0)
        inverse.append(inv)
        for i in range(k + 1, BASIS):
            factor = mat[k][i] * inv
            for j in range(i, BASIS):
                mat[i][j] = mat[i][j] - factor * mat[k][j]
            rhs[i] = rhs[i] - factor * rhs[k]
    out = [None] * BASIS
    for i in reversed(range(BASIS)):
        value = rhs[i]
        for j in range(i + 1, BASIS):
            value = value - mat[i][j] * out[j]
        out[i] = value * inverse[i]
    return out


def relays(n_sec, ingots):
    if (n_sec, ingots) != (16, 4):
        return []
    return [(3, 5), (2, 5), (3, 6), (1, 5), (2, 6), (0, 4)]


def kernel(
    n_sec,
    n_slab,
    part_hbm,
    line_hbm,
    flag_hbm,
    instant_ref,
    heat_ref,
    factor_ref,
    dual_ref,
    both_ref,
    part_ref,
    line_ref,
    flag_ref,
    heat,
    coef,
    dual,
    a1,
    a2,
    a3,
    keep,
    mu3,
    mu2,
    mu1,
    w4,
    w3,
    w2,
    w1,
    pick,
    pick_t,
    offered,
    slots,
    back,
    basis_rows,
    relay,
    returned,
    sums_ref,
    packed_ref,
    gather,
    local_sem,
    halo_send,
    halo_recv,
    row_send,
    row_recv,
    side_send,
    side_recv,
    sum_send,
    sum_recv,
    ready,
    known,
    relay_send,
    relay_recv,
):
    ingots, contact = part_hbm.shape
    melts = n_sec - ingots
    early = 2 * melts // 3
    depth, height, width = heat_ref.shape
    first, last = depth, 2 * depth
    sec, slab = lax.axis_index("sec"), lax.axis_index("slab")
    is_melt = sec < melts
    is_early = sec < early
    relayed = relays(n_sec, ingots)
    targets = sorted({m for _, m in relayed})
    has_left, has_right = slab > 0, slab < n_slab - 1
    state_ref, adjoint_ref = both_ref.at[0], both_ref.at[1]

    loads = [
        pltpu.make_async_copy(src, dst.at[pl.ds(first, depth)], local_sem.at[i])
        for i, (src, dst) in enumerate(((heat_ref, heat), (factor_ref, coef), (dual_ref, dual)))
    ]
    tables = [
        pltpu.make_async_copy(src, dst, local_sem.at[3 + i])
        for i, (src, dst) in enumerate(((part_hbm, part_ref), (line_hbm, line_ref), (flag_hbm, flag_ref)))
    ]
    barrier = pltpu.get_barrier_semaphore()

    def greet(to_sec, to_slab, sem=barrier):
        pl.semaphore_signal(sem, inc=1, device_id=(to_sec, to_slab), device_id_type=MESH)

    def along(offset):
        return lax.rem(slab + offset % n_slab, n_slab)

    sizes = (4, 4, 2) if n_slab == 32 else (n_slab,)
    partners = []
    for flat in range(1, n_slab):
        shift, rest = [], flat
        for size in reversed(sizes):
            shift.insert(0, rest % size)
            rest //= size
        partners.append((sum(min(step, size - step) for step, size in zip(shift, sizes)), tuple(shift)))
    partners.sort(key=lambda entry: (-entry[0], entry[1]))

    def partner(shift):
        index, stride, rest = 0, 1, slab
        for step, size in zip(reversed(shift), reversed(sizes)):
            index = index + lax.rem(lax.rem(rest, size) + step, size) * stride
            rest, stride = rest // size, stride * size
        return index

    near = sorted({offset % n_slab for offset in range(-CLOSE, CLOSE + 1)} - {0})

    @pl.when(is_melt)
    def _():
        pl.when(has_left)(lambda: greet(sec, slab - 1))
        pl.when(has_right)(lambda: greet(sec, slab + 1))

        @pl.when(is_early)
        def _():
            for j in range(ingots):
                greet(melts + j, slab)

        for m in targets:
            pl.when(sec == m)(lambda: greet(early, slab))

    @pl.when(jnp.logical_not(is_melt))
    def _():
        for offset in near:
            greet(sec, along(offset))
        for m in range(early, melts):
            greet(m, slab)

    beside = has_left.astype(jnp.int32) + has_right.astype(jnp.int32)
    heard = jnp.where(is_melt, beside + jnp.where(is_early, 0, ingots), len(near) + early)
    heard = heard + jnp.where(sec == early, len(targets), 0) if targets else heard
    for load in tables + loads:
        load.start()
    pl.semaphore_wait(barrier, heard)

    def halo(index, src, dst, to_left, to_right):
        (left_src, left_dst), (right_src, right_dst) = to_left, to_right
        send, recv = halo_send.at[index], halo_recv.at[index]
        return (
            pltpu.make_async_remote_copy(
                src_ref=src.at[left_src], dst_ref=dst.at[left_dst], send_sem=send.at[0], recv_sem=recv.at[1],
                device_id=(sec, slab - 1), device_id_type=MESH,
            ),
            pltpu.make_async_remote_copy(
                src_ref=src.at[right_src], dst_ref=dst.at[right_dst], send_sem=send.at[1], recv_sem=recv.at[0],
                device_id=(sec, slab + 1), device_id_type=MESH,
            ),
        )

    def start(pair):
        pl.when(has_left)(lambda: pair[0].start())
        pl.when(has_right)(lambda: pair[1].start())

    def wait_recv(pair):
        pl.when(has_right)(lambda: pair[0].wait_recv())
        pl.when(has_left)(lambda: pair[1].wait_recv())

    def wait_send(pair):
        pl.when(has_left)(lambda: pair[0].wait_send())
        pl.when(has_right)(lambda: pair[1].wait_send())

    def lower(planes, offset=0):
        return pl.ds(offset, planes), pl.ds(last + offset, planes)

    def upper(planes, offset=0):
        at = depth - planes - offset
        return pl.ds(at, planes), pl.ds(at, planes)

    def pass_on(buf, rows, index):
        here = buf.at[pl.ds(first, depth), rows]
        pair = []
        for side, there, to in ((0, last, slab - 1), (1, 0, slab + 1)):
            pair.append(
                pltpu.make_async_remote_copy(
                    src_ref=here, dst_ref=buf.at[pl.ds(there, depth), rows], send_sem=side_send.at[side, index],
                    recv_sem=side_recv.at[1 - side], device_id=(sec, to), device_id_type=MESH,
                )
            )
        start(pair)
        return pair

    def take(buf, side):
        region = buf.at[pl.ds(2 * depth * side, depth)]
        pltpu.make_async_copy(region, region, side_recv.at[side]).wait()

    zero = jnp.zeros((height, width), jnp.float32)

    def clear(*bufs):
        @pl.when(jnp.logical_not(has_left))
        def _():
            for buf in bufs:
                buf[first - 1] = zero

        @pl.when(jnp.logical_not(has_right))
        def _():
            for buf in bufs:
                buf[last] = zero

    row_i = lax.broadcasted_iota(jnp.int32, (contact, contact), 0)
    lane_i = lax.broadcasted_iota(jnp.int32, (contact, contact), 1)

    def column(row):
        return jnp.sum(jnp.where(row_i == lane_i, row, 0.0), axis=1, keepdims=True)

    def slot_rows(index):
        return pl.ds(index * PAIRCAP, PAIRCAP)

    @pl.when(is_melt)
    def _():
        heat_halo = halo(0, heat_ref, heat, lower(depth), upper(depth))
        coef_halo = halo(1, factor_ref, coef, lower(depth - 1), upper(depth - 1))
        edge_halo = halo(2, factor_ref, coef, lower(1, depth - 1), upper(1, depth - 1))
        dual_halo = halo(3, dual_ref, dual, lower(depth), upper(depth))
        start(heat_halo)
        start(coef_halo)

        @pl.when(jnp.logical_not(is_early))
        def _():
            for j in range(ingots):
                greet(melts + j, slab, ready)

        clear(heat, dual, w4)
        for load in tables:
            load.wait()

        for j in range(ingots):
            named = part_ref[j : j + 1, :].astype(jnp.float32) == sec.astype(jnp.float32)
            lines = line_ref[j : j + 1, :].astype(jnp.float32)
            before = column(jnp.where(named, 1.0, 0.0))
            rank = jnp.sum(jnp.where(row_i < lane_i, before, 0.0), axis=0, keepdims=True)
            slot = lax.broadcasted_iota(jnp.int32, (PAIRCAP, contact), 0).astype(jnp.float32)
            chosen = jnp.where(named, 1.0, 0.0) * jnp.where(rank == slot, 1.0, 0.0)
            slot_line = jnp.sum(chosen * lines, axis=1, keepdims=True)
            live = jnp.sum(chosen, axis=1, keepdims=True)
            q = lax.broadcasted_iota(jnp.int32, (PAIRCAP, height), 1).astype(jnp.float32)
            pick[slot_rows(j), :] = jnp.where(q == slot_line, live, 0.0)
        eye = jnp.where(
            lax.broadcasted_iota(jnp.int32, (height, height), 0) == lax.broadcasted_iota(jnp.int32, (height, height), 1),
            1.0, 0.0,
        )
        pick_t[...] = lax.dot_general(
            eye, pick[...], (((1,), (1,)), ((), ())), precision=HIGHEST, preferred_element_type=jnp.float32
        )

        archived = instant_ref[0].astype(jnp.float32)
        speeds = []
        for k in range(STEPS):
            phase = jnp.full((1, width), archived + k)
            speeds.append(1.0 + 0.5 * jnp.sin(2.0 * math.pi * phase / period_steps))

        for load in loads:
            load.wait()
        wait_recv(heat_halo)
        wait_recv(coef_halo)
        start(edge_halo)
        start(dual_halo)

        states = (heat, a1, a2, a3, state_ref)
        for k in range(STEPS):
            src, dst = states[k], states[k + 1]
            final = k == STEPS - 1
            shift = first if final else 0

            def forward(z, carry, k=k, src=src, dst=dst, shift=shift):
                c = src[z]
                below = src[z - 1]
                total = (below + src[z + 1]) + in_plane(c)
                change = coef[z] * (total - 6.0 * c) - speeds[k] * (c - below)
                bent = jnp.tanh(c)
                dst[z - shift] = c + time_step * change - time_step * sink_rate * bent
                keep[k, z] = 1.0 - time_step * sink_rate * (1.0 - bent * bent)
                return carry

            lax.fori_loop(1 + k, 3 * depth - 1 - k, forward, 0, unroll=2)
            if not final:
                clear(dst)

        for z in range(depth):
            offered[z] = jnp.dot(pick[...], state_ref[z], precision=HIGHEST, preferred_element_type=jnp.float32)
        pl.when(is_early)(lambda: pl.semaphore_wait(ready, ingots))
        sends = []
        for j in range(ingots):
            send = pltpu.make_async_remote_copy(
                src_ref=offered.at[:, slot_rows(j), :],
                dst_ref=slots.at[pl.ds(first, depth), pl.ds(pl.multiple_of(sec * PAIRCAP, PAIRCAP), PAIRCAP), :],
                send_sem=row_send.at[j], recv_sem=row_recv.at[sec], device_id=(melts + j, slab), device_id_type=MESH,
            )
            send.start()
            sends.append(send)
        keep3 = keep.at[3]
        keep_halo = halo(
            4, keep3, keep3, (pl.ds(first, depth - 1), pl.ds(last, depth - 1)), (pl.ds(first + 1, depth - 1), pl.ds(1, depth - 1))
        )
        start(keep_halo)

        for z in (first - 2, last + 1):
            bent = jnp.tanh(a2[z])
            keep[2, z] = 1.0 - time_step * sink_rate * (1.0 - bent * bent)
        wait_recv(edge_halo)
        wait_recv(dual_halo)
        wait_recv(keep_halo)

        def relay_on(index):
            j, m = relayed[index]
            return pltpu.make_async_remote_copy(
                src_ref=relay.at[index], dst_ref=returned.at[pl.ds(first, depth), slot_rows(j), :],
                send_sem=relay_send.at[index], recv_sem=row_recv.at[j], device_id=(m, slab), device_id_type=MESH,
            )

        if relayed:

            @pl.when(sec == early)
            def _():
                for index in range(len(relayed)):
                    pltpu.make_async_copy(relay.at[index], relay.at[index], relay_recv.at[index]).wait()
                    relay_on(index).start()

        passed = []
        for j in reversed(range(ingots)):
            region = returned.at[pl.ds(first, depth), slot_rows(j)]
            pltpu.make_async_copy(region, region, row_recv.at[j]).wait()
            passed.append(pass_on(returned, slot_rows(j), j))

        def add_returned(at):
            for z in range(at, at + depth):
                rows = jnp.dot(pick_t[...], returned[z], precision=HIGHEST, preferred_element_type=jnp.float32)
                value = dual[z] + rows
                dual[z] = value
                w4[z] = coef[z] * value

        add_returned(first)

        mus, ws = (adjoint_ref, mu1, mu2, mu3, dual), (None, w1, w2, w3, w4)

        def backward(k, lo, hi):
            src, dst, wsrc, wdst = mus[k + 1], mus[k], ws[k + 1], ws[k]
            shift = first if k == 0 else 0

            def plane(z, carry):
                c, w = src[z], wsrc[z]
                total = (wsrc[z - 1] + wsrc[z + 1]) + in_plane(w)
                change = total - 6.0 * w - speeds[k] * (c - src[z + 1])
                value = keep[k, z] * c + time_step * change
                dst[z - shift] = value
                if wdst is not None:
                    wdst[z] = coef[z] * value
                return carry

            lax.fori_loop(lo, hi, plane, 0, unroll=2)
            if wdst is not None:
                clear(dst, wdst)

        @pl.when(slab % 2 == 0)
        def _():
            take(returned, 1)
            add_returned(last)
            for k in (3, 2, 1):
                backward(k, first + STEPS - k, last + k)

            @pl.when(has_left)
            def _():
                take(returned, 0)
                add_returned(0)

            for k in (3, 2, 1, 0):
                backward(k, first - k, first + STEPS - k)

        @pl.when(slab % 2 == 1)
        def _():
            take(returned, 0)
            add_returned(0)
            for k in (3, 2, 1):
                backward(k, first - k, last - STEPS + k)

            @pl.when(has_right)
            def _():
                take(returned, 1)
                add_returned(last)

            for k in (3, 2, 1, 0):
                backward(k, last - STEPS + k, last + k)

        if relayed:

            @pl.when(sec == early)
            def _():
                for index in range(len(relayed)):
                    relay_on(index).wait_send()

        for pair in [heat_halo, coef_halo, edge_halo, dual_halo, keep_halo] + passed:
            wait_send(pair)
        for send in sends:
            send.wait_send()

    @pl.when(jnp.logical_not(is_melt))
    def _():
        dual_near = halo(3, dual_ref, dual, lower(2), upper(2))
        coef_near = halo(1, factor_ref, coef, lower(1), upper(1))
        dual_far = halo(4, dual_ref, dual, lower(depth - 2, 2), upper(depth - 3, 2))
        coef_far = halo(2, factor_ref, coef, lower(depth - 2, 1), upper(depth - 3, 1))
        heat_halo = halo(0, heat_ref, heat, lower(depth), upper(depth - 1))
        start(dual_near)
        start(coef_near)
        start(coef_far)
        start(dual_far)
        for m in range(early):
            greet(m, slab, ready)
        rounds = []
        reach = CLOSE
        while reach < n_slab // 2:
            rounds.append(reach)
            reach *= 2

        def tell(index):
            for offset in (-rounds[index], rounds[index]):
                greet(sec, along(offset), known.at[index])

        if rounds:
            tell(0)
        clear(heat, dual)

        for load in tables:
            load.wait()
        mine = sec - melts
        names = part_ref[pl.ds(mine, 1), :].astype(jnp.float32)
        flags = flag_ref[pl.ds(mine, 1), :].astype(jnp.float32)
        names_col, flags_col = column(names), column(flags)
        same = jnp.where(names_col == names, 1.0, 0.0)
        rank_col = jnp.sum(jnp.where(lane_i < row_i, same, 0.0), axis=1, keepdims=True)
        rank_row = jnp.sum(jnp.where(row_i < lane_i, same, 0.0), axis=0, keepdims=True)
        count = melts * PAIRCAP
        slot_lane = lax.broadcasted_iota(jnp.int32, (contact, count), 1).astype(jnp.float32)
        slot_row = lax.broadcasted_iota(jnp.int32, (count, contact), 0).astype(jnp.float32)
        place = jnp.where(slot_lane == names_col * PAIRCAP + rank_col, flags_col, 0.0)
        give = jnp.where(slot_row == names * PAIRCAP + rank_row, flags, 0.0)

        for load in loads:
            load.wait()
        for index in range(len(rounds)):
            pl.semaphore_wait(known.at[index], 2)
            if index + 1 < len(rounds):
                tell(index + 1)

        def solve(which, t0, out, arrive_near, arrive_far, meanwhile, then):
            ts = (t0, a1, a2, a3)

            def grow(k, z):
                t = ts[k - 1]
                c = t[z]
                value = (coef[z] - (CENTRE - 6.0)) * c - ((t[z - 1] + t[z + 1]) + in_plane(c))
                if k == 1:
                    ts[k][z] = value * (1.0 / RADIUS)
                else:
                    ts[k][z] = value * (2.0 / RADIUS) - ts[k - 2][z]

            def grow_all(k, lo, hi):
                lax.fori_loop(lo, hi, lambda z, carry: grow(k, z) or carry, 0, unroll=2)

            def add_up(terms, count):
                def plane(z, sums):
                    return tuple(s + fold(term) for s, term in zip(sums, terms(z)))

                sums = lax.fori_loop(first, last, plane, (jnp.zeros((8, width), jnp.float32),) * count, unroll=2)
                return [jnp.sum(total, axis=0, keepdims=True) for total in sums]

            def near_terms(z):
                x0, x1, x2 = (ref[z] for ref in ts[:3])
                return x0 * x0, x0 * x1, x1 * x1, x1 * x2, x2 * x2

            def far_terms(z):
                x2, x3 = a2[z], a3[z]
                image = (coef[z] - (CENTRE - 6.0)) * x3 - 2.0 * a3[z + 1] - in_plane(x3)
                return x2 * x3, x3 * x3, x3 * image * (1.0 / RADIUS)

            arrive_near()
            grow_all(1, first - 1, last + 1)
            clear(a1)
            grow_all(2, first, last)
            sums = add_up(near_terms, 5)
            arrive_far()
            for z in (first - 2, last + 1, last + 2):
                grow(1, z)
            for z in (first - 1, last, last + 1):
                grow(2, z)
            clear(a2)
            grow_all(3, first, last)
            grow(3, last)
            clear(a3)
            sums += add_up(far_terms, 3)
            for k in range(8):
                sums_ref[pl.ds(k, 1), :] = sums[k]
            packed = pack(sums_ref[...])
            packed_ref[which] = packed
            for index, (_, shift) in enumerate(partners):
                pltpu.make_async_remote_copy(
                    src_ref=packed_ref.at[which], dst_ref=gather.at[which, pl.ds(index, 1)],
                    send_sem=sum_send.at[which], recv_sem=sum_recv.at[which],
                    device_id=(sec, partner(shift)), device_id_type=MESH,
                ).start()
            meanwhile()
            others = gather.at[which, pl.ds(0, n_slab - 1)]
            pltpu.make_async_copy(others, others, sum_recv.at[which]).wait()
            c = coefficients(packed + jnp.sum(gather[which, : n_slab - 1, :], axis=0, keepdims=True))
            then(c)

            def combine(z, carry):
                out[z - first] = (c[0] * ts[0][z] + c[1] * ts[1][z]) + (c[2] * ts[2][z] + c[3] * ts[3][z])
                return carry

            lax.fori_loop(first, last, combine, 0, unroll=2)

        def arrive_near():
            wait_recv(dual_near)
            wait_recv(coef_near)

        def arrive_far():
            wait_recv(coef_far)
            wait_recv(dual_far)
            start(heat_halo)

        def pick_basis():
            for i, t in enumerate((dual, a1, a2, a3)):
                for z in range(depth):
                    basis_rows[i, z] = jnp.dot(
                        give, t[first + z, :contact, :], precision=HIGHEST, preferred_element_type=jnp.float32
                    )

        sends = []

        def send_back(c):
            for z in range(depth):
                back[z] = (c[0] * basis_rows[0, z] + c[1] * basis_rows[1, z]) + (
                    c[2] * basis_rows[2, z] + c[3] * basis_rows[3, z]
                )
            pl.semaphore_wait(ready, melts - early)
            for index, (j, m) in enumerate(relayed):

                @pl.when(mine == j)
                def _():
                    pltpu.make_async_remote_copy(
                        src_ref=back.at[:, slot_rows(m), :], dst_ref=relay.at[index], send_sem=row_send.at[m],
                        recv_sem=relay_recv.at[index], device_id=(early, slab), device_id_type=MESH,
                    ).start()

            for m in range(melts):
                direct = [j for j in range(ingots) if (j, m) not in relayed]
                send = pltpu.make_async_remote_copy(
                    src_ref=back.at[:, slot_rows(m), :],
                    dst_ref=returned.at[pl.ds(first, depth), pl.ds(pl.multiple_of(mine * PAIRCAP, PAIRCAP), PAIRCAP), :],
                    send_sem=row_send.at[m], recv_sem=row_recv.at[mine], device_id=(m, slab), device_id_type=MESH,
                )
                if len(direct) == ingots:
                    send.start()
                elif direct:
                    pl.when(functools.reduce(jnp.logical_or, [mine == j for j in direct]))(lambda send=send: send.start())
                sends.append(send)

        solve(0, dual, adjoint_ref, arrive_near, arrive_far, pick_basis, send_back)

        passed = []
        for m in range(melts):
            region = slots.at[pl.ds(first, depth), slot_rows(m)]
            pltpu.make_async_copy(region, region, row_recv.at[m]).wait()
            passed.append(pass_on(slots, slot_rows(m), m))

        def load_up(at):
            for z in range(at, at + depth):
                rows = jnp.dot(place, slots[z], precision=HIGHEST, preferred_element_type=jnp.float32)
                heat[z, pl.ds(0, contact), :] = heat[z, pl.ds(0, contact), :] + rows

        wait_recv(heat_halo)
        load_up(first)

        @pl.when(has_left)
        def _():
            take(slots, 0)
            load_up(0)

        @pl.when(has_right)
        def _():
            take(slots, 1)
            load_up(last)

        solve(1, heat, state_ref, lambda: None, lambda: None, lambda: None, lambda c: None)

        for pair in [dual_near, coef_near, dual_far, coef_far, heat_halo] + passed:
            wait_send(pair)
        for send in sends:
            send.wait_send()
        for which in range(2):
            others = gather.at[which, pl.ds(0, n_slab - 1)]
            pltpu.make_async_copy(others, others, sum_send.at[which]).wait()


def body(n_sec, n_slab, heat_level, material_factor, dual_sensitivity, part, line, flag, instant):
    ingots, contact = line.shape
    melts = n_sec - ingots
    _, depth, height, width = heat_level.shape
    f32 = jnp.float32
    wide = pltpu.VMEM((3 * depth, height, width), f32)
    table = pltpu.VMEM((ingots, contact), jnp.int32)
    dma = pltpu.SemaphoreType.DMA
    most = max(melts, ingots)
    scratch = [
        table, table, table,
        wide, wide, wide, wide, wide, wide,
        pltpu.VMEM((STEPS, 3 * depth, height, width), f32),
        wide, wide, wide, wide, wide, wide, wide,
        pltpu.VMEM((ingots * PAIRCAP, height), f32),
        pltpu.VMEM((height, ingots * PAIRCAP), f32),
        pltpu.VMEM((depth, ingots * PAIRCAP, width), f32),
        pltpu.VMEM((3 * depth, melts * PAIRCAP, width), f32),
        pltpu.VMEM((depth, melts * PAIRCAP, width), f32),
        pltpu.VMEM((BASIS, depth, melts * PAIRCAP, width), f32),
        pltpu.VMEM((max(len(relays(n_sec, ingots)), 1), depth, PAIRCAP, width), f32),
        pltpu.VMEM((3 * depth, ingots * PAIRCAP, width), f32),
        pltpu.VMEM((8, width), f32),
        pltpu.VMEM((2, 1, width), f32),
        pltpu.VMEM((2, n_slab, width), f32),
        dma((6,)), dma((5, 2)), dma((5, 2)),
        dma((most,)), dma((most,)), dma((2, most)), dma((2,)),
        dma((2,)), dma((2,)), pltpu.SemaphoreType.REGULAR, pltpu.SemaphoreType.REGULAR((4,)),
        dma((8,)), dma((8,)),
    ]
    hbm, vmem, smem = (pl.BlockSpec(memory_space=s) for s in (pltpu.HBM, pltpu.VMEM, pltpu.SMEM))
    fields = (part[:, :, 0], line, flag, heat_level[0], material_factor[0], dual_sensitivity[0])
    fields = [pltpu.with_memory_space_constraint(field, pltpu.HBM) for field in fields]
    both = pl.pallas_call(
        functools.partial(kernel, n_sec, n_slab),
        out_shape=jax.ShapeDtypeStruct((2, depth, height, width), f32),
        in_specs=[hbm, hbm, hbm, smem, hbm, hbm, hbm],
        out_specs=vmem,
        scratch_shapes=scratch,
        compiler_params=pltpu.CompilerParams(
            collective_id=0, has_side_effects=True, vmem_limit_bytes=32 * 1024 * 1024
        ),
    )(*fields[:3], instant, *fields[3:])
    return both[0:1], both[1:2]


def solution(mesh):
    n_sec, n_slab = mesh.shape["sec"], mesh.shape["slab"]
    fields = P("sec", "slab", None, None)
    return jax.shard_map(
        functools.partial(body, n_sec, n_slab),
        mesh=mesh,
        in_specs=(fields, fields, fields, P(), P(), P(), P()),
        out_specs=(fields, fields),
        check_vma=False,
    )
```

```python
import functools
import math

import jax
import jax.numpy as jnp
from jax import lax
from jax.experimental import pallas as pl
from jax.experimental.pallas import tpu as pltpu
from jax.sharding import PartitionSpec as P

STEPS = 4
PAIRCAP = 8
BASIS = 4
CLOSE = 4

time_step = 0.1
sink_rate = 0.5
period_steps = 16.0

CENTRE = 6.8
RADIUS = 6.4

MESH = pl.DeviceIdType.MESH
HIGHEST = lax.Precision.HIGHEST


def in_plane(c):
    rows, cols = c.shape
    row = lax.broadcasted_iota(jnp.int32, c.shape, 0)
    col = lax.broadcasted_iota(jnp.int32, c.shape, 1)
    up = jnp.where(row == 0, 0.0, pltpu.roll(c, 1, 0))
    down = jnp.where(row == rows - 1, 0.0, pltpu.roll(c, rows - 1, 0))
    left = jnp.where(col == 0, 0.0, pltpu.roll(c, 1, 1))
    right = jnp.where(col == cols - 1, 0.0, pltpu.roll(c, cols - 1, 1))
    return (up + down) + (left + right)


def fold(values):
    rows, cols = values.shape
    return jnp.sum(values.reshape(rows // 8, 8, cols), axis=0)


def own_lanes(values):
    row = lax.broadcasted_iota(jnp.int32, values.shape, 0)
    lane = lax.broadcasted_iota(jnp.int32, values.shape, 1)
    each = values.shape[1] // values.shape[0]
    return jnp.where((lane >= row * each) & (lane < (row + 1) * each), values, 0.0)


def pack(values):
    lanes = values.shape[1]
    for distance in (lanes // 2, lanes // 4, lanes // 8):
        values = values + pltpu.roll(values, distance, 1)
    return jnp.sum(own_lanes(values), axis=0, keepdims=True)


def coefficients(packed):
    spread = own_lanes(jnp.broadcast_to(packed, (8, packed.shape[1])))
    total = jnp.broadcast_to(jnp.sum(spread, axis=1, keepdims=True), spread.shape)
    s = [total[k : k + 1, :] for k in range(8)]
    nu = [s[0], s[1], 2.0 * s[2] - s[0], 2.0 * s[3] - s[1], 2.0 * s[4] - s[0], 2.0 * s[5] - s[1], 2.0 * s[6] - s[0]]
    nu.append(4.0 * s[7] - 2.0 * s[5] - s[1])
    shift = 2.0 * CENTRE / RADIUS
    u = [shift * nu[k] + nu[k + 1] + nu[abs(k - 1)] for k in range(7)]
    mat = [[u[i + j] + u[abs(i - j)] for j in range(BASIS)] for i in range(BASIS)]
    diag = [mat[i][i] for i in range(BASIS)]
    rhs = [(4.0 / RADIUS) * nu[i] for i in range(BASIS)]
    inverse = []
    for k in range(BASIS):
        good = mat[k][k] > 1e-8 * diag[k]
        inv = jnp.where(good, 1.0 / jnp.where(good, mat[k][k], 1.0), 0.0)
        inverse.append(inv)
        for i in range(k + 1, BASIS):
            factor = mat[k][i] * inv
            for j in range(i, BASIS):
                mat[i][j] = mat[i][j] - factor * mat[k][j]
            rhs[i] = rhs[i] - factor * rhs[k]
    out = [None] * BASIS
    for i in reversed(range(BASIS)):
        value = rhs[i]
        for j in range(i + 1, BASIS):
            value = value - mat[i][j] * out[j]
        out[i] = value * inverse[i]
    return out


def relays(n_sec, ingots):
    if (n_sec, ingots) != (16, 4):
        return []
    return [(1, 5), (2, 5), (3, 5), (2, 6), (3, 6)]


def kernel(
    n_sec,
    n_slab,
    part_hbm,
    line_hbm,
    flag_hbm,
    instant_ref,
    heat_ref,
    factor_ref,
    dual_ref,
    both_ref,
    part_ref,
    line_ref,
    flag_ref,
    heat,
    coef,
    dual,
    a1,
    a2,
    a3,
    keep,
    mu3,
    mu2,
    mu1,
    w4,
    w3,
    w2,
    w1,
    pick,
    pick_t,
    offered,
    slots,
    back,
    basis_rows,
    relay,
    returned,
    sums_ref,
    packed_ref,
    gather,
    local_sem,
    halo_send,
    halo_recv,
    row_send,
    row_recv,
    side_send,
    side_recv,
    sum_send,
    sum_recv,
    ready,
    known,
    relay_send,
    relay_recv,
):
    ingots, contact = part_hbm.shape
    melts = n_sec - ingots
    early = 2 * melts // 3
    depth, height, width = heat_ref.shape
    first, last = depth, 2 * depth
    sec, slab = lax.axis_index("sec"), lax.axis_index("slab")
    is_melt = sec < melts
    is_early = sec < early
    relayed = relays(n_sec, ingots)
    targets = sorted({m for _, m in relayed})
    has_left, has_right = slab > 0, slab < n_slab - 1
    state_ref, adjoint_ref = both_ref.at[0], both_ref.at[1]

    loads = [
        pltpu.make_async_copy(src, dst.at[pl.ds(first, depth)], local_sem.at[i])
        for i, (src, dst) in enumerate(((heat_ref, heat), (factor_ref, coef), (dual_ref, dual)))
    ]
    tables = [
        pltpu.make_async_copy(src, dst, local_sem.at[3 + i])
        for i, (src, dst) in enumerate(((part_hbm, part_ref), (line_hbm, line_ref), (flag_hbm, flag_ref)))
    ]
    barrier = pltpu.get_barrier_semaphore()

    def greet(to_sec, to_slab, sem=barrier):
        pl.semaphore_signal(sem, inc=1, device_id=(to_sec, to_slab), device_id_type=MESH)

    def along(offset):
        return lax.rem(slab + offset % n_slab, n_slab)

    sizes = (4, 4, 2) if n_slab == 32 else (n_slab,)
    partners = []
    for flat in range(1, n_slab):
        shift, rest = [], flat
        for size in reversed(sizes):
            shift.insert(0, rest % size)
            rest //= size
        partners.append((sum(min(step, size - step) for step, size in zip(shift, sizes)), tuple(shift)))
    partners.sort(key=lambda entry: (-entry[0], entry[1]))

    def partner(shift):
        index, stride, rest = 0, 1, slab
        for step, size in zip(reversed(shift), reversed(sizes)):
            index = index + lax.rem(lax.rem(rest, size) + step, size) * stride
            rest, stride = rest // size, stride * size
        return index

    near = sorted({offset % n_slab for offset in range(-CLOSE, CLOSE + 1)} - {0})

    @pl.when(is_melt)
    def _():
        pl.when(has_left)(lambda: greet(sec, slab - 1))
        pl.when(has_right)(lambda: greet(sec, slab + 1))

        @pl.when(is_early)
        def _():
            for j in range(ingots):
                greet(melts + j, slab)

        for m in targets:
            pl.when(sec == m)(lambda: greet(early, slab))

    @pl.when(jnp.logical_not(is_melt))
    def _():
        for offset in near:
            greet(sec, along(offset))
        for m in range(early, melts):
            greet(m, slab)

    beside = has_left.astype(jnp.int32) + has_right.astype(jnp.int32)
    heard = jnp.where(is_melt, beside + jnp.where(is_early, 0, ingots), len(near) + early)
    heard = heard + jnp.where(sec == early, len(targets), 0) if targets else heard
    for load in tables + loads:
        load.start()
    pl.semaphore_wait(barrier, heard)

    def halo(index, src, dst, to_left, to_right):
        (left_src, left_dst), (right_src, right_dst) = to_left, to_right
        send, recv = halo_send.at[index], halo_recv.at[index]
        return (
            pltpu.make_async_remote_copy(
                src_ref=src.at[left_src], dst_ref=dst.at[left_dst], send_sem=send.at[0], recv_sem=recv.at[1],
                device_id=(sec, slab - 1), device_id_type=MESH,
            ),
            pltpu.make_async_remote_copy(
                src_ref=src.at[right_src], dst_ref=dst.at[right_dst], send_sem=send.at[1], recv_sem=recv.at[0],
                device_id=(sec, slab + 1), device_id_type=MESH,
            ),
        )

    def start(pair):
        pl.when(has_left)(lambda: pair[0].start())
        pl.when(has_right)(lambda: pair[1].start())

    def wait_recv(pair):
        pl.when(has_right)(lambda: pair[0].wait_recv())
        pl.when(has_left)(lambda: pair[1].wait_recv())

    def wait_send(pair):
        pl.when(has_left)(lambda: pair[0].wait_send())
        pl.when(has_right)(lambda: pair[1].wait_send())

    def lower(planes, offset=0):
        return pl.ds(offset, planes), pl.ds(last + offset, planes)

    def upper(planes, offset=0):
        at = depth - planes - offset
        return pl.ds(at, planes), pl.ds(at, planes)

    def pass_on(buf, rows, index):
        here = buf.at[pl.ds(first, depth), rows]
        pair = []
        for side, there, to in ((0, last, slab - 1), (1, 0, slab + 1)):
            pair.append(
                pltpu.make_async_remote_copy(
                    src_ref=here, dst_ref=buf.at[pl.ds(there, depth), rows], send_sem=side_send.at[side, index],
                    recv_sem=side_recv.at[1 - side], device_id=(sec, to), device_id_type=MESH,
                )
            )
        start(pair)
        return pair

    def take(buf, side):
        region = buf.at[pl.ds(2 * depth * side, depth)]
        pltpu.make_async_copy(region, region, side_recv.at[side]).wait()

    zero = jnp.zeros((height, width), jnp.float32)

    def clear(*bufs):
        @pl.when(jnp.logical_not(has_left))
        def _():
            for buf in bufs:
                buf[first - 1] = zero

        @pl.when(jnp.logical_not(has_right))
        def _():
            for buf in bufs:
                buf[last] = zero

    row_i = lax.broadcasted_iota(jnp.int32, (contact, contact), 0)
    lane_i = lax.broadcasted_iota(jnp.int32, (contact, contact), 1)

    def column(row):
        return jnp.sum(jnp.where(row_i == lane_i, row, 0.0), axis=1, keepdims=True)

    def slot_rows(index):
        return pl.ds(index * PAIRCAP, PAIRCAP)

    @pl.when(is_melt)
    def _():
        heat_halo = halo(0, heat_ref, heat, lower(depth), upper(depth))
        coef_halo = halo(1, factor_ref, coef, lower(depth - 1), upper(depth - 1))
        edge_halo = halo(2, factor_ref, coef, lower(1, depth - 1), upper(1, depth - 1))
        dual_halo = halo(3, dual_ref, dual, lower(depth), upper(depth))
        start(heat_halo)
        start(coef_halo)

        @pl.when(jnp.logical_not(is_early))
        def _():
            for j in range(ingots):
                greet(melts + j, slab, ready)

        clear(heat, dual, w4)
        for load in tables:
            load.wait()

        for j in range(ingots):
            named = part_ref[j : j + 1, :].astype(jnp.float32) == sec.astype(jnp.float32)
            lines = line_ref[j : j + 1, :].astype(jnp.float32)
            before = column(jnp.where(named, 1.0, 0.0))
            rank = jnp.sum(jnp.where(row_i < lane_i, before, 0.0), axis=0, keepdims=True)
            slot = lax.broadcasted_iota(jnp.int32, (PAIRCAP, contact), 0).astype(jnp.float32)
            chosen = jnp.where(named, 1.0, 0.0) * jnp.where(rank == slot, 1.0, 0.0)
            slot_line = jnp.sum(chosen * lines, axis=1, keepdims=True)
            live = jnp.sum(chosen, axis=1, keepdims=True)
            q = lax.broadcasted_iota(jnp.int32, (PAIRCAP, height), 1).astype(jnp.float32)
            pick[slot_rows(j), :] = jnp.where(q == slot_line, live, 0.0)
        eye = jnp.where(
            lax.broadcasted_iota(jnp.int32, (height, height), 0) == lax.broadcasted_iota(jnp.int32, (height, height), 1),
            1.0, 0.0,
        )
        pick_t[...] = lax.dot_general(
            eye, pick[...], (((1,), (1,)), ((), ())), precision=HIGHEST, preferred_element_type=jnp.float32
        )

        archived = instant_ref[0].astype(jnp.float32)
        speeds = []
        for k in range(STEPS):
            phase = jnp.full((1, width), archived + k)
            speeds.append(1.0 + 0.5 * jnp.sin(2.0 * math.pi * phase / period_steps))

        for load in loads:
            load.wait()
        wait_recv(heat_halo)
        wait_recv(coef_halo)
        start(edge_halo)
        start(dual_halo)

        states = (heat, a1, a2, a3, state_ref)
        for k in range(STEPS):
            src, dst = states[k], states[k + 1]
            final = k == STEPS - 1
            shift = first if final else 0

            def forward(z, carry, k=k, src=src, dst=dst, shift=shift):
                c = src[z]
                below = src[z - 1]
                total = (below + src[z + 1]) + in_plane(c)
                change = coef[z] * (total - 6.0 * c) - speeds[k] * (c - below)
                bent = jnp.tanh(c)
                dst[z - shift] = c + time_step * change - time_step * sink_rate * bent
                keep[k, z] = 1.0 - time_step * sink_rate * (1.0 - bent * bent)
                return carry

            lax.fori_loop(1 + k, 3 * depth - 1 - k, forward, 0, unroll=2)
            if not final:
                clear(dst)

        for z in range(depth):
            offered[z] = jnp.dot(pick[...], state_ref[z], precision=HIGHEST, preferred_element_type=jnp.float32)
        pl.when(is_early)(lambda: pl.semaphore_wait(ready, ingots))
        sends = []
        for j in range(ingots):
            send = pltpu.make_async_remote_copy(
                src_ref=offered.at[:, slot_rows(j), :],
                dst_ref=slots.at[pl.ds(first, depth), pl.ds(pl.multiple_of(sec * PAIRCAP, PAIRCAP), PAIRCAP), :],
                send_sem=row_send.at[j], recv_sem=row_recv.at[sec], device_id=(melts + j, slab), device_id_type=MESH,
            )
            send.start()
            sends.append(send)
        keep3 = keep.at[3]
        keep_halo = halo(
            4, keep3, keep3, (pl.ds(first, depth - 1), pl.ds(last, depth - 1)), (pl.ds(first + 1, depth - 1), pl.ds(1, depth - 1))
        )
        start(keep_halo)

        for z in (first - 2, last + 1):
            bent = jnp.tanh(a2[z])
            keep[2, z] = 1.0 - time_step * sink_rate * (1.0 - bent * bent)
        wait_recv(edge_halo)
        wait_recv(dual_halo)
        wait_recv(keep_halo)

        def relay_on(index):
            j, m = relayed[index]
            return pltpu.make_async_remote_copy(
                src_ref=relay.at[index], dst_ref=returned.at[pl.ds(first, depth), slot_rows(j), :],
                send_sem=relay_send.at[index], recv_sem=row_recv.at[j], device_id=(m, slab), device_id_type=MESH,
            )

        if relayed:

            @pl.when(sec == early)
            def _():
                for index in range(len(relayed)):
                    pltpu.make_async_copy(relay.at[index], relay.at[index], relay_recv.at[index]).wait()
                    relay_on(index).start()

        passed = []
        for j in reversed(range(ingots)):
            region = returned.at[pl.ds(first, depth), slot_rows(j)]
            pltpu.make_async_copy(region, region, row_recv.at[j]).wait()
            passed.append(pass_on(returned, slot_rows(j), j))

        def add_returned(at):
            for z in range(at, at + depth):
                rows = jnp.dot(pick_t[...], returned[z], precision=HIGHEST, preferred_element_type=jnp.float32)
                value = dual[z] + rows
                dual[z] = value
                w4[z] = coef[z] * value

        add_returned(first)

        mus, ws = (adjoint_ref, mu1, mu2, mu3, dual), (None, w1, w2, w3, w4)

        def backward(k, lo, hi):
            src, dst, wsrc, wdst = mus[k + 1], mus[k], ws[k + 1], ws[k]
            shift = first if k == 0 else 0

            def plane(z, carry):
                c, w = src[z], wsrc[z]
                total = (wsrc[z - 1] + wsrc[z + 1]) + in_plane(w)
                change = total - 6.0 * w - speeds[k] * (c - src[z + 1])
                value = keep[k, z] * c + time_step * change
                dst[z - shift] = value
                if wdst is not None:
                    wdst[z] = coef[z] * value
                return carry

            lax.fori_loop(lo, hi, plane, 0, unroll=2)
            if wdst is not None:
                clear(dst, wdst)

        @pl.when(slab % 2 == 0)
        def _():
            take(returned, 1)
            add_returned(last)
            for k in (3, 2, 1):
                backward(k, first + STEPS - k, last + k)

            @pl.when(has_left)
            def _():
                take(returned, 0)
                add_returned(0)

            for k in (3, 2, 1, 0):
                backward(k, first - k, first + STEPS - k)

        @pl.when(slab % 2 == 1)
        def _():
            take(returned, 0)
            add_returned(0)
            for k in (3, 2, 1):
                backward(k, first - k, last - STEPS + k)

            @pl.when(has_right)
            def _():
                take(returned, 1)
                add_returned(last)

            for k in (3, 2, 1, 0):
                backward(k, last - STEPS + k, last + k)

        if relayed:

            @pl.when(sec == early)
            def _():
                for index in range(len(relayed)):
                    relay_on(index).wait_send()

        for pair in [heat_halo, coef_halo, edge_halo, dual_halo, keep_halo] + passed:
            wait_send(pair)
        for send in sends:
            send.wait_send()

    @pl.when(jnp.logical_not(is_melt))
    def _():
        dual_near = halo(3, dual_ref, dual, lower(2), upper(2))
        coef_near = halo(1, factor_ref, coef, lower(1), upper(1))
        dual_far = halo(4, dual_ref, dual, lower(depth - 2, 2), upper(depth - 3, 2))
        coef_far = halo(2, factor_ref, coef, lower(depth - 2, 1), upper(depth - 3, 1))
        heat_halo = halo(0, heat_ref, heat, lower(depth), upper(depth - 1))
        start(dual_near)
        start(coef_near)
        start(coef_far)
        start(dual_far)
        for m in range(early):
            greet(m, slab, ready)
        rounds = []
        reach = CLOSE
        while reach < n_slab // 2:
            rounds.append(reach)
            reach *= 2

        def tell(index):
            for offset in (-rounds[index], rounds[index]):
                greet(sec, along(offset), known.at[index])

        if rounds:
            tell(0)
        clear(heat, dual)

        for load in tables:
            load.wait()
        mine = sec - melts
        names = part_ref[pl.ds(mine, 1), :].astype(jnp.float32)
        flags = flag_ref[pl.ds(mine, 1), :].astype(jnp.float32)
        names_col, flags_col = column(names), column(flags)
        same = jnp.where(names_col == names, 1.0, 0.0)
        rank_col = jnp.sum(jnp.where(lane_i < row_i, same, 0.0), axis=1, keepdims=True)
        rank_row = jnp.sum(jnp.where(row_i < lane_i, same, 0.0), axis=0, keepdims=True)
        count = melts * PAIRCAP
        slot_lane = lax.broadcasted_iota(jnp.int32, (contact, count), 1).astype(jnp.float32)
        slot_row = lax.broadcasted_iota(jnp.int32, (count, contact), 0).astype(jnp.float32)
        place = jnp.where(slot_lane == names_col * PAIRCAP + rank_col, flags_col, 0.0)
        give = jnp.where(slot_row == names * PAIRCAP + rank_row, flags, 0.0)

        for load in loads:
            load.wait()
        told = [0]

        def hear(count):
            while told[0] < min(count, len(rounds)):
                pl.semaphore_wait(known.at[told[0]], 2)
                told[0] += 1
                if told[0] < len(rounds):
                    tell(told[0])

        def solve(which, t0, out, arrive_near, arrive_far, meanwhile, then):
            ts = (t0, a1, a2, a3)

            def grow(k, z):
                t = ts[k - 1]
                c = t[z]
                value = (coef[z] - (CENTRE - 6.0)) * c - ((t[z - 1] + t[z + 1]) + in_plane(c))
                if k == 1:
                    ts[k][z] = value * (1.0 / RADIUS)
                else:
                    ts[k][z] = value * (2.0 / RADIUS) - ts[k - 2][z]

            def grow_all(k, lo, hi):
                lax.fori_loop(lo, hi, lambda z, carry: grow(k, z) or carry, 0, unroll=2)

            def add_up(terms, count):
                def plane(z, sums):
                    return tuple(s + fold(term) for s, term in zip(sums, terms(z)))

                sums = lax.fori_loop(first, last, plane, (jnp.zeros((8, width), jnp.float32),) * count, unroll=2)
                return [jnp.sum(total, axis=0, keepdims=True) for total in sums]

            def near_terms(z):
                x0, x1, x2 = (ref[z] for ref in ts[:3])
                return x0 * x0, x0 * x1, x1 * x1, x1 * x2, x2 * x2

            def far_terms(z):
                x2, x3 = a2[z], a3[z]
                image = (coef[z] - (CENTRE - 6.0)) * x3 - 2.0 * a3[z + 1] - in_plane(x3)
                return x2 * x3, x3 * x3, x3 * image * (1.0 / RADIUS)

            arrive_near()
            grow_all(1, first - 1, last + 1)
            clear(a1)
            grow_all(2, first, last)
            sums = add_up(near_terms, 5)
            arrive_far()
            for z in (first - 2, last + 1, last + 2):
                grow(1, z)
            for z in (first - 1, last, last + 1):
                grow(2, z)
            clear(a2)
            grow_all(3, first, last)
            grow(3, last)
            clear(a3)
            sums += add_up(far_terms, 3)
            for k in range(8):
                sums_ref[pl.ds(k, 1), :] = sums[k]
            hear(len(rounds))
            packed = pack(sums_ref[...])
            packed_ref[which] = packed
            for index, (_, shift) in enumerate(partners):
                pltpu.make_async_remote_copy(
                    src_ref=packed_ref.at[which], dst_ref=gather.at[which, pl.ds(index, 1)],
                    send_sem=sum_send.at[which], recv_sem=sum_recv.at[which],
                    device_id=(sec, partner(shift)), device_id_type=MESH,
                ).start()
            meanwhile()
            others = gather.at[which, pl.ds(0, n_slab - 1)]
            pltpu.make_async_copy(others, others, sum_recv.at[which]).wait()
            c = coefficients(packed + jnp.sum(gather[which, : n_slab - 1, :], axis=0, keepdims=True))
            then(c)

            def combine(z, carry):
                out[z - first] = (c[0] * ts[0][z] + c[1] * ts[1][z]) + (c[2] * ts[2][z] + c[3] * ts[3][z])
                return carry

            lax.fori_loop(first, last, combine, 0, unroll=2)

        def arrive_near():
            hear(1)
            wait_recv(dual_near)
            wait_recv(coef_near)

        def arrive_far():
            hear(2)
            wait_recv(coef_far)
            wait_recv(dual_far)
            start(heat_halo)

        def pick_basis():
            for i, t in enumerate((dual, a1, a2, a3)):
                for z in range(depth):
                    basis_rows[i, z] = jnp.dot(
                        give, t[first + z, :contact, :], precision=HIGHEST, preferred_element_type=jnp.float32
                    )

        sends = []

        def send_back(c):
            for z in range(depth):
                back[z] = (c[0] * basis_rows[0, z] + c[1] * basis_rows[1, z]) + (
                    c[2] * basis_rows[2, z] + c[3] * basis_rows[3, z]
                )
            pl.semaphore_wait(ready, melts - early)
            for index, (j, m) in enumerate(relayed):

                @pl.when(mine == j)
                def _():
                    pltpu.make_async_remote_copy(
                        src_ref=back.at[:, slot_rows(m), :], dst_ref=relay.at[index], send_sem=row_send.at[m],
                        recv_sem=relay_recv.at[index], device_id=(early, slab), device_id_type=MESH,
                    ).start()

            for m in range(melts):
                direct = [j for j in range(ingots) if (j, m) not in relayed]
                send = pltpu.make_async_remote_copy(
                    src_ref=back.at[:, slot_rows(m), :],
                    dst_ref=returned.at[pl.ds(first, depth), pl.ds(pl.multiple_of(mine * PAIRCAP, PAIRCAP), PAIRCAP), :],
                    send_sem=row_send.at[m], recv_sem=row_recv.at[mine], device_id=(m, slab), device_id_type=MESH,
                )
                if len(direct) == ingots:
                    send.start()
                elif direct:
                    pl.when(functools.reduce(jnp.logical_or, [mine == j for j in direct]))(lambda send=send: send.start())
                sends.append(send)

        solve(0, dual, adjoint_ref, arrive_near, arrive_far, pick_basis, send_back)

        passed = []
        for m in range(melts):
            region = slots.at[pl.ds(first, depth), slot_rows(m)]
            pltpu.make_async_copy(region, region, row_recv.at[m]).wait()
            passed.append(pass_on(slots, slot_rows(m), m))

        def load_up(at):
            for z in range(at, at + depth):
                rows = jnp.dot(place, slots[z], precision=HIGHEST, preferred_element_type=jnp.float32)
                heat[z, pl.ds(0, contact), :] = heat[z, pl.ds(0, contact), :] + rows

        wait_recv(heat_halo)
        load_up(first)

        @pl.when(has_left)
        def _():
            take(slots, 0)
            load_up(0)

        @pl.when(has_right)
        def _():
            take(slots, 1)
            load_up(last)

        solve(1, heat, state_ref, lambda: None, lambda: None, lambda: None, lambda c: None)

        for pair in [dual_near, coef_near, dual_far, coef_far, heat_halo] + passed:
            wait_send(pair)
        for send in sends:
            send.wait_send()
        for which in range(2):
            others = gather.at[which, pl.ds(0, n_slab - 1)]
            pltpu.make_async_copy(others, others, sum_send.at[which]).wait()


def body(n_sec, n_slab, heat_level, material_factor, dual_sensitivity, part, line, flag, instant):
    ingots, contact = line.shape
    melts = n_sec - ingots
    _, depth, height, width = heat_level.shape
    f32 = jnp.float32
    wide = pltpu.VMEM((3 * depth, height, width), f32)
    table = pltpu.VMEM((ingots, contact), jnp.int32)
    dma = pltpu.SemaphoreType.DMA
    most = max(melts, ingots)
    scratch = [
        table, table, table,
        wide, wide, wide, wide, wide, wide,
        pltpu.VMEM((STEPS, 3 * depth, height, width), f32),
        wide, wide, wide, wide, wide, wide, wide,
        pltpu.VMEM((ingots * PAIRCAP, height), f32),
        pltpu.VMEM((height, ingots * PAIRCAP), f32),
        pltpu.VMEM((depth, ingots * PAIRCAP, width), f32),
        pltpu.VMEM((3 * depth, melts * PAIRCAP, width), f32),
        pltpu.VMEM((depth, melts * PAIRCAP, width), f32),
        pltpu.VMEM((BASIS, depth, melts * PAIRCAP, width), f32),
        pltpu.VMEM((max(len(relays(n_sec, ingots)), 1), depth, PAIRCAP, width), f32),
        pltpu.VMEM((3 * depth, ingots * PAIRCAP, width), f32),
        pltpu.VMEM((8, width), f32),
        pltpu.VMEM((2, 1, width), f32),
        pltpu.VMEM((2, n_slab, width), f32),
        dma((6,)), dma((5, 2)), dma((5, 2)),
        dma((most,)), dma((most,)), dma((2, most)), dma((2,)),
        dma((2,)), dma((2,)), pltpu.SemaphoreType.REGULAR, pltpu.SemaphoreType.REGULAR((4,)),
        dma((8,)), dma((8,)),
    ]
    hbm, vmem, smem = (pl.BlockSpec(memory_space=s) for s in (pltpu.HBM, pltpu.VMEM, pltpu.SMEM))
    fields = (part[:, :, 0], line, flag, heat_level[0], material_factor[0], dual_sensitivity[0])
    fields = [pltpu.with_memory_space_constraint(field, pltpu.HBM) for field in fields]
    both = pl.pallas_call(
        functools.partial(kernel, n_sec, n_slab),
        out_shape=jax.ShapeDtypeStruct((2, depth, height, width), f32),
        in_specs=[hbm, hbm, hbm, smem, hbm, hbm, hbm],
        out_specs=vmem,
        scratch_shapes=scratch,
        compiler_params=pltpu.CompilerParams(
            collective_id=0, has_side_effects=True, vmem_limit_bytes=32 * 1024 * 1024
        ),
    )(*fields[:3], instant, *fields[3:])
    return both[0:1], both[1:2]


def solution(mesh):
    n_sec, n_slab = mesh.shape["sec"], mesh.shape["slab"]
    fields = P("sec", "slab", None, None)
    return jax.shard_map(
        functools.partial(body, n_sec, n_slab),
        mesh=mesh,
        in_specs=(fields, fields, fields, P(), P(), P(), P()),
        out_specs=(fields, fields),
        check_vma=False,
    )
```

```python
import functools
import math

import jax
import jax.numpy as jnp
from jax import lax
from jax.experimental import pallas as pl
from jax.experimental.pallas import tpu as pltpu
from jax.sharding import PartitionSpec as P

STEPS = 4
PAIRCAP = 8
BASIS = 4
AHEAD = 1
CLOSE = 4

time_step = 0.1
sink_rate = 0.5
period_steps = 16.0

CENTRE = 6.8
RADIUS = 6.4

MESH = pl.DeviceIdType.MESH
HIGHEST = lax.Precision.HIGHEST


def in_plane(c):
    rows, cols = c.shape
    row = lax.broadcasted_iota(jnp.int32, c.shape, 0)
    col = lax.broadcasted_iota(jnp.int32, c.shape, 1)
    up = jnp.where(row == 0, 0.0, pltpu.roll(c, 1, 0))
    down = jnp.where(row == rows - 1, 0.0, pltpu.roll(c, rows - 1, 0))
    left = jnp.where(col == 0, 0.0, pltpu.roll(c, 1, 1))
    right = jnp.where(col == cols - 1, 0.0, pltpu.roll(c, cols - 1, 1))
    return (up + down) + (left + right)


def fold(values):
    rows, cols = values.shape
    return jnp.sum(values.reshape(rows // 8, 8, cols), axis=0)


def own_lanes(values):
    row = lax.broadcasted_iota(jnp.int32, values.shape, 0)
    lane = lax.broadcasted_iota(jnp.int32, values.shape, 1)
    each = values.shape[1] // values.shape[0]
    return jnp.where((lane >= row * each) & (lane < (row + 1) * each), values, 0.0)


def pack(values):
    lanes = values.shape[1]
    for distance in (lanes // 2, lanes // 4, lanes // 8):
        values = values + pltpu.roll(values, distance, 1)
    return jnp.sum(own_lanes(values), axis=0, keepdims=True)


def coefficients(packed):
    spread = own_lanes(jnp.broadcast_to(packed, (8, packed.shape[1])))
    total = jnp.broadcast_to(jnp.sum(spread, axis=1, keepdims=True), spread.shape)
    s = [total[k : k + 1, :] for k in range(8)]
    nu = [s[0], s[1], 2.0 * s[2] - s[0], 2.0 * s[3] - s[1], 2.0 * s[4] - s[0], 2.0 * s[5] - s[1], 2.0 * s[6] - s[0]]
    nu.append(4.0 * s[7] - 2.0 * s[5] - s[1])
    shift = 2.0 * CENTRE / RADIUS
    u = [shift * nu[k] + nu[k + 1] + nu[abs(k - 1)] for k in range(7)]
    mat = [[u[i + j] + u[abs(i - j)] for j in range(BASIS)] for i in range(BASIS)]
    diag = [mat[i][i] for i in range(BASIS)]
    rhs = [(4.0 / RADIUS) * nu[i] for i in range(BASIS)]
    inverse = []
    for k in range(BASIS):
        good = mat[k][k] > 1e-8 * diag[k]
        inv = jnp.where(good, 1.0 / jnp.where(good, mat[k][k], 1.0), 0.0)
        inverse.append(inv)
        for i in range(k + 1, BASIS):
            factor = mat[k][i] * inv
            for j in range(i, BASIS):
                mat[i][j] = mat[i][j] - factor * mat[k][j]
            rhs[i] = rhs[i] - factor * rhs[k]
    out = [None] * BASIS
    for i in reversed(range(BASIS)):
        value = rhs[i]
        for j in range(i + 1, BASIS):
            value = value - mat[i][j] * out[j]
        out[i] = value * inverse[i]
    return out


def relays(n_sec, ingots):
    if (n_sec, ingots) != (16, 4):
        return []
    return [(1, 5), (2, 5), (3, 5), (2, 6), (3, 6)]


def kernel(
    n_sec,
    n_slab,
    part_hbm,
    line_hbm,
    flag_hbm,
    instant_ref,
    heat_ref,
    factor_ref,
    dual_ref,
    both_ref,
    part_ref,
    line_ref,
    flag_ref,
    heat,
    coef,
    dual,
    a1,
    a2,
    a3,
    keep,
    mu3,
    mu2,
    mu1,
    w4,
    w3,
    w2,
    w1,
    pick,
    pick_t,
    offered,
    slots,
    back,
    basis_rows,
    relay,
    got,
    weights,
    weights_in,
    returned,
    sums_ref,
    packed_ref,
    gather,
    local_sem,
    halo_send,
    halo_recv,
    row_send,
    row_recv,
    side_send,
    side_recv,
    sum_send,
    sum_recv,
    ready,
    known,
    relay_send,
    relay_recv,
    ahead_send,
    ahead_recv,
    weight_recv,
):
    ingots, contact = part_hbm.shape
    melts = n_sec - ingots
    early = 2 * melts // 3
    depth, height, width = heat_ref.shape
    first, last = depth, 2 * depth
    sec, slab = lax.axis_index("sec"), lax.axis_index("slab")
    is_melt = sec < melts
    is_early = sec < early
    relayed = relays(n_sec, ingots)
    targets = sorted({m for _, m in relayed})
    ahead = [m for m in range(AHEAD) if m < early]
    has_left, has_right = slab > 0, slab < n_slab - 1
    state_ref, adjoint_ref = both_ref.at[0], both_ref.at[1]

    loads = [
        pltpu.make_async_copy(src, dst.at[pl.ds(first, depth)], local_sem.at[i])
        for i, (src, dst) in enumerate(((heat_ref, heat), (factor_ref, coef), (dual_ref, dual)))
    ]
    tables = [
        pltpu.make_async_copy(src, dst, local_sem.at[3 + i])
        for i, (src, dst) in enumerate(((part_hbm, part_ref), (line_hbm, line_ref), (flag_hbm, flag_ref)))
    ]
    barrier = pltpu.get_barrier_semaphore()

    def greet(to_sec, to_slab, sem=barrier):
        pl.semaphore_signal(sem, inc=1, device_id=(to_sec, to_slab), device_id_type=MESH)

    def along(offset):
        return lax.rem(slab + offset % n_slab, n_slab)

    sizes = (4, 4, 2) if n_slab == 32 else (n_slab,)
    partners = []
    for flat in range(1, n_slab):
        shift, rest = [], flat
        for size in reversed(sizes):
            shift.insert(0, rest % size)
            rest //= size
        partners.append((sum(min(step, size - step) for step, size in zip(shift, sizes)), tuple(shift)))
    partners.sort(key=lambda entry: (-entry[0], entry[1]))

    def partner(shift):
        index, stride, rest = 0, 1, slab
        for step, size in zip(reversed(shift), reversed(sizes)):
            index = index + lax.rem(lax.rem(rest, size) + step, size) * stride
            rest, stride = rest // size, stride * size
        return index

    near = sorted({offset % n_slab for offset in range(-CLOSE, CLOSE + 1)} - {0})

    @pl.when(is_melt)
    def _():
        pl.when(has_left)(lambda: greet(sec, slab - 1))
        pl.when(has_right)(lambda: greet(sec, slab + 1))

        @pl.when(is_early)
        def _():
            for j in range(ingots):
                greet(melts + j, slab)

        for m in targets:
            pl.when(sec == m)(lambda: greet(early, slab))

    @pl.when(jnp.logical_not(is_melt))
    def _():
        for offset in near:
            greet(sec, along(offset))
        for m in range(early, melts):
            greet(m, slab)

    beside = has_left.astype(jnp.int32) + has_right.astype(jnp.int32)
    heard = jnp.where(is_melt, beside + jnp.where(is_early, 0, ingots), len(near) + early)
    heard = heard + jnp.where(sec == early, len(targets), 0) if targets else heard
    for load in tables + loads:
        load.start()
    pl.semaphore_wait(barrier, heard)

    def halo(index, src, dst, to_left, to_right):
        (left_src, left_dst), (right_src, right_dst) = to_left, to_right
        send, recv = halo_send.at[index], halo_recv.at[index]
        return (
            pltpu.make_async_remote_copy(
                src_ref=src.at[left_src], dst_ref=dst.at[left_dst], send_sem=send.at[0], recv_sem=recv.at[1],
                device_id=(sec, slab - 1), device_id_type=MESH,
            ),
            pltpu.make_async_remote_copy(
                src_ref=src.at[right_src], dst_ref=dst.at[right_dst], send_sem=send.at[1], recv_sem=recv.at[0],
                device_id=(sec, slab + 1), device_id_type=MESH,
            ),
        )

    def start(pair):
        pl.when(has_left)(lambda: pair[0].start())
        pl.when(has_right)(lambda: pair[1].start())

    def wait_recv(pair):
        pl.when(has_right)(lambda: pair[0].wait_recv())
        pl.when(has_left)(lambda: pair[1].wait_recv())

    def wait_send(pair):
        pl.when(has_left)(lambda: pair[0].wait_send())
        pl.when(has_right)(lambda: pair[1].wait_send())

    def lower(planes, offset=0):
        return pl.ds(offset, planes), pl.ds(last + offset, planes)

    def upper(planes, offset=0):
        at = depth - planes - offset
        return pl.ds(at, planes), pl.ds(at, planes)

    def pass_on(buf, rows, index):
        here = buf.at[pl.ds(first, depth), rows]
        pair = []
        for side, there, to in ((0, last, slab - 1), (1, 0, slab + 1)):
            pair.append(
                pltpu.make_async_remote_copy(
                    src_ref=here, dst_ref=buf.at[pl.ds(there, depth), rows], send_sem=side_send.at[side, index],
                    recv_sem=side_recv.at[1 - side], device_id=(sec, to), device_id_type=MESH,
                )
            )
        start(pair)
        return pair

    def take(buf, side):
        region = buf.at[pl.ds(2 * depth * side, depth)]
        pltpu.make_async_copy(region, region, side_recv.at[side]).wait()

    zero = jnp.zeros((height, width), jnp.float32)

    def clear(*bufs):
        @pl.when(jnp.logical_not(has_left))
        def _():
            for buf in bufs:
                buf[first - 1] = zero

        @pl.when(jnp.logical_not(has_right))
        def _():
            for buf in bufs:
                buf[last] = zero

    row_i = lax.broadcasted_iota(jnp.int32, (contact, contact), 0)
    lane_i = lax.broadcasted_iota(jnp.int32, (contact, contact), 1)

    def column(row):
        return jnp.sum(jnp.where(row_i == lane_i, row, 0.0), axis=1, keepdims=True)

    def slot_rows(index):
        return pl.ds(index * PAIRCAP, PAIRCAP)

    @pl.when(is_melt)
    def _():
        heat_halo = halo(0, heat_ref, heat, lower(depth), upper(depth))
        coef_halo = halo(1, factor_ref, coef, lower(depth - 1), upper(depth - 1))
        edge_halo = halo(2, factor_ref, coef, lower(1, depth - 1), upper(1, depth - 1))
        dual_halo = halo(3, dual_ref, dual, lower(depth), upper(depth))
        start(heat_halo)
        start(coef_halo)

        @pl.when(jnp.logical_not(is_early))
        def _():
            for j in range(ingots):
                greet(melts + j, slab, ready)

        clear(heat, dual, w4)
        for load in tables:
            load.wait()

        for j in range(ingots):
            named = part_ref[j : j + 1, :].astype(jnp.float32) == sec.astype(jnp.float32)
            lines = line_ref[j : j + 1, :].astype(jnp.float32)
            before = column(jnp.where(named, 1.0, 0.0))
            rank = jnp.sum(jnp.where(row_i < lane_i, before, 0.0), axis=0, keepdims=True)
            slot = lax.broadcasted_iota(jnp.int32, (PAIRCAP, contact), 0).astype(jnp.float32)
            chosen = jnp.where(named, 1.0, 0.0) * jnp.where(rank == slot, 1.0, 0.0)
            slot_line = jnp.sum(chosen * lines, axis=1, keepdims=True)
            live = jnp.sum(chosen, axis=1, keepdims=True)
            q = lax.broadcasted_iota(jnp.int32, (PAIRCAP, height), 1).astype(jnp.float32)
            pick[slot_rows(j), :] = jnp.where(q == slot_line, live, 0.0)
        eye = jnp.where(
            lax.broadcasted_iota(jnp.int32, (height, height), 0) == lax.broadcasted_iota(jnp.int32, (height, height), 1),
            1.0, 0.0,
        )
        pick_t[...] = lax.dot_general(
            eye, pick[...], (((1,), (1,)), ((), ())), precision=HIGHEST, preferred_element_type=jnp.float32
        )

        archived = instant_ref[0].astype(jnp.float32)
        speeds = []
        for k in range(STEPS):
            phase = jnp.full((1, width), archived + k)
            speeds.append(1.0 + 0.5 * jnp.sin(2.0 * math.pi * phase / period_steps))

        for load in loads:
            load.wait()
        wait_recv(heat_halo)
        wait_recv(coef_halo)
        start(edge_halo)
        start(dual_halo)

        states = (heat, a1, a2, a3, state_ref)
        for k in range(STEPS):
            src, dst = states[k], states[k + 1]
            final = k == STEPS - 1
            shift = first if final else 0

            def forward(z, carry, k=k, src=src, dst=dst, shift=shift):
                c = src[z]
                below = src[z - 1]
                total = (below + src[z + 1]) + in_plane(c)
                change = coef[z] * (total - 6.0 * c) - speeds[k] * (c - below)
                bent = jnp.tanh(c)
                dst[z - shift] = c + time_step * change - time_step * sink_rate * bent
                keep[k, z] = 1.0 - time_step * sink_rate * (1.0 - bent * bent)
                return carry

            lax.fori_loop(1 + k, 3 * depth - 1 - k, forward, 0, unroll=2)
            if not final:
                clear(dst)

        for z in range(depth):
            offered[z] = jnp.dot(pick[...], state_ref[z], precision=HIGHEST, preferred_element_type=jnp.float32)
        pl.when(is_early)(lambda: pl.semaphore_wait(ready, ingots))
        sends = []
        for j in range(ingots):
            send = pltpu.make_async_remote_copy(
                src_ref=offered.at[:, slot_rows(j), :],
                dst_ref=slots.at[pl.ds(first, depth), pl.ds(pl.multiple_of(sec * PAIRCAP, PAIRCAP), PAIRCAP), :],
                send_sem=row_send.at[j], recv_sem=row_recv.at[sec], device_id=(melts + j, slab), device_id_type=MESH,
            )
            send.start()
            sends.append(send)
        keep3 = keep.at[3]
        keep_halo = halo(
            4, keep3, keep3, (pl.ds(first, depth - 1), pl.ds(last, depth - 1)), (pl.ds(first + 1, depth - 1), pl.ds(1, depth - 1))
        )
        start(keep_halo)

        for z in (first - 2, last + 1):
            bent = jnp.tanh(a2[z])
            keep[2, z] = 1.0 - time_step * sink_rate * (1.0 - bent * bent)
        wait_recv(edge_halo)
        wait_recv(dual_halo)
        wait_recv(keep_halo)

        def relay_on(index):
            j, m = relayed[index]
            return pltpu.make_async_remote_copy(
                src_ref=relay.at[index], dst_ref=returned.at[pl.ds(first, depth), slot_rows(j), :],
                send_sem=relay_send.at[index], recv_sem=row_recv.at[j], device_id=(m, slab), device_id_type=MESH,
            )

        if relayed:

            @pl.when(sec == early)
            def _():
                for index in range(len(relayed)):
                    pltpu.make_async_copy(relay.at[index], relay.at[index], relay_recv.at[index]).wait()
                    relay_on(index).start()

        passed = []
        for j in reversed(range(ingots)):
            rows = slot_rows(j)

            def arrive(j=j, rows=rows):
                region = returned.at[pl.ds(first, depth), rows]
                pltpu.make_async_copy(region, region, row_recv.at[j]).wait()

            def add_up(j=j, rows=rows):
                region = got.at[:, :, rows]
                pltpu.make_async_copy(region, region, ahead_recv.at[j]).wait()
                pltpu.make_async_copy(weights_in.at[j], weights_in.at[j], weight_recv.at[j]).wait()
                c = [weights_in[j, i : i + 1, :] for i in range(BASIS)]
                for z in range(depth):
                    returned[first + z, rows, :] = (c[0] * got[0, z, rows, :] + c[1] * got[1, z, rows, :]) + (
                        c[2] * got[2, z, rows, :] + c[3] * got[3, z, rows, :]
                    )

            if ahead:
                pl.when(sec < len(ahead))(add_up)
                pl.when(sec >= len(ahead))(arrive)
            else:
                arrive()
            passed.append(pass_on(returned, rows, j))

        def add_returned(at):
            for z in range(at, at + depth):
                rows = jnp.dot(pick_t[...], returned[z], precision=HIGHEST, preferred_element_type=jnp.float32)
                value = dual[z] + rows
                dual[z] = value
                w4[z] = coef[z] * value

        add_returned(first)

        mus, ws = (adjoint_ref, mu1, mu2, mu3, dual), (None, w1, w2, w3, w4)

        def backward(k, lo, hi):
            src, dst, wsrc, wdst = mus[k + 1], mus[k], ws[k + 1], ws[k]
            shift = first if k == 0 else 0

            def plane(z, carry):
                c, w = src[z], wsrc[z]
                total = (wsrc[z - 1] + wsrc[z + 1]) + in_plane(w)
                change = total - 6.0 * w - speeds[k] * (c - src[z + 1])
                value = keep[k, z] * c + time_step * change
                dst[z - shift] = value
                if wdst is not None:
                    wdst[z] = coef[z] * value
                return carry

            lax.fori_loop(lo, hi, plane, 0, unroll=2)
            if wdst is not None:
                clear(dst, wdst)

        @pl.when(slab % 2 == 0)
        def _():
            take(returned, 1)
            add_returned(last)
            for k in (3, 2, 1):
                backward(k, first + STEPS - k, last + k)

            @pl.when(has_left)
            def _():
                take(returned, 0)
                add_returned(0)

            for k in (3, 2, 1, 0):
                backward(k, first - k, first + STEPS - k)

        @pl.when(slab % 2 == 1)
        def _():
            take(returned, 0)
            add_returned(0)
            for k in (3, 2, 1):
                backward(k, first - k, last - STEPS + k)

            @pl.when(has_right)
            def _():
                take(returned, 1)
                add_returned(last)

            for k in (3, 2, 1, 0):
                backward(k, last - STEPS + k, last + k)

        if relayed:

            @pl.when(sec == early)
            def _():
                for index in range(len(relayed)):
                    relay_on(index).wait_send()

        for pair in [heat_halo, coef_halo, edge_halo, dual_halo, keep_halo] + passed:
            wait_send(pair)
        for send in sends:
            send.wait_send()

    @pl.when(jnp.logical_not(is_melt))
    def _():
        dual_near = halo(3, dual_ref, dual, lower(2), upper(2))
        coef_near = halo(1, factor_ref, coef, lower(1), upper(1))
        dual_far = halo(4, dual_ref, dual, lower(depth - 2, 2), upper(depth - 3, 2))
        coef_far = halo(2, factor_ref, coef, lower(depth - 2, 1), upper(depth - 3, 1))
        heat_halo = halo(0, heat_ref, heat, lower(depth), upper(depth - 1))
        start(dual_near)
        start(coef_near)
        start(coef_far)
        start(dual_far)
        for m in range(early):
            greet(m, slab, ready)
        rounds = []
        reach = CLOSE
        while reach < n_slab // 2:
            rounds.append(reach)
            reach *= 2

        def tell(index):
            for offset in (-rounds[index], rounds[index]):
                greet(sec, along(offset), known.at[index])

        if rounds:
            tell(0)
        clear(heat, dual)

        for load in tables:
            load.wait()
        mine = sec - melts
        names = part_ref[pl.ds(mine, 1), :].astype(jnp.float32)
        flags = flag_ref[pl.ds(mine, 1), :].astype(jnp.float32)
        names_col, flags_col = column(names), column(flags)
        same = jnp.where(names_col == names, 1.0, 0.0)
        rank_col = jnp.sum(jnp.where(lane_i < row_i, same, 0.0), axis=1, keepdims=True)
        rank_row = jnp.sum(jnp.where(row_i < lane_i, same, 0.0), axis=0, keepdims=True)
        count = melts * PAIRCAP
        slot_lane = lax.broadcasted_iota(jnp.int32, (contact, count), 1).astype(jnp.float32)
        slot_row = lax.broadcasted_iota(jnp.int32, (count, contact), 0).astype(jnp.float32)
        place = jnp.where(slot_lane == names_col * PAIRCAP + rank_col, flags_col, 0.0)
        give = jnp.where(slot_row == names * PAIRCAP + rank_row, flags, 0.0)

        for load in loads:
            load.wait()
        told = [0]

        def hear(count):
            while told[0] < min(count, len(rounds)):
                pl.semaphore_wait(known.at[told[0]], 2)
                told[0] += 1
                if told[0] < len(rounds):
                    tell(told[0])

        early_sends = []

        def pick_basis(i):
            t = (dual, a1, a2, a3)[i]
            for z in range(depth):
                basis_rows[i, z] = jnp.dot(
                    give, t[first + z, :contact, :], precision=HIGHEST, preferred_element_type=jnp.float32
                )
            for m in ahead:
                send = pltpu.make_async_remote_copy(
                    src_ref=basis_rows.at[i, :, slot_rows(m), :],
                    dst_ref=got.at[i, :, pl.ds(pl.multiple_of(mine * PAIRCAP, PAIRCAP), PAIRCAP), :],
                    send_sem=ahead_send.at[m, i], recv_sem=ahead_recv.at[mine], device_id=(m, slab), device_id_type=MESH,
                )
                send.start()
                early_sends.append(send)

        def solve(which, t0, out, arrive_near, arrive_far, meanwhile, then):
            ts = (t0, a1, a2, a3)

            def grow(k, z):
                t = ts[k - 1]
                c = t[z]
                value = (coef[z] - (CENTRE - 6.0)) * c - ((t[z - 1] + t[z + 1]) + in_plane(c))
                if k == 1:
                    ts[k][z] = value * (1.0 / RADIUS)
                else:
                    ts[k][z] = value * (2.0 / RADIUS) - ts[k - 2][z]

            def grow_all(k, lo, hi):
                lax.fori_loop(lo, hi, lambda z, carry: grow(k, z) or carry, 0, unroll=2)

            def add_up(terms, count):
                def plane(z, sums):
                    return tuple(s + fold(term) for s, term in zip(sums, terms(z)))

                sums = lax.fori_loop(first, last, plane, (jnp.zeros((8, width), jnp.float32),) * count, unroll=2)
                return [jnp.sum(total, axis=0, keepdims=True) for total in sums]

            def near_terms(z):
                x0, x1, x2 = (ref[z] for ref in ts[:3])
                return x0 * x0, x0 * x1, x1 * x1, x1 * x2, x2 * x2

            def far_terms(z):
                x2, x3 = a2[z], a3[z]
                image = (coef[z] - (CENTRE - 6.0)) * x3 - 2.0 * a3[z + 1] - in_plane(x3)
                return x2 * x3, x3 * x3, x3 * image * (1.0 / RADIUS)

            arrive_near()
            grow_all(1, first - 1, last + 1)
            clear(a1)
            grow_all(2, first, last)
            sums = add_up(near_terms, 5)
            arrive_far()
            for z in (first - 2, last + 1, last + 2):
                grow(1, z)
            for z in (first - 1, last, last + 1):
                grow(2, z)
            clear(a2)
            grow_all(3, first, last)
            grow(3, last)
            clear(a3)
            sums += add_up(far_terms, 3)
            for k in range(8):
                sums_ref[pl.ds(k, 1), :] = sums[k]
            hear(len(rounds))
            packed = pack(sums_ref[...])
            packed_ref[which] = packed
            for index, (_, shift) in enumerate(partners):
                pltpu.make_async_remote_copy(
                    src_ref=packed_ref.at[which], dst_ref=gather.at[which, pl.ds(index, 1)],
                    send_sem=sum_send.at[which], recv_sem=sum_recv.at[which],
                    device_id=(sec, partner(shift)), device_id_type=MESH,
                ).start()
            meanwhile()
            others = gather.at[which, pl.ds(0, n_slab - 1)]
            pltpu.make_async_copy(others, others, sum_recv.at[which]).wait()
            c = coefficients(packed + jnp.sum(gather[which, : n_slab - 1, :], axis=0, keepdims=True))
            then(c)

            def combine(z, carry):
                out[z - first] = (c[0] * ts[0][z] + c[1] * ts[1][z]) + (c[2] * ts[2][z] + c[3] * ts[3][z])
                return carry

            lax.fori_loop(first, last, combine, 0, unroll=2)

        def arrive_near():
            pick_basis(0)
            hear(1)
            wait_recv(dual_near)
            wait_recv(coef_near)

        def arrive_far():
            pick_basis(1)
            pick_basis(2)
            hear(2)
            wait_recv(coef_far)
            wait_recv(dual_far)
            start(heat_halo)

        sends = []

        def send_back(c):
            weights[...] = jnp.concatenate(c + c, axis=0)
            for m in ahead:
                send = pltpu.make_async_remote_copy(
                    src_ref=weights, dst_ref=weights_in.at[mine], send_sem=row_send.at[m], recv_sem=weight_recv.at[mine],
                    device_id=(m, slab), device_id_type=MESH,
                )
                send.start()
                early_sends.append(send)
            for z in range(depth):
                back[z] = (c[0] * basis_rows[0, z] + c[1] * basis_rows[1, z]) + (
                    c[2] * basis_rows[2, z] + c[3] * basis_rows[3, z]
                )
            pl.semaphore_wait(ready, melts - early)
            for index, (j, m) in enumerate(relayed):

                @pl.when(mine == j)
                def _():
                    pltpu.make_async_remote_copy(
                        src_ref=back.at[:, slot_rows(m), :], dst_ref=relay.at[index], send_sem=row_send.at[m],
                        recv_sem=relay_recv.at[index], device_id=(early, slab), device_id_type=MESH,
                    ).start()

            for m in [m for m in range(melts) if m not in ahead]:
                direct = [j for j in range(ingots) if (j, m) not in relayed]
                send = pltpu.make_async_remote_copy(
                    src_ref=back.at[:, slot_rows(m), :],
                    dst_ref=returned.at[pl.ds(first, depth), pl.ds(pl.multiple_of(mine * PAIRCAP, PAIRCAP), PAIRCAP), :],
                    send_sem=row_send.at[m], recv_sem=row_recv.at[mine], device_id=(m, slab), device_id_type=MESH,
                )
                if len(direct) == ingots:
                    send.start()
                elif direct:
                    pl.when(functools.reduce(jnp.logical_or, [mine == j for j in direct]))(lambda send=send: send.start())
                sends.append(send)

        solve(0, dual, adjoint_ref, arrive_near, arrive_far, lambda: pick_basis(3), send_back)

        passed = []
        for m in range(melts):
            region = slots.at[pl.ds(first, depth), slot_rows(m)]
            pltpu.make_async_copy(region, region, row_recv.at[m]).wait()
            passed.append(pass_on(slots, slot_rows(m), m))

        def load_up(at):
            for z in range(at, at + depth):
                rows = jnp.dot(place, slots[z], precision=HIGHEST, preferred_element_type=jnp.float32)
                heat[z, pl.ds(0, contact), :] = heat[z, pl.ds(0, contact), :] + rows

        wait_recv(heat_halo)
        load_up(first)

        @pl.when(has_left)
        def _():
            take(slots, 0)
            load_up(0)

        @pl.when(has_right)
        def _():
            take(slots, 1)
            load_up(last)

        solve(1, heat, state_ref, lambda: None, lambda: None, lambda: None, lambda c: None)

        for pair in [dual_near, coef_near, dual_far, coef_far, heat_halo] + passed:
            wait_send(pair)
        for send in sends + early_sends:
            send.wait_send()
        for which in range(2):
            others = gather.at[which, pl.ds(0, n_slab - 1)]
            pltpu.make_async_copy(others, others, sum_send.at[which]).wait()


def body(n_sec, n_slab, heat_level, material_factor, dual_sensitivity, part, line, flag, instant):
    ingots, contact = line.shape
    melts = n_sec - ingots
    _, depth, height, width = heat_level.shape
    f32 = jnp.float32
    wide = pltpu.VMEM((3 * depth, height, width), f32)
    table = pltpu.VMEM((ingots, contact), jnp.int32)
    dma = pltpu.SemaphoreType.DMA
    most = max(melts, ingots)
    scratch = [
        table, table, table,
        wide, wide, wide, wide, wide, wide,
        pltpu.VMEM((STEPS, 3 * depth, height, width), f32),
        wide, wide, wide, wide, wide, wide, wide,
        pltpu.VMEM((ingots * PAIRCAP, height), f32),
        pltpu.VMEM((height, ingots * PAIRCAP), f32),
        pltpu.VMEM((depth, ingots * PAIRCAP, width), f32),
        pltpu.VMEM((3 * depth, melts * PAIRCAP, width), f32),
        pltpu.VMEM((depth, melts * PAIRCAP, width), f32),
        pltpu.VMEM((BASIS, depth, melts * PAIRCAP, width), f32),
        pltpu.VMEM((max(len(relays(n_sec, ingots)), 1), depth, PAIRCAP, width), f32),
        pltpu.VMEM((BASIS, depth, ingots * PAIRCAP, width), f32),
        pltpu.VMEM((8, width), f32),
        pltpu.VMEM((ingots, 8, width), f32),
        pltpu.VMEM((3 * depth, ingots * PAIRCAP, width), f32),
        pltpu.VMEM((8, width), f32),
        pltpu.VMEM((2, 1, width), f32),
        pltpu.VMEM((2, n_slab, width), f32),
        dma((6,)), dma((5, 2)), dma((5, 2)),
        dma((most,)), dma((most,)), dma((2, most)), dma((2,)),
        dma((2,)), dma((2,)), pltpu.SemaphoreType.REGULAR, pltpu.SemaphoreType.REGULAR((4,)),
        dma((8,)), dma((8,)), dma((max(AHEAD, 1), BASIS)), dma((ingots,)), dma((ingots,)),
    ]
    hbm, vmem, smem = (pl.BlockSpec(memory_space=s) for s in (pltpu.HBM, pltpu.VMEM, pltpu.SMEM))
    fields = (part[:, :, 0], line, flag, heat_level[0], material_factor[0], dual_sensitivity[0])
    fields = [pltpu.with_memory_space_constraint(field, pltpu.HBM) for field in fields]
    both = pl.pallas_call(
        functools.partial(kernel, n_sec, n_slab),
        out_shape=jax.ShapeDtypeStruct((2, depth, height, width), f32),
        in_specs=[hbm, hbm, hbm, smem, hbm, hbm, hbm],
        out_specs=vmem,
        scratch_shapes=scratch,
        compiler_params=pltpu.CompilerParams(
            collective_id=0, has_side_effects=True, vmem_limit_bytes=32 * 1024 * 1024
        ),
    )(*fields[:3], instant, *fields[3:])
    return both[0:1], both[1:2]


def solution(mesh):
    n_sec, n_slab = mesh.shape["sec"], mesh.shape["slab"]
    fields = P("sec", "slab", None, None)
    return jax.shard_map(
        functools.partial(body, n_sec, n_slab),
        mesh=mesh,
        in_specs=(fields, fields, fields, P(), P(), P(), P()),
        out_specs=(fields, fields),
        check_vma=False,
    )
```

```python
import functools
import math

import jax
import jax.numpy as jnp
from jax import lax
from jax.experimental import pallas as pl
from jax.experimental.pallas import tpu as pltpu
from jax.sharding import PartitionSpec as P

STEPS = 4
PAIRCAP = 8
BASIS = 4
CLOSE = 4

time_step = 0.1
sink_rate = 0.5
period_steps = 16.0

CENTRE = 6.8
RADIUS = 6.4

MESH = pl.DeviceIdType.MESH
HIGHEST = lax.Precision.HIGHEST


def in_plane(c):
    rows, cols = c.shape
    row = lax.broadcasted_iota(jnp.int32, c.shape, 0)
    col = lax.broadcasted_iota(jnp.int32, c.shape, 1)
    up = jnp.where(row == 0, 0.0, pltpu.roll(c, 1, 0))
    down = jnp.where(row == rows - 1, 0.0, pltpu.roll(c, rows - 1, 0))
    left = jnp.where(col == 0, 0.0, pltpu.roll(c, 1, 1))
    right = jnp.where(col == cols - 1, 0.0, pltpu.roll(c, cols - 1, 1))
    return (up + down) + (left + right)


def fold(values):
    rows, cols = values.shape
    return jnp.sum(values.reshape(rows // 8, 8, cols), axis=0)


def own_lanes(values):
    row = lax.broadcasted_iota(jnp.int32, values.shape, 0)
    lane = lax.broadcasted_iota(jnp.int32, values.shape, 1)
    each = values.shape[1] // values.shape[0]
    return jnp.where((lane >= row * each) & (lane < (row + 1) * each), values, 0.0)


def pack(values):
    lanes = values.shape[1]
    for distance in (lanes // 2, lanes // 4, lanes // 8):
        values = values + pltpu.roll(values, distance, 1)
    return jnp.sum(own_lanes(values), axis=0, keepdims=True)


def coefficients(packed):
    spread = own_lanes(jnp.broadcast_to(packed, (8, packed.shape[1])))
    total = jnp.broadcast_to(jnp.sum(spread, axis=1, keepdims=True), spread.shape)
    s = [total[k : k + 1, :] for k in range(8)]
    nu = [s[0], s[1], 2.0 * s[2] - s[0], 2.0 * s[3] - s[1], 2.0 * s[4] - s[0], 2.0 * s[5] - s[1], 2.0 * s[6] - s[0]]
    nu.append(4.0 * s[7] - 2.0 * s[5] - s[1])
    shift = 2.0 * CENTRE / RADIUS
    u = [shift * nu[k] + nu[k + 1] + nu[abs(k - 1)] for k in range(7)]
    mat = [[u[i + j] + u[abs(i - j)] for j in range(BASIS)] for i in range(BASIS)]
    diag = [mat[i][i] for i in range(BASIS)]
    rhs = [(4.0 / RADIUS) * nu[i] for i in range(BASIS)]
    inverse = []
    for k in range(BASIS):
        good = mat[k][k] > 1e-8 * diag[k]
        inv = jnp.where(good, 1.0 / jnp.where(good, mat[k][k], 1.0), 0.0)
        inverse.append(inv)
        for i in range(k + 1, BASIS):
            factor = mat[k][i] * inv
            for j in range(i, BASIS):
                mat[i][j] = mat[i][j] - factor * mat[k][j]
            rhs[i] = rhs[i] - factor * rhs[k]
    out = [None] * BASIS
    for i in reversed(range(BASIS)):
        value = rhs[i]
        for j in range(i + 1, BASIS):
            value = value - mat[i][j] * out[j]
        out[i] = value * inverse[i]
    return out


def relays(n_sec, ingots):
    if (n_sec, ingots) != (16, 4):
        return []
    return [(2, 6), (3, 6)]


def ahead_of(ingots, early):
    if early < 2:
        return {}
    return {0: list(range(ingots)), 1: list(range(ingots // 2, ingots))}


def kernel(
    n_sec,
    n_slab,
    part_hbm,
    line_hbm,
    flag_hbm,
    instant_ref,
    heat_ref,
    factor_ref,
    dual_ref,
    both_ref,
    part_ref,
    line_ref,
    flag_ref,
    heat,
    coef,
    dual,
    a1,
    a2,
    a3,
    keep,
    mu3,
    mu2,
    mu1,
    w4,
    w3,
    w2,
    w1,
    pick,
    pick_t,
    offered,
    slots,
    back,
    basis_rows,
    relay,
    got,
    weights,
    weights_in,
    returned,
    sums_ref,
    packed_ref,
    gather,
    local_sem,
    halo_send,
    halo_recv,
    row_send,
    row_recv,
    side_send,
    side_recv,
    sum_send,
    sum_recv,
    ready,
    known,
    relay_send,
    relay_recv,
    ahead_send,
    ahead_recv,
    weight_recv,
):
    ingots, contact = part_hbm.shape
    melts = n_sec - ingots
    early = 2 * melts // 3
    depth, height, width = heat_ref.shape
    first, last = depth, 2 * depth
    sec, slab = lax.axis_index("sec"), lax.axis_index("slab")
    is_melt = sec < melts
    is_early = sec < early
    relayed = relays(n_sec, ingots)
    targets = sorted({m for _, m in relayed})
    ahead = ahead_of(ingots, early)

    def any_of(value, choices):
        return functools.reduce(jnp.logical_or, [value == choice for choice in choices])

    def only(value, choices, count, action):
        if len(choices) == count:
            action()
        elif choices:
            pl.when(any_of(value, choices))(action)

    has_left, has_right = slab > 0, slab < n_slab - 1
    state_ref, adjoint_ref = both_ref.at[0], both_ref.at[1]

    loads = [
        pltpu.make_async_copy(src, dst.at[pl.ds(first, depth)], local_sem.at[i])
        for i, (src, dst) in enumerate(((heat_ref, heat), (factor_ref, coef), (dual_ref, dual)))
    ]
    tables = [
        pltpu.make_async_copy(src, dst, local_sem.at[3 + i])
        for i, (src, dst) in enumerate(((part_hbm, part_ref), (line_hbm, line_ref), (flag_hbm, flag_ref)))
    ]
    barrier = pltpu.get_barrier_semaphore()

    def greet(to_sec, to_slab, sem=barrier):
        pl.semaphore_signal(sem, inc=1, device_id=(to_sec, to_slab), device_id_type=MESH)

    def along(offset):
        return lax.rem(slab + offset % n_slab, n_slab)

    sizes = (4, 4, 2) if n_slab == 32 else (n_slab,)
    partners = []
    for flat in range(1, n_slab):
        shift, rest = [], flat
        for size in reversed(sizes):
            shift.insert(0, rest % size)
            rest //= size
        partners.append((sum(min(step, size - step) for step, size in zip(shift, sizes)), tuple(shift)))
    partners.sort(key=lambda entry: (-entry[0], entry[1]))

    digits, rest = [], slab
    for size in reversed(sizes):
        digits.insert(0, lax.rem(rest, size))
        rest = lax.div(rest, size)
    strides = [math.prod(sizes[place + 1 :]) for place in range(len(sizes))]
    moved = [
        [lax.rem(digit + step, size) * stride for step in range(size)]
        for digit, size, stride in zip(digits, sizes, strides)
    ]

    def partner(shift):
        return sum(moved[place][step] for place, step in enumerate(shift))

    near = sorted({offset % n_slab for offset in range(-CLOSE, CLOSE + 1)} - {0})

    @pl.when(is_melt)
    def _():
        pl.when(has_left)(lambda: greet(sec, slab - 1))
        pl.when(has_right)(lambda: greet(sec, slab + 1))

        @pl.when(is_early)
        def _():
            for j in range(ingots):
                greet(melts + j, slab)

        for m in targets:
            pl.when(sec == m)(lambda: greet(early, slab))

    @pl.when(jnp.logical_not(is_melt))
    def _():
        for offset in near:
            greet(sec, along(offset))
        for m in range(early, melts):
            greet(m, slab)

    beside = has_left.astype(jnp.int32) + has_right.astype(jnp.int32)
    heard = jnp.where(is_melt, beside + jnp.where(is_early, 0, ingots), len(near) + early)
    heard = heard + jnp.where(sec == early, len(targets), 0) if targets else heard
    for load in tables + loads:
        load.start()
    pl.semaphore_wait(barrier, heard)

    def halo(index, src, dst, to_left, to_right):
        (left_src, left_dst), (right_src, right_dst) = to_left, to_right
        send, recv = halo_send.at[index], halo_recv.at[index]
        return (
            pltpu.make_async_remote_copy(
                src_ref=src.at[left_src], dst_ref=dst.at[left_dst], send_sem=send.at[0], recv_sem=recv.at[1],
                device_id=(sec, slab - 1), device_id_type=MESH,
            ),
            pltpu.make_async_remote_copy(
                src_ref=src.at[right_src], dst_ref=dst.at[right_dst], send_sem=send.at[1], recv_sem=recv.at[0],
                device_id=(sec, slab + 1), device_id_type=MESH,
            ),
        )

    def start(pair):
        pl.when(has_left)(lambda: pair[0].start())
        pl.when(has_right)(lambda: pair[1].start())

    def wait_recv(pair):
        pl.when(has_right)(lambda: pair[0].wait_recv())
        pl.when(has_left)(lambda: pair[1].wait_recv())

    def wait_send(pair):
        pl.when(has_left)(lambda: pair[0].wait_send())
        pl.when(has_right)(lambda: pair[1].wait_send())

    def lower(planes, offset=0):
        return pl.ds(offset, planes), pl.ds(last + offset, planes)

    def upper(planes, offset=0):
        at = depth - planes - offset
        return pl.ds(at, planes), pl.ds(at, planes)

    def pass_on(buf, rows, index):
        here = buf.at[pl.ds(first, depth), rows]
        pair = []
        for side, there, to in ((0, last, slab - 1), (1, 0, slab + 1)):
            pair.append(
                pltpu.make_async_remote_copy(
                    src_ref=here, dst_ref=buf.at[pl.ds(there, depth), rows], send_sem=side_send.at[side, index],
                    recv_sem=side_recv.at[1 - side], device_id=(sec, to), device_id_type=MESH,
                )
            )
        start(pair)
        return pair

    def take(buf, side):
        region = buf.at[pl.ds(2 * depth * side, depth)]
        pltpu.make_async_copy(region, region, side_recv.at[side]).wait()

    zero = jnp.zeros((height, width), jnp.float32)

    def clear(*bufs):
        @pl.when(jnp.logical_not(has_left))
        def _():
            for buf in bufs:
                buf[first - 1] = zero

        @pl.when(jnp.logical_not(has_right))
        def _():
            for buf in bufs:
                buf[last] = zero

    row_i = lax.broadcasted_iota(jnp.int32, (contact, contact), 0)
    lane_i = lax.broadcasted_iota(jnp.int32, (contact, contact), 1)

    def column(row):
        return jnp.sum(jnp.where(row_i == lane_i, row, 0.0), axis=1, keepdims=True)

    def slot_rows(index):
        return pl.ds(index * PAIRCAP, PAIRCAP)

    @pl.when(is_melt)
    def _():
        heat_halo = halo(0, heat_ref, heat, lower(depth), upper(depth))
        coef_halo = halo(1, factor_ref, coef, lower(depth - 1), upper(depth - 1))
        edge_halo = halo(2, factor_ref, coef, lower(1, depth - 1), upper(1, depth - 1))
        dual_halo = halo(3, dual_ref, dual, lower(depth), upper(depth))
        start(heat_halo)
        start(coef_halo)

        @pl.when(jnp.logical_not(is_early))
        def _():
            for j in range(ingots):
                greet(melts + j, slab, ready)

        clear(heat, dual, w4)
        for load in tables:
            load.wait()

        for j in range(ingots):
            named = part_ref[j : j + 1, :].astype(jnp.float32) == sec.astype(jnp.float32)
            lines = line_ref[j : j + 1, :].astype(jnp.float32)
            before = column(jnp.where(named, 1.0, 0.0))
            rank = jnp.sum(jnp.where(row_i < lane_i, before, 0.0), axis=0, keepdims=True)
            slot = lax.broadcasted_iota(jnp.int32, (PAIRCAP, contact), 0).astype(jnp.float32)
            chosen = jnp.where(named, 1.0, 0.0) * jnp.where(rank == slot, 1.0, 0.0)
            slot_line = jnp.sum(chosen * lines, axis=1, keepdims=True)
            live = jnp.sum(chosen, axis=1, keepdims=True)
            q = lax.broadcasted_iota(jnp.int32, (PAIRCAP, height), 1).astype(jnp.float32)
            pick[slot_rows(j), :] = jnp.where(q == slot_line, live, 0.0)
        eye = jnp.where(
            lax.broadcasted_iota(jnp.int32, (height, height), 0) == lax.broadcasted_iota(jnp.int32, (height, height), 1),
            1.0, 0.0,
        )
        pick_t[...] = lax.dot_general(
            eye, pick[...], (((1,), (1,)), ((), ())), precision=HIGHEST, preferred_element_type=jnp.float32
        )

        archived = instant_ref[0].astype(jnp.float32)
        speeds = []
        for k in range(STEPS):
            phase = jnp.full((1, width), archived + k)
            speeds.append(1.0 + 0.5 * jnp.sin(2.0 * math.pi * phase / period_steps))

        for load in loads:
            load.wait()
        wait_recv(heat_halo)
        wait_recv(coef_halo)
        start(edge_halo)
        start(dual_halo)

        states = (heat, a1, a2, a3, state_ref)
        for k in range(STEPS):
            src, dst = states[k], states[k + 1]
            final = k == STEPS - 1
            shift = first if final else 0

            def forward(z, carry, k=k, src=src, dst=dst, shift=shift):
                c = src[z]
                below = src[z - 1]
                total = (below + src[z + 1]) + in_plane(c)
                change = coef[z] * (total - 6.0 * c) - speeds[k] * (c - below)
                bent = jnp.tanh(c)
                dst[z - shift] = c + time_step * change - time_step * sink_rate * bent
                keep[k, z] = 1.0 - time_step * sink_rate * (1.0 - bent * bent)
                return carry

            lax.fori_loop(1 + k, 3 * depth - 1 - k, forward, 0, unroll=2)
            if not final:
                clear(dst)

        for z in range(depth):
            offered[z] = jnp.dot(pick[...], state_ref[z], precision=HIGHEST, preferred_element_type=jnp.float32)
        pl.when(is_early)(lambda: pl.semaphore_wait(ready, ingots))
        sends = []
        for j in range(ingots):
            send = pltpu.make_async_remote_copy(
                src_ref=offered.at[:, slot_rows(j), :],
                dst_ref=slots.at[pl.ds(first, depth), pl.ds(pl.multiple_of(sec * PAIRCAP, PAIRCAP), PAIRCAP), :],
                send_sem=row_send.at[j], recv_sem=row_recv.at[sec], device_id=(melts + j, slab), device_id_type=MESH,
            )
            send.start()
            sends.append(send)
        keep3 = keep.at[3]
        keep_halo = halo(
            4, keep3, keep3, (pl.ds(first, depth - 1), pl.ds(last, depth - 1)), (pl.ds(first + 1, depth - 1), pl.ds(1, depth - 1))
        )
        start(keep_halo)

        for z in (first - 2, last + 1):
            bent = jnp.tanh(a2[z])
            keep[2, z] = 1.0 - time_step * sink_rate * (1.0 - bent * bent)
        wait_recv(edge_halo)
        wait_recv(dual_halo)
        wait_recv(keep_halo)

        def relay_on(index):
            j, m = relayed[index]
            return pltpu.make_async_remote_copy(
                src_ref=relay.at[index], dst_ref=returned.at[pl.ds(first, depth), slot_rows(j), :],
                send_sem=relay_send.at[index], recv_sem=row_recv.at[j], device_id=(m, slab), device_id_type=MESH,
            )

        if relayed:

            @pl.when(sec == early)
            def _():
                for index in range(len(relayed)):
                    pltpu.make_async_copy(relay.at[index], relay.at[index], relay_recv.at[index]).wait()
                    relay_on(index).start()

        passed = []
        for j in reversed(range(ingots)):
            rows = slot_rows(j)

            def arrive(j=j, rows=rows):
                region = returned.at[pl.ds(first, depth), rows]
                pltpu.make_async_copy(region, region, row_recv.at[j]).wait()

            def add_up(j=j, rows=rows):
                region = got.at[:, :, rows]
                pltpu.make_async_copy(region, region, ahead_recv.at[j]).wait()
                pltpu.make_async_copy(weights_in.at[j], weights_in.at[j], weight_recv.at[j]).wait()
                c = [weights_in[j, i : i + 1, :] for i in range(BASIS)]
                for z in range(depth):
                    returned[first + z, rows, :] = (c[0] * got[0, z, rows, :] + c[1] * got[1, z, rows, :]) + (
                        c[2] * got[2, z, rows, :] + c[3] * got[3, z, rows, :]
                    )

            summed = [m for m in ahead if j in ahead[m]]
            if summed:
                pl.when(any_of(sec, summed))(add_up)
                pl.when(jnp.logical_not(any_of(sec, summed)))(arrive)
            else:
                arrive()
            passed.append(pass_on(returned, rows, j))

        def add_returned(at):
            for z in range(at, at + depth):
                rows = jnp.dot(pick_t[...], returned[z], precision=HIGHEST, preferred_element_type=jnp.float32)
                value = dual[z] + rows
                dual[z] = value
                w4[z] = coef[z] * value

        add_returned(first)

        mus, ws = (adjoint_ref, mu1, mu2, mu3, dual), (None, w1, w2, w3, w4)

        def backward(k, lo, hi):
            src, dst, wsrc, wdst = mus[k + 1], mus[k], ws[k + 1], ws[k]
            shift = first if k == 0 else 0

            def plane(z, carry):
                c, w = src[z], wsrc[z]
                total = (wsrc[z - 1] + wsrc[z + 1]) + in_plane(w)
                change = total - 6.0 * w - speeds[k] * (c - src[z + 1])
                value = keep[k, z] * c + time_step * change
                dst[z - shift] = value
                if wdst is not None:
                    wdst[z] = coef[z] * value
                return carry

            lax.fori_loop(lo, hi, plane, 0, unroll=hi - lo if hi - lo == 4 else 2)
            if wdst is not None:
                clear(dst, wdst)

        @pl.when(slab % 2 == 0)
        def _():
            take(returned, 1)
            add_returned(last)
            for k in (3, 2, 1):
                backward(k, first + STEPS - k, last + k)

            @pl.when(has_left)
            def _():
                take(returned, 0)
                add_returned(0)

            for k in (3, 2, 1, 0):
                backward(k, first - k, first + STEPS - k)

        @pl.when(slab % 2 == 1)
        def _():
            take(returned, 0)
            add_returned(0)
            for k in (3, 2, 1):
                backward(k, first - k, last - STEPS + k)

            @pl.when(has_right)
            def _():
                take(returned, 1)
                add_returned(last)

            for k in (3, 2, 1, 0):
                backward(k, last - STEPS + k, last + k)

        if relayed:

            @pl.when(sec == early)
            def _():
                for index in range(len(relayed)):
                    relay_on(index).wait_send()

        for pair in [heat_halo, coef_halo, edge_halo, dual_halo, keep_halo] + passed:
            wait_send(pair)
        for send in sends:
            send.wait_send()

    @pl.when(jnp.logical_not(is_melt))
    def _():
        dual_near = halo(3, dual_ref, dual, lower(2), upper(2))
        coef_near = halo(1, factor_ref, coef, lower(1), upper(1))
        dual_far = halo(4, dual_ref, dual, lower(depth - 2, 2), upper(depth - 3, 2))
        coef_far = halo(2, factor_ref, coef, lower(depth - 2, 1), upper(depth - 3, 1))
        heat_halo = halo(0, heat_ref, heat, lower(depth), upper(depth - 1))
        start(dual_near)
        start(coef_near)
        start(coef_far)
        start(dual_far)
        for m in range(early):
            greet(m, slab, ready)
        rounds = []
        reach = CLOSE
        while reach < n_slab // 2:
            rounds.append(reach)
            reach *= 2

        def tell(index):
            for offset in (-rounds[index], rounds[index]):
                greet(sec, along(offset), known.at[index])

        if rounds:
            tell(0)
        clear(heat, dual)

        for load in tables:
            load.wait()
        mine = sec - melts
        names = part_ref[pl.ds(mine, 1), :].astype(jnp.float32)
        flags = flag_ref[pl.ds(mine, 1), :].astype(jnp.float32)
        names_col, flags_col = column(names), column(flags)
        same = jnp.where(names_col == names, 1.0, 0.0)
        rank_col = jnp.sum(jnp.where(lane_i < row_i, same, 0.0), axis=1, keepdims=True)
        rank_row = jnp.sum(jnp.where(row_i < lane_i, same, 0.0), axis=0, keepdims=True)
        count = melts * PAIRCAP
        slot_lane = lax.broadcasted_iota(jnp.int32, (contact, count), 1).astype(jnp.float32)
        slot_row = lax.broadcasted_iota(jnp.int32, (count, contact), 0).astype(jnp.float32)
        place = jnp.where(slot_lane == names_col * PAIRCAP + rank_col, flags_col, 0.0)
        give = jnp.where(slot_row == names * PAIRCAP + rank_row, flags, 0.0)

        for load in loads:
            load.wait()
        told = [0]

        def hear(count):
            while told[0] < min(count, len(rounds)):
                pl.semaphore_wait(known.at[told[0]], 2)
                told[0] += 1
                if told[0] < len(rounds):
                    tell(told[0])

        early_sends = []

        def pick_basis(i):
            t = (dual, a1, a2, a3)[i]
            for z in range(depth):
                basis_rows[i, z] = jnp.dot(
                    give, t[first + z, :contact, :], precision=HIGHEST, preferred_element_type=jnp.float32
                )
            for place_m, m in enumerate(ahead):
                send = pltpu.make_async_remote_copy(
                    src_ref=basis_rows.at[i, :, slot_rows(m), :],
                    dst_ref=got.at[i, :, pl.ds(pl.multiple_of(mine * PAIRCAP, PAIRCAP), PAIRCAP), :],
                    send_sem=ahead_send.at[place_m, i], recv_sem=ahead_recv.at[mine], device_id=(m, slab), device_id_type=MESH,
                )
                only(mine, ahead[m], ingots, send.start)
                early_sends.append((m, send))

        def solve(which, t0, out, arrive_near, arrive_far, meanwhile, then):
            ts = (t0, a1, a2, a3)

            def grow(k, z):
                t = ts[k - 1]
                c = t[z]
                value = (coef[z] - (CENTRE - 6.0)) * c - ((t[z - 1] + t[z + 1]) + in_plane(c))
                if k == 1:
                    ts[k][z] = value * (1.0 / RADIUS)
                else:
                    ts[k][z] = value * (2.0 / RADIUS) - ts[k - 2][z]

            def grow_all(k, lo, hi):
                lax.fori_loop(lo, hi, lambda z, carry: grow(k, z) or carry, 0, unroll=hi - lo if hi - lo == 4 else 2)

            def add_up(terms, count):
                def plane(z, sums):
                    return tuple(s + fold(term) for s, term in zip(sums, terms(z)))

                sums = lax.fori_loop(first, last, plane, (jnp.zeros((8, width), jnp.float32),) * count, unroll=2)
                return [jnp.sum(total, axis=0, keepdims=True) for total in sums]

            def near_terms(z):
                x0, x1, x2 = (ref[z] for ref in ts[:3])
                return x0 * x0, x0 * x1, x1 * x1, x1 * x2, x2 * x2

            def far_terms(z):
                x2, x3 = a2[z], a3[z]
                image = (coef[z] - (CENTRE - 6.0)) * x3 - 2.0 * a3[z + 1] - in_plane(x3)
                return x2 * x3, x3 * x3, x3 * image * (1.0 / RADIUS)

            arrive_near()
            grow_all(1, first - 1, last + 1)
            clear(a1)
            grow_all(2, first, last)
            sums = add_up(near_terms, 5)
            arrive_far()
            for z in (first - 2, last + 1, last + 2):
                grow(1, z)
            for z in (first - 1, last, last + 1):
                grow(2, z)
            clear(a2)
            grow_all(3, first, last)
            grow(3, last)
            clear(a3)
            sums += add_up(far_terms, 3)
            for k in range(8):
                sums_ref[pl.ds(k, 1), :] = sums[k]
            hear(len(rounds))
            packed = pack(sums_ref[...])
            packed_ref[which] = packed
            for index, (_, shift) in enumerate(partners):
                pltpu.make_async_remote_copy(
                    src_ref=packed_ref.at[which], dst_ref=gather.at[which, pl.ds(index, 1)],
                    send_sem=sum_send.at[which], recv_sem=sum_recv.at[which],
                    device_id=(sec, partner(shift)), device_id_type=MESH,
                ).start()
            meanwhile()
            others = gather.at[which, pl.ds(0, n_slab - 1)]
            pltpu.make_async_copy(others, others, sum_recv.at[which]).wait()
            c = coefficients(packed + jnp.sum(gather[which, : n_slab - 1, :], axis=0, keepdims=True))
            then(c)

            def combine(z, carry):
                out[z - first] = (c[0] * ts[0][z] + c[1] * ts[1][z]) + (c[2] * ts[2][z] + c[3] * ts[3][z])
                return carry

            lax.fori_loop(first, last, combine, 0, unroll=2)

        def arrive_near():
            pick_basis(0)
            hear(1)
            wait_recv(dual_near)
            wait_recv(coef_near)

        def arrive_far():
            pick_basis(1)
            pick_basis(2)
            hear(2)
            wait_recv(coef_far)
            wait_recv(dual_far)
            start(heat_halo)

        sends = []

        def send_back(c):
            weights[...] = jnp.concatenate(c + c, axis=0)
            for m in ahead:
                send = pltpu.make_async_remote_copy(
                    src_ref=weights, dst_ref=weights_in.at[mine], send_sem=row_send.at[m], recv_sem=weight_recv.at[mine],
                    device_id=(m, slab), device_id_type=MESH,
                )
                only(mine, ahead[m], ingots, send.start)
            for z in range(depth):
                back[z] = (c[0] * basis_rows[0, z] + c[1] * basis_rows[1, z]) + (
                    c[2] * basis_rows[2, z] + c[3] * basis_rows[3, z]
                )
            pl.semaphore_wait(ready, melts - early)
            for index, (j, m) in enumerate(relayed):

                @pl.when(mine == j)
                def _():
                    pltpu.make_async_remote_copy(
                        src_ref=back.at[:, slot_rows(m), :], dst_ref=relay.at[index], send_sem=row_send.at[m],
                        recv_sem=relay_recv.at[index], device_id=(early, slab), device_id_type=MESH,
                    ).start()

            for m in range(melts):
                direct = [j for j in range(ingots) if (j, m) not in relayed and j not in ahead.get(m, [])]
                send = pltpu.make_async_remote_copy(
                    src_ref=back.at[:, slot_rows(m), :],
                    dst_ref=returned.at[pl.ds(first, depth), pl.ds(pl.multiple_of(mine * PAIRCAP, PAIRCAP), PAIRCAP), :],
                    send_sem=row_send.at[m], recv_sem=row_recv.at[mine], device_id=(m, slab), device_id_type=MESH,
                )
                only(mine, direct, ingots, send.start)
                sends.append((m, send))

        solve(0, dual, adjoint_ref, arrive_near, arrive_far, lambda: pick_basis(3), send_back)

        passed = []
        for m in range(melts):
            region = slots.at[pl.ds(first, depth), slot_rows(m)]
            pltpu.make_async_copy(region, region, row_recv.at[m]).wait()
            passed.append(pass_on(slots, slot_rows(m), m))

        def load_up(at):
            for z in range(at, at + depth):
                rows = jnp.dot(place, slots[z], precision=HIGHEST, preferred_element_type=jnp.float32)
                heat[z, pl.ds(0, contact), :] = heat[z, pl.ds(0, contact), :] + rows

        wait_recv(heat_halo)
        load_up(first)

        @pl.when(has_left)
        def _():
            take(slots, 0)
            load_up(0)

        @pl.when(has_right)
        def _():
            take(slots, 1)
            load_up(last)

        solve(1, heat, state_ref, lambda: None, lambda: None, lambda: None, lambda c: None)

        for pair in [dual_near, coef_near, dual_far, coef_far, heat_halo] + passed:
            wait_send(pair)
        for m, send in early_sends:
            only(mine, ahead[m], ingots, send.wait_send)
        for m, send in sends:
            summed = ahead.get(m, [])
            only(mine, summed, ingots, lambda m=m: pltpu.make_async_copy(weights, weights, row_send.at[m]).wait())
            only(mine, [j for j in range(ingots) if j not in summed], ingots, send.wait_send)
        for which in range(2):
            others = gather.at[which, pl.ds(0, n_slab - 1)]
            pltpu.make_async_copy(others, others, sum_send.at[which]).wait()


def body(n_sec, n_slab, heat_level, material_factor, dual_sensitivity, part, line, flag, instant):
    ingots, contact = line.shape
    melts = n_sec - ingots
    _, depth, height, width = heat_level.shape
    f32 = jnp.float32
    wide = pltpu.VMEM((3 * depth, height, width), f32)
    table = pltpu.VMEM((ingots, contact), jnp.int32)
    dma = pltpu.SemaphoreType.DMA
    most = max(melts, ingots)
    scratch = [
        table, table, table,
        wide, wide, wide, wide, wide, wide,
        pltpu.VMEM((STEPS, 3 * depth, height, width), f32),
        wide, wide, wide, wide, wide, wide, wide,
        pltpu.VMEM((ingots * PAIRCAP, height), f32),
        pltpu.VMEM((height, ingots * PAIRCAP), f32),
        pltpu.VMEM((depth, ingots * PAIRCAP, width), f32),
        pltpu.VMEM((3 * depth, melts * PAIRCAP, width), f32),
        pltpu.VMEM((depth, melts * PAIRCAP, width), f32),
        pltpu.VMEM((BASIS, depth, melts * PAIRCAP, width), f32),
        pltpu.VMEM((max(len(relays(n_sec, ingots)), 1), depth, PAIRCAP, width), f32),
        pltpu.VMEM((BASIS, depth, ingots * PAIRCAP, width), f32),
        pltpu.VMEM((8, width), f32),
        pltpu.VMEM((ingots, 8, width), f32),
        pltpu.VMEM((3 * depth, ingots * PAIRCAP, width), f32),
        pltpu.VMEM((8, width), f32),
        pltpu.VMEM((2, 1, width), f32),
        pltpu.VMEM((2, n_slab, width), f32),
        dma((6,)), dma((5, 2)), dma((5, 2)),
        dma((most,)), dma((most,)), dma((2, most)), dma((2,)),
        dma((2,)), dma((2,)), pltpu.SemaphoreType.REGULAR, pltpu.SemaphoreType.REGULAR((4,)),
        dma((8,)), dma((8,)), dma((4, BASIS)), dma((ingots,)), dma((ingots,)),
    ]
    hbm, vmem, smem = (pl.BlockSpec(memory_space=s) for s in (pltpu.HBM, pltpu.VMEM, pltpu.SMEM))
    fields = (part[:, :, 0], line, flag, heat_level[0], material_factor[0], dual_sensitivity[0])
    fields = [pltpu.with_memory_space_constraint(field, pltpu.HBM) for field in fields]
    both = pl.pallas_call(
        functools.partial(kernel, n_sec, n_slab),
        out_shape=jax.ShapeDtypeStruct((2, depth, height, width), f32),
        in_specs=[hbm, hbm, hbm, smem, hbm, hbm, hbm],
        out_specs=vmem,
        scratch_shapes=scratch,
        compiler_params=pltpu.CompilerParams(
            collective_id=0, has_side_effects=True, vmem_limit_bytes=32 * 1024 * 1024
        ),
    )(*fields[:3], instant, *fields[3:])
    return both[0:1], both[1:2]


def solution(mesh):
    n_sec, n_slab = mesh.shape["sec"], mesh.shape["slab"]
    fields = P("sec", "slab", None, None)
    return jax.shard_map(
        functools.partial(body, n_sec, n_slab),
        mesh=mesh,
        in_specs=(fields, fields, fields, P(), P(), P(), P()),
        out_specs=(fields, fields),
        check_vma=False,
    )
```

```python
import functools
import math

import jax
import jax.numpy as jnp
from jax import lax
from jax.experimental import pallas as pl
from jax.experimental.pallas import tpu as pltpu
from jax.sharding import PartitionSpec as P

STEPS = 4
PAIRCAP = 8
BASIS = 4
CLOSE = 4

time_step = 0.1
sink_rate = 0.5
period_steps = 16.0

CENTRE = 6.8
RADIUS = 6.4

MESH = pl.DeviceIdType.MESH
HIGHEST = lax.Precision.HIGHEST


def in_plane(c):
    rows, cols = c.shape
    row = lax.broadcasted_iota(jnp.int32, c.shape, 0)
    col = lax.broadcasted_iota(jnp.int32, c.shape, 1)
    up = jnp.where(row == 0, 0.0, pltpu.roll(c, 1, 0))
    down = jnp.where(row == rows - 1, 0.0, pltpu.roll(c, rows - 1, 0))
    left = jnp.where(col == 0, 0.0, pltpu.roll(c, 1, 1))
    right = jnp.where(col == cols - 1, 0.0, pltpu.roll(c, cols - 1, 1))
    return (up + down) + (left + right)


def fold(values):
    rows, cols = values.shape
    return jnp.sum(values.reshape(rows // 8, 8, cols), axis=0)


def own_lanes(values):
    row = lax.broadcasted_iota(jnp.int32, values.shape, 0)
    lane = lax.broadcasted_iota(jnp.int32, values.shape, 1)
    each = values.shape[1] // values.shape[0]
    return jnp.where((lane >= row * each) & (lane < (row + 1) * each), values, 0.0)


def pack(values):
    lanes = values.shape[1]
    for distance in (lanes // 2, lanes // 4, lanes // 8):
        values = values + pltpu.roll(values, distance, 1)
    return jnp.sum(own_lanes(values), axis=0, keepdims=True)


def coefficients(packed):
    spread = own_lanes(jnp.broadcast_to(packed, (8, packed.shape[1])))
    total = jnp.broadcast_to(jnp.sum(spread, axis=1, keepdims=True), spread.shape)
    s = [total[k : k + 1, :] for k in range(8)]
    nu = [s[0], s[1], 2.0 * s[2] - s[0], 2.0 * s[3] - s[1], 2.0 * s[4] - s[0], 2.0 * s[5] - s[1], 2.0 * s[6] - s[0]]
    nu.append(4.0 * s[7] - 2.0 * s[5] - s[1])
    shift = 2.0 * CENTRE / RADIUS
    u = [shift * nu[k] + nu[k + 1] + nu[abs(k - 1)] for k in range(7)]
    mat = [[u[i + j] + u[abs(i - j)] for j in range(BASIS)] for i in range(BASIS)]
    diag = [mat[i][i] for i in range(BASIS)]
    rhs = [(4.0 / RADIUS) * nu[i] for i in range(BASIS)]
    inverse = []
    for k in range(BASIS):
        good = mat[k][k] > 1e-8 * diag[k]
        inv = jnp.where(good, 1.0 / jnp.where(good, mat[k][k], 1.0), 0.0)
        inverse.append(inv)
        for i in range(k + 1, BASIS):
            factor = mat[k][i] * inv
            for j in range(i, BASIS):
                mat[i][j] = mat[i][j] - factor * mat[k][j]
            rhs[i] = rhs[i] - factor * rhs[k]
    out = [None] * BASIS
    for i in reversed(range(BASIS)):
        value = rhs[i]
        for j in range(i + 1, BASIS):
            value = value - mat[i][j] * out[j]
        out[i] = value * inverse[i]
    return out


def relays(n_sec, ingots):
    if (n_sec, ingots) != (16, 4):
        return []
    return [(2, 6), (3, 6)]


def ahead_of(ingots, lead):
    return dict([(0, list(range(ingots))), (1, list(range(ingots // 2, ingots)))][:lead])


def kernel(
    n_sec,
    n_slab,
    part_hbm,
    line_hbm,
    flag_hbm,
    instant_ref,
    heat_ref,
    factor_ref,
    dual_ref,
    both_ref,
    part_ref,
    line_ref,
    flag_ref,
    heat,
    coef,
    dual,
    a1,
    a2,
    a3,
    keep,
    mu3,
    mu2,
    mu1,
    w4,
    w3,
    w2,
    w1,
    pick,
    pick_t,
    offered,
    slots,
    back,
    basis_rows,
    relay,
    got,
    weights,
    weights_in,
    returned,
    sums_ref,
    packed_ref,
    gather,
    local_sem,
    halo_send,
    halo_recv,
    row_send,
    row_recv,
    side_send,
    side_recv,
    sum_send,
    sum_recv,
    ready,
    known,
    relay_send,
    relay_recv,
    ahead_send,
    ahead_recv,
    weight_recv,
):
    ingots, contact = part_hbm.shape
    melts = n_sec - ingots
    lead = melts // 3
    early = 2 * lead
    depth, height, width = heat_ref.shape
    first, last = depth, 2 * depth
    sec, slab = lax.axis_index("sec"), lax.axis_index("slab")
    is_melt = sec < melts
    is_early = sec < early
    is_lead = sec < lead
    relayed = relays(n_sec, ingots)
    targets = sorted({m for _, m in relayed})
    ahead = ahead_of(ingots, lead)

    def any_of(value, choices):
        return functools.reduce(jnp.logical_or, [value == choice for choice in choices])

    def only(value, choices, count, action):
        if len(choices) == count:
            action()
        elif choices:
            pl.when(any_of(value, choices))(action)

    has_left, has_right = slab > 0, slab < n_slab - 1
    state_ref, adjoint_ref = both_ref.at[0], both_ref.at[1]

    loads = [
        pltpu.make_async_copy(src, dst.at[pl.ds(first, depth)], local_sem.at[i])
        for i, (src, dst) in enumerate(((heat_ref, heat), (factor_ref, coef), (dual_ref, dual)))
    ]
    tables = [
        pltpu.make_async_copy(src, dst, local_sem.at[3 + i])
        for i, (src, dst) in enumerate(((part_hbm, part_ref), (line_hbm, line_ref), (flag_hbm, flag_ref)))
    ]
    barrier = pltpu.get_barrier_semaphore()

    def greet(to_sec, to_slab, sem=barrier):
        pl.semaphore_signal(sem, inc=1, device_id=(to_sec, to_slab), device_id_type=MESH)

    def along(offset):
        return lax.rem(slab + offset % n_slab, n_slab)

    sizes = (4, 4, 2) if n_slab == 32 else (n_slab,)
    partners = []
    for flat in range(1, n_slab):
        shift, rest = [], flat
        for size in reversed(sizes):
            shift.insert(0, rest % size)
            rest //= size
        partners.append((sum(min(step, size - step) for step, size in zip(shift, sizes)), tuple(shift)))
    partners.sort(key=lambda entry: (-entry[0], entry[1]))

    digits, rest = [], slab
    for size in reversed(sizes):
        digits.insert(0, lax.rem(rest, size))
        rest = lax.div(rest, size)
    strides = [math.prod(sizes[place + 1 :]) for place in range(len(sizes))]
    moved = [
        [lax.rem(digit + step, size) * stride for step in range(size)]
        for digit, size, stride in zip(digits, sizes, strides)
    ]

    def partner(shift):
        return sum(moved[place][step] for place, step in enumerate(shift))

    near = sorted({offset % n_slab for offset in range(-CLOSE, CLOSE + 1)} - {0})

    @pl.when(is_melt)
    def _():
        pl.when(has_left)(lambda: greet(sec, slab - 1))
        pl.when(has_right)(lambda: greet(sec, slab + 1))

        @pl.when(is_lead)
        def _():
            for j in range(ingots):
                greet(melts + j, slab)

        @pl.when(is_early & jnp.logical_not(is_lead))
        def _():
            greet(sec - lead, slab)

        for m in targets:
            pl.when(sec == m)(lambda: greet(early, slab))

    @pl.when(jnp.logical_not(is_melt))
    def _():
        for offset in near:
            greet(sec, along(offset))
        for m in range(early, melts):
            greet(m, slab)

    beside = has_left.astype(jnp.int32) + has_right.astype(jnp.int32)
    heard = jnp.where(is_melt, beside + jnp.where(is_lead, 1, jnp.where(is_early, 0, ingots)), len(near) + lead)
    heard = heard + jnp.where(sec == early, len(targets), 0) if targets else heard
    for load in tables + loads:
        load.start()
    pl.semaphore_wait(barrier, heard)

    def halo(index, src, dst, to_left, to_right):
        (left_src, left_dst), (right_src, right_dst) = to_left, to_right
        send, recv = halo_send.at[index], halo_recv.at[index]
        return (
            pltpu.make_async_remote_copy(
                src_ref=src.at[left_src], dst_ref=dst.at[left_dst], send_sem=send.at[0], recv_sem=recv.at[1],
                device_id=(sec, slab - 1), device_id_type=MESH,
            ),
            pltpu.make_async_remote_copy(
                src_ref=src.at[right_src], dst_ref=dst.at[right_dst], send_sem=send.at[1], recv_sem=recv.at[0],
                device_id=(sec, slab + 1), device_id_type=MESH,
            ),
        )

    def start(pair):
        pl.when(has_left)(lambda: pair[0].start())
        pl.when(has_right)(lambda: pair[1].start())

    def wait_recv(pair):
        pl.when(has_right)(lambda: pair[0].wait_recv())
        pl.when(has_left)(lambda: pair[1].wait_recv())

    def wait_send(pair):
        pl.when(has_left)(lambda: pair[0].wait_send())
        pl.when(has_right)(lambda: pair[1].wait_send())

    def lower(planes, offset=0):
        return pl.ds(offset, planes), pl.ds(last + offset, planes)

    def upper(planes, offset=0):
        at = depth - planes - offset
        return pl.ds(at, planes), pl.ds(at, planes)

    def pass_on(buf, rows, index):
        here = buf.at[pl.ds(first, depth), rows]
        pair = []
        for side, there, to in ((0, last, slab - 1), (1, 0, slab + 1)):
            pair.append(
                pltpu.make_async_remote_copy(
                    src_ref=here, dst_ref=buf.at[pl.ds(there, depth), rows], send_sem=side_send.at[side, index],
                    recv_sem=side_recv.at[1 - side], device_id=(sec, to), device_id_type=MESH,
                )
            )
        start(pair)
        return pair

    def take(buf, side):
        region = buf.at[pl.ds(2 * depth * side, depth)]
        pltpu.make_async_copy(region, region, side_recv.at[side]).wait()

    zero = jnp.zeros((height, width), jnp.float32)

    def clear(*bufs):
        @pl.when(jnp.logical_not(has_left))
        def _():
            for buf in bufs:
                buf[first - 1] = zero

        @pl.when(jnp.logical_not(has_right))
        def _():
            for buf in bufs:
                buf[last] = zero

    row_i = lax.broadcasted_iota(jnp.int32, (contact, contact), 0)
    lane_i = lax.broadcasted_iota(jnp.int32, (contact, contact), 1)

    def column(row):
        return jnp.sum(jnp.where(row_i == lane_i, row, 0.0), axis=1, keepdims=True)

    def slot_rows(index):
        return pl.ds(index * PAIRCAP, PAIRCAP)

    @pl.when(is_melt)
    def _():
        heat_halo = halo(0, heat_ref, heat, lower(depth), upper(depth))
        coef_halo = halo(1, factor_ref, coef, lower(depth - 1), upper(depth - 1))
        edge_halo = halo(2, factor_ref, coef, lower(1, depth - 1), upper(1, depth - 1))
        dual_halo = halo(3, dual_ref, dual, lower(depth), upper(depth))
        start(heat_halo)
        start(coef_halo)

        @pl.when(jnp.logical_not(is_early))
        def _():
            for j in range(ingots):
                greet(melts + j, slab, ready)

        clear(heat, dual, w4)
        for load in tables:
            load.wait()

        for j in range(ingots):
            named = part_ref[j : j + 1, :].astype(jnp.float32) == sec.astype(jnp.float32)
            lines = line_ref[j : j + 1, :].astype(jnp.float32)
            before = column(jnp.where(named, 1.0, 0.0))
            rank = jnp.sum(jnp.where(row_i < lane_i, before, 0.0), axis=0, keepdims=True)
            slot = lax.broadcasted_iota(jnp.int32, (PAIRCAP, contact), 0).astype(jnp.float32)
            chosen = jnp.where(named, 1.0, 0.0) * jnp.where(rank == slot, 1.0, 0.0)
            slot_line = jnp.sum(chosen * lines, axis=1, keepdims=True)
            live = jnp.sum(chosen, axis=1, keepdims=True)
            q = lax.broadcasted_iota(jnp.int32, (PAIRCAP, height), 1).astype(jnp.float32)
            pick[slot_rows(j), :] = jnp.where(q == slot_line, live, 0.0)
        eye = jnp.where(
            lax.broadcasted_iota(jnp.int32, (height, height), 0) == lax.broadcasted_iota(jnp.int32, (height, height), 1),
            1.0, 0.0,
        )
        pick_t[...] = lax.dot_general(
            eye, pick[...], (((1,), (1,)), ((), ())), precision=HIGHEST, preferred_element_type=jnp.float32
        )

        archived = instant_ref[0].astype(jnp.float32)
        speeds = []
        for k in range(STEPS):
            phase = jnp.full((1, width), archived + k)
            speeds.append(1.0 + 0.5 * jnp.sin(2.0 * math.pi * phase / period_steps))

        for load in loads:
            load.wait()
        wait_recv(heat_halo)
        wait_recv(coef_halo)
        start(edge_halo)
        start(dual_halo)

        states = (heat, a1, a2, a3, state_ref)
        for k in range(STEPS):
            src, dst = states[k], states[k + 1]
            final = k == STEPS - 1
            shift = first if final else 0

            def forward(z, carry, k=k, src=src, dst=dst, shift=shift):
                c = src[z]
                below = src[z - 1]
                total = (below + src[z + 1]) + in_plane(c)
                change = coef[z] * (total - 6.0 * c) - speeds[k] * (c - below)
                bent = jnp.tanh(c)
                dst[z - shift] = c + time_step * change - time_step * sink_rate * bent
                keep[k, z] = 1.0 - time_step * sink_rate * (1.0 - bent * bent)
                return carry

            lax.fori_loop(1 + k, 3 * depth - 1 - k, forward, 0, unroll=2)
            if not final:
                clear(dst)

        for z in range(depth):
            offered[z] = jnp.dot(pick[...], state_ref[z], precision=HIGHEST, preferred_element_type=jnp.float32)
        @pl.when(is_lead)
        def _():
            pl.semaphore_wait(ready, ingots)
            greet(sec + lead, slab, ready)
            for j in range(ingots):
                greet(melts + j, slab, ready)

        @pl.when(is_early & jnp.logical_not(is_lead))
        def _():
            pl.semaphore_wait(ready, 1)

        sends = []
        for j in range(ingots):
            send = pltpu.make_async_remote_copy(
                src_ref=offered.at[:, slot_rows(j), :],
                dst_ref=slots.at[pl.ds(first, depth), pl.ds(pl.multiple_of(sec * PAIRCAP, PAIRCAP), PAIRCAP), :],
                send_sem=row_send.at[j], recv_sem=row_recv.at[sec], device_id=(melts + j, slab), device_id_type=MESH,
            )
            send.start()
            sends.append(send)
        keep3 = keep.at[3]
        keep_halo = halo(
            4, keep3, keep3, (pl.ds(first, depth - 1), pl.ds(last, depth - 1)), (pl.ds(first + 1, depth - 1), pl.ds(1, depth - 1))
        )
        start(keep_halo)

        for z in (first - 2, last + 1):
            bent = jnp.tanh(a2[z])
            keep[2, z] = 1.0 - time_step * sink_rate * (1.0 - bent * bent)
        wait_recv(edge_halo)
        wait_recv(dual_halo)
        wait_recv(keep_halo)

        def relay_on(index):
            j, m = relayed[index]
            return pltpu.make_async_remote_copy(
                src_ref=relay.at[index], dst_ref=returned.at[pl.ds(first, depth), slot_rows(j), :],
                send_sem=relay_send.at[index], recv_sem=row_recv.at[j], device_id=(m, slab), device_id_type=MESH,
            )

        if relayed:

            @pl.when(sec == early)
            def _():
                for index in range(len(relayed)):
                    pltpu.make_async_copy(relay.at[index], relay.at[index], relay_recv.at[index]).wait()
                    relay_on(index).start()

        passed = []
        for j in reversed(range(ingots)):
            rows = slot_rows(j)

            def arrive(j=j, rows=rows):
                region = returned.at[pl.ds(first, depth), rows]
                pltpu.make_async_copy(region, region, row_recv.at[j]).wait()

            def add_up(j=j, rows=rows):
                region = got.at[:, :, rows]
                pltpu.make_async_copy(region, region, ahead_recv.at[j]).wait()
                pltpu.make_async_copy(weights_in.at[j], weights_in.at[j], weight_recv.at[j]).wait()
                c = [weights_in[j, i : i + 1, :] for i in range(BASIS)]
                for z in range(depth):
                    returned[first + z, rows, :] = (c[0] * got[0, z, rows, :] + c[1] * got[1, z, rows, :]) + (
                        c[2] * got[2, z, rows, :] + c[3] * got[3, z, rows, :]
                    )

            summed = [m for m in ahead if j in ahead[m]]
            if summed:
                pl.when(any_of(sec, summed))(add_up)
                pl.when(jnp.logical_not(any_of(sec, summed)))(arrive)
            else:
                arrive()
            passed.append(pass_on(returned, rows, j))

        def add_returned(at):
            for z in range(at, at + depth):
                rows = jnp.dot(pick_t[...], returned[z], precision=HIGHEST, preferred_element_type=jnp.float32)
                value = dual[z] + rows
                dual[z] = value
                w4[z] = coef[z] * value

        add_returned(first)

        mus, ws = (adjoint_ref, mu1, mu2, mu3, dual), (None, w1, w2, w3, w4)

        def backward(k, lo, hi):
            src, dst, wsrc, wdst = mus[k + 1], mus[k], ws[k + 1], ws[k]
            shift = first if k == 0 else 0

            def plane(z, carry):
                c, w = src[z], wsrc[z]
                total = (wsrc[z - 1] + wsrc[z + 1]) + in_plane(w)
                change = total - 6.0 * w - speeds[k] * (c - src[z + 1])
                value = keep[k, z] * c + time_step * change
                dst[z - shift] = value
                if wdst is not None:
                    wdst[z] = coef[z] * value
                return carry

            lax.fori_loop(lo, hi, plane, 0, unroll=hi - lo if hi - lo == 4 else 2)
            if wdst is not None:
                clear(dst, wdst)

        right_first = (slab % 2 == 0) | ((sec == 0) & (slab == 1) & has_right)

        @pl.when(right_first)
        def _():
            take(returned, 1)
            add_returned(last)
            for k in (3, 2, 1):
                backward(k, first + STEPS - k, last + k)

            @pl.when(has_left)
            def _():
                take(returned, 0)
                add_returned(0)

            for k in (3, 2, 1, 0):
                backward(k, first - k, first + STEPS - k)

        @pl.when(jnp.logical_not(right_first))
        def _():
            take(returned, 0)
            add_returned(0)
            for k in (3, 2, 1):
                backward(k, first - k, last - STEPS + k)

            @pl.when(has_right)
            def _():
                take(returned, 1)
                add_returned(last)

            for k in (3, 2, 1, 0):
                backward(k, last - STEPS + k, last + k)

        if relayed:

            @pl.when(sec == early)
            def _():
                for index in range(len(relayed)):
                    relay_on(index).wait_send()

        for pair in [heat_halo, coef_halo, edge_halo, dual_halo, keep_halo] + passed:
            wait_send(pair)
        for send in sends:
            send.wait_send()

    @pl.when(jnp.logical_not(is_melt))
    def _():
        dual_near = halo(3, dual_ref, dual, lower(2), upper(2))
        coef_near = halo(1, factor_ref, coef, lower(1), upper(1))
        dual_far = halo(4, dual_ref, dual, lower(depth - 2, 2), upper(depth - 3, 2))
        coef_far = halo(2, factor_ref, coef, lower(depth - 2, 1), upper(depth - 3, 1))
        heat_halo = halo(0, heat_ref, heat, lower(depth), upper(depth - 1))
        start(dual_near)
        start(coef_near)
        start(coef_far)
        start(dual_far)
        for m in range(lead):
            greet(m, slab, ready)
        rounds = []
        reach = CLOSE
        while reach < n_slab // 2:
            rounds.append(reach)
            reach *= 2

        def tell(index):
            for offset in (-rounds[index], rounds[index]):
                greet(sec, along(offset), known.at[index])

        if rounds:
            tell(0)
        clear(heat, dual)

        for load in tables:
            load.wait()
        mine = sec - melts
        names = part_ref[pl.ds(mine, 1), :].astype(jnp.float32)
        flags = flag_ref[pl.ds(mine, 1), :].astype(jnp.float32)
        names_col, flags_col = column(names), column(flags)
        same = jnp.where(names_col == names, 1.0, 0.0)
        rank_col = jnp.sum(jnp.where(lane_i < row_i, same, 0.0), axis=1, keepdims=True)
        rank_row = jnp.sum(jnp.where(row_i < lane_i, same, 0.0), axis=0, keepdims=True)
        count = melts * PAIRCAP
        slot_lane = lax.broadcasted_iota(jnp.int32, (contact, count), 1).astype(jnp.float32)
        slot_row = lax.broadcasted_iota(jnp.int32, (count, contact), 0).astype(jnp.float32)
        place = jnp.where(slot_lane == names_col * PAIRCAP + rank_col, flags_col, 0.0)
        give = jnp.where(slot_row == names * PAIRCAP + rank_row, flags, 0.0)

        for load in loads:
            load.wait()
        told = [0]

        def hear(count):
            while told[0] < min(count, len(rounds)):
                pl.semaphore_wait(known.at[told[0]], 2)
                told[0] += 1
                if told[0] < len(rounds):
                    tell(told[0])

        early_sends = []

        def pick_basis(i):
            t = (dual, a1, a2, a3)[i]
            for z in range(depth):
                basis_rows[i, z] = jnp.dot(
                    give, t[first + z, :contact, :], precision=HIGHEST, preferred_element_type=jnp.float32
                )
            for place_m, m in enumerate(ahead):
                send = pltpu.make_async_remote_copy(
                    src_ref=basis_rows.at[i, :, slot_rows(m), :],
                    dst_ref=got.at[i, :, pl.ds(pl.multiple_of(mine * PAIRCAP, PAIRCAP), PAIRCAP), :],
                    send_sem=ahead_send.at[place_m, i], recv_sem=ahead_recv.at[mine], device_id=(m, slab), device_id_type=MESH,
                )
                only(mine, ahead[m], ingots, send.start)
                early_sends.append((m, send))

        def solve(which, t0, out, arrive_near, arrive_far, meanwhile, then):
            ts = (t0, a1, a2, a3)

            def grow(k, z):
                t = ts[k - 1]
                c = t[z]
                value = (coef[z] - (CENTRE - 6.0)) * c - ((t[z - 1] + t[z + 1]) + in_plane(c))
                if k == 1:
                    ts[k][z] = value * (1.0 / RADIUS)
                else:
                    ts[k][z] = value * (2.0 / RADIUS) - ts[k - 2][z]

            def grow_all(k, lo, hi):
                lax.fori_loop(lo, hi, lambda z, carry: grow(k, z) or carry, 0, unroll=hi - lo if hi - lo == 4 else 2)

            def add_up(terms, count):
                def plane(z, sums):
                    return tuple(s + fold(term) for s, term in zip(sums, terms(z)))

                sums = lax.fori_loop(first, last, plane, (jnp.zeros((8, width), jnp.float32),) * count, unroll=2)
                return [jnp.sum(total, axis=0, keepdims=True) for total in sums]

            def near_terms(z):
                x0, x1, x2 = (ref[z] for ref in ts[:3])
                return x0 * x0, x0 * x1, x1 * x1, x1 * x2, x2 * x2

            def far_terms(z):
                x2, x3 = a2[z], a3[z]
                image = (coef[z] - (CENTRE - 6.0)) * x3 - 2.0 * a3[z + 1] - in_plane(x3)
                return x2 * x3, x3 * x3, x3 * image * (1.0 / RADIUS)

            arrive_near()
            grow_all(1, first - 1, last + 1)
            clear(a1)
            grow_all(2, first, last)
            sums = add_up(near_terms, 5)
            arrive_far()
            for z in (first - 2, last + 1, last + 2):
                grow(1, z)
            for z in (first - 1, last, last + 1):
                grow(2, z)
            clear(a2)
            grow_all(3, first, last)
            grow(3, last)
            clear(a3)
            sums += add_up(far_terms, 3)
            for k in range(8):
                sums_ref[pl.ds(k, 1), :] = sums[k]
            hear(len(rounds))
            packed = pack(sums_ref[...])
            packed_ref[which] = packed
            for index, (_, shift) in enumerate(partners):
                pltpu.make_async_remote_copy(
                    src_ref=packed_ref.at[which], dst_ref=gather.at[which, pl.ds(index, 1)],
                    send_sem=sum_send.at[which], recv_sem=sum_recv.at[which],
                    device_id=(sec, partner(shift)), device_id_type=MESH,
                ).start()
            meanwhile()
            others = gather.at[which, pl.ds(0, n_slab - 1)]
            pltpu.make_async_copy(others, others, sum_recv.at[which]).wait()
            c = coefficients(packed + jnp.sum(gather[which, : n_slab - 1, :], axis=0, keepdims=True))
            then(c)

            def combine(z, carry):
                out[z - first] = (c[0] * ts[0][z] + c[1] * ts[1][z]) + (c[2] * ts[2][z] + c[3] * ts[3][z])
                return carry

            lax.fori_loop(first, last, combine, 0, unroll=2)

        def arrive_near():
            pick_basis(0)
            hear(1)
            wait_recv(dual_near)
            wait_recv(coef_near)

        def arrive_far():
            pick_basis(1)
            pick_basis(2)
            hear(2)
            wait_recv(coef_far)
            wait_recv(dual_far)
            start(heat_halo)

        sends = []

        def send_back(c):
            weights[...] = jnp.concatenate(c + c, axis=0)
            for m in ahead:
                send = pltpu.make_async_remote_copy(
                    src_ref=weights, dst_ref=weights_in.at[mine], send_sem=row_send.at[m], recv_sem=weight_recv.at[mine],
                    device_id=(m, slab), device_id_type=MESH,
                )
                only(mine, ahead[m], ingots, send.start)
            for z in range(depth):
                back[z] = (c[0] * basis_rows[0, z] + c[1] * basis_rows[1, z]) + (
                    c[2] * basis_rows[2, z] + c[3] * basis_rows[3, z]
                )
            pl.semaphore_wait(ready, melts - early + lead)
            for index, (j, m) in enumerate(relayed):

                @pl.when(mine == j)
                def _():
                    pltpu.make_async_remote_copy(
                        src_ref=back.at[:, slot_rows(m), :], dst_ref=relay.at[index], send_sem=row_send.at[m],
                        recv_sem=relay_recv.at[index], device_id=(early, slab), device_id_type=MESH,
                    ).start()

            for m in range(melts):
                direct = [j for j in range(ingots) if (j, m) not in relayed and j not in ahead.get(m, [])]
                send = pltpu.make_async_remote_copy(
                    src_ref=back.at[:, slot_rows(m), :],
                    dst_ref=returned.at[pl.ds(first, depth), pl.ds(pl.multiple_of(mine * PAIRCAP, PAIRCAP), PAIRCAP), :],
                    send_sem=row_send.at[m], recv_sem=row_recv.at[mine], device_id=(m, slab), device_id_type=MESH,
                )
                only(mine, direct, ingots, send.start)
                sends.append((m, send))

        solve(0, dual, adjoint_ref, arrive_near, arrive_far, lambda: pick_basis(3), send_back)

        passed = []
        for m in range(melts):
            region = slots.at[pl.ds(first, depth), slot_rows(m)]
            pltpu.make_async_copy(region, region, row_recv.at[m]).wait()
            passed.append(pass_on(slots, slot_rows(m), m))

        def load_up(at):
            for z in range(at, at + depth):
                rows = jnp.dot(place, slots[z], precision=HIGHEST, preferred_element_type=jnp.float32)
                heat[z, pl.ds(0, contact), :] = heat[z, pl.ds(0, contact), :] + rows

        wait_recv(heat_halo)
        load_up(first)

        @pl.when(has_left)
        def _():
            take(slots, 0)
            load_up(0)

        @pl.when(has_right)
        def _():
            take(slots, 1)
            load_up(last)

        solve(1, heat, state_ref, lambda: None, lambda: None, lambda: None, lambda c: None)

        for pair in [dual_near, coef_near, dual_far, coef_far, heat_halo] + passed:
            wait_send(pair)
        for m, send in early_sends:
            only(mine, ahead[m], ingots, send.wait_send)
        for m, send in sends:
            summed = ahead.get(m, [])
            only(mine, summed, ingots, lambda m=m: pltpu.make_async_copy(weights, weights, row_send.at[m]).wait())
            only(mine, [j for j in range(ingots) if j not in summed], ingots, send.wait_send)
        for which in range(2):
            others = gather.at[which, pl.ds(0, n_slab - 1)]
            pltpu.make_async_copy(others, others, sum_send.at[which]).wait()


def body(n_sec, n_slab, heat_level, material_factor, dual_sensitivity, part, line, flag, instant):
    ingots, contact = line.shape
    melts = n_sec - ingots
    _, depth, height, width = heat_level.shape
    f32 = jnp.float32
    wide = pltpu.VMEM((3 * depth, height, width), f32)
    table = pltpu.VMEM((ingots, contact), jnp.int32)
    dma = pltpu.SemaphoreType.DMA
    most = max(melts, ingots)
    scratch = [
        table, table, table,
        wide, wide, wide, wide, wide, wide,
        pltpu.VMEM((STEPS, 3 * depth, height, width), f32),
        wide, wide, wide, wide, wide, wide, wide,
        pltpu.VMEM((ingots * PAIRCAP, height), f32),
        pltpu.VMEM((height, ingots * PAIRCAP), f32),
        pltpu.VMEM((depth, ingots * PAIRCAP, width), f32),
        pltpu.VMEM((3 * depth, melts * PAIRCAP, width), f32),
        pltpu.VMEM((depth, melts * PAIRCAP, width), f32),
        pltpu.VMEM((BASIS, depth, melts * PAIRCAP, width), f32),
        pltpu.VMEM((max(len(relays(n_sec, ingots)), 1), depth, PAIRCAP, width), f32),
        pltpu.VMEM((BASIS, depth, ingots * PAIRCAP, width), f32),
        pltpu.VMEM((8, width), f32),
        pltpu.VMEM((ingots, 8, width), f32),
        pltpu.VMEM((3 * depth, ingots * PAIRCAP, width), f32),
        pltpu.VMEM((8, width), f32),
        pltpu.VMEM((2, 1, width), f32),
        pltpu.VMEM((2, n_slab, width), f32),
        dma((6,)), dma((5, 2)), dma((5, 2)),
        dma((most,)), dma((most,)), dma((2, most)), dma((2,)),
        dma((2,)), dma((2,)), pltpu.SemaphoreType.REGULAR, pltpu.SemaphoreType.REGULAR((4,)),
        dma((8,)), dma((8,)), dma((4, BASIS)), dma((ingots,)), dma((ingots,)),
    ]
    hbm, vmem, smem = (pl.BlockSpec(memory_space=s) for s in (pltpu.HBM, pltpu.VMEM, pltpu.SMEM))
    fields = (part[:, :, 0], line, flag, heat_level[0], material_factor[0], dual_sensitivity[0])
    fields = [pltpu.with_memory_space_constraint(field, pltpu.HBM) for field in fields]
    both = pl.pallas_call(
        functools.partial(kernel, n_sec, n_slab),
        out_shape=jax.ShapeDtypeStruct((2, depth, height, width), f32),
        in_specs=[hbm, hbm, hbm, smem, hbm, hbm, hbm],
        out_specs=vmem,
        scratch_shapes=scratch,
        compiler_params=pltpu.CompilerParams(
            collective_id=0, has_side_effects=True, vmem_limit_bytes=32 * 1024 * 1024
        ),
    )(*fields[:3], instant, *fields[3:])
    return both[0:1], both[1:2]


def solution(mesh):
    n_sec, n_slab = mesh.shape["sec"], mesh.shape["slab"]
    fields = P("sec", "slab", None, None)
    return jax.shard_map(
        functools.partial(body, n_sec, n_slab),
        mesh=mesh,
        in_specs=(fields, fields, fields, P(), P(), P(), P()),
        out_specs=(fields, fields),
        check_vma=False,
    )
```

```python
import functools
import math

import jax
import jax.numpy as jnp
from jax import lax
from jax.experimental import pallas as pl
from jax.experimental.pallas import tpu as pltpu
from jax.sharding import PartitionSpec as P

STEPS = 4
PAIRCAP = 8
BASIS = 4
CLOSE = 4

time_step = 0.1
sink_rate = 0.5
period_steps = 16.0

CENTRE = 6.8
RADIUS = 6.4

MESH = pl.DeviceIdType.MESH
HIGHEST = lax.Precision.HIGHEST


def in_plane(c):
    rows, cols = c.shape
    row = lax.broadcasted_iota(jnp.int32, c.shape, 0)
    col = lax.broadcasted_iota(jnp.int32, c.shape, 1)
    up = jnp.where(row == 0, 0.0, pltpu.roll(c, 1, 0))
    down = jnp.where(row == rows - 1, 0.0, pltpu.roll(c, rows - 1, 0))
    left = jnp.where(col == 0, 0.0, pltpu.roll(c, 1, 1))
    right = jnp.where(col == cols - 1, 0.0, pltpu.roll(c, cols - 1, 1))
    return (up + down) + (left + right)


def fold(values):
    rows, cols = values.shape
    return jnp.sum(values.reshape(rows // 8, 8, cols), axis=0)


def own_lanes(values):
    row = lax.broadcasted_iota(jnp.int32, values.shape, 0)
    lane = lax.broadcasted_iota(jnp.int32, values.shape, 1)
    each = values.shape[1] // values.shape[0]
    return jnp.where((lane >= row * each) & (lane < (row + 1) * each), values, 0.0)


def pack(values):
    lanes = values.shape[1]
    for distance in (lanes // 2, lanes // 4, lanes // 8):
        values = values + pltpu.roll(values, distance, 1)
    return jnp.sum(own_lanes(values), axis=0, keepdims=True)


def unpack(packed):
    spread = own_lanes(jnp.broadcast_to(packed, (8, packed.shape[1])))
    total = jnp.broadcast_to(jnp.sum(spread, axis=1, keepdims=True), spread.shape)
    return [total[k : k + 1, :] for k in range(8)]


def coefficients(packed):
    s = unpack(packed)
    nu = [s[0], s[1], 2.0 * s[2] - s[0], 2.0 * s[3] - s[1], 2.0 * s[4] - s[0], 2.0 * s[5] - s[1], 2.0 * s[6] - s[0]]
    nu.append(4.0 * s[7] - 2.0 * s[5] - s[1])
    shift = 2.0 * CENTRE / RADIUS
    u = [shift * nu[k] + nu[k + 1] + nu[abs(k - 1)] for k in range(7)]
    mat = [[u[i + j] + u[abs(i - j)] for j in range(BASIS)] for i in range(BASIS)]
    diag = [mat[i][i] for i in range(BASIS)]
    inverse, factors = [], {}
    for k in range(BASIS):
        good = mat[k][k] > 1e-8 * diag[k]
        inv = jnp.where(good, 1.0 / jnp.where(good, mat[k][k], 1.0), 0.0)
        inverse.append(inv)
        for i in range(k + 1, BASIS):
            factor = mat[k][i] * inv
            for j in range(i, BASIS):
                mat[i][j] = mat[i][j] - factor * mat[k][j]
            factors[i, k] = factor

    def solve(right):
        rhs = [(4.0 / RADIUS) * value for value in right]
        for k in range(BASIS):
            for i in range(k + 1, BASIS):
                rhs[i] = rhs[i] - factors[i, k] * rhs[k]
        out = [None] * BASIS
        for i in reversed(range(BASIS)):
            value = rhs[i]
            for j in range(i + 1, BASIS):
                value = value - mat[i][j] * out[j]
            out[i] = value * inverse[i]
        return out

    return solve(nu[:BASIS]), solve


def relays(n_sec, ingots):
    if (n_sec, ingots) != (16, 4):
        return []
    return [(2, 6), (3, 6)]


def ahead_of(ingots, lead):
    return dict([(0, list(range(ingots))), (1, list(range(ingots // 2, ingots)))][:lead])


def kernel(
    n_sec,
    n_slab,
    part_hbm,
    line_hbm,
    flag_hbm,
    instant_ref,
    heat_ref,
    factor_ref,
    dual_ref,
    both_ref,
    part_ref,
    line_ref,
    flag_ref,
    heat,
    coef,
    dual,
    a1,
    a2,
    a3,
    keep,
    mu3,
    mu2,
    mu1,
    w4,
    w3,
    w2,
    w1,
    pick,
    pick_t,
    offered,
    slots,
    back,
    basis_rows,
    relay,
    got,
    weights,
    weights_in,
    returned,
    sums_ref,
    packed_ref,
    gather,
    local_sem,
    halo_send,
    halo_recv,
    row_send,
    row_recv,
    side_send,
    side_recv,
    sum_send,
    sum_recv,
    ready,
    known,
    relay_send,
    relay_recv,
    ahead_send,
    ahead_recv,
    weight_recv,
):
    ingots, contact = part_hbm.shape
    melts = n_sec - ingots
    lead = melts // 3
    early = 2 * lead
    depth, height, width = heat_ref.shape
    first, last = depth, 2 * depth
    sec, slab = lax.axis_index("sec"), lax.axis_index("slab")
    is_melt = sec < melts
    is_early = sec < early
    is_lead = sec < lead
    relayed = relays(n_sec, ingots)
    targets = sorted({m for _, m in relayed})
    ahead = ahead_of(ingots, lead)

    def any_of(value, choices):
        return functools.reduce(jnp.logical_or, [value == choice for choice in choices])

    def only(value, choices, count, action):
        if len(choices) == count:
            action()
        elif choices:
            pl.when(any_of(value, choices))(action)

    has_left, has_right = slab > 0, slab < n_slab - 1
    state_ref, adjoint_ref = both_ref.at[0], both_ref.at[1]

    loads = [
        pltpu.make_async_copy(src, dst.at[pl.ds(first, depth)], local_sem.at[i])
        for i, (src, dst) in enumerate(((heat_ref, heat), (factor_ref, coef), (dual_ref, dual)))
    ]
    tables = [
        pltpu.make_async_copy(src, dst, local_sem.at[3 + i])
        for i, (src, dst) in enumerate(((part_hbm, part_ref), (line_hbm, line_ref), (flag_hbm, flag_ref)))
    ]
    barrier = pltpu.get_barrier_semaphore()

    def greet(to_sec, to_slab, sem=barrier):
        pl.semaphore_signal(sem, inc=1, device_id=(to_sec, to_slab), device_id_type=MESH)

    def along(offset):
        return lax.rem(slab + offset % n_slab, n_slab)

    sizes = (4, 4, 2) if n_slab == 32 else (n_slab,)
    partners = []
    for flat in range(1, n_slab):
        shift, rest = [], flat
        for size in reversed(sizes):
            shift.insert(0, rest % size)
            rest //= size
        partners.append((sum(min(step, size - step) for step, size in zip(shift, sizes)), tuple(shift)))
    partners.sort(key=lambda entry: (-entry[0], entry[1]))

    digits, rest = [], slab
    for size in reversed(sizes):
        digits.insert(0, lax.rem(rest, size))
        rest = lax.div(rest, size)
    strides = [math.prod(sizes[place + 1 :]) for place in range(len(sizes))]
    moved = [
        [lax.rem(digit + step, size) * stride for step in range(size)]
        for digit, size, stride in zip(digits, sizes, strides)
    ]

    def partner(shift):
        return sum(moved[place][step] for place, step in enumerate(shift))

    near = sorted({offset % n_slab for offset in range(-CLOSE, CLOSE + 1)} - {0})

    @pl.when(is_melt)
    def _():
        pl.when(has_left)(lambda: greet(sec, slab - 1))
        pl.when(has_right)(lambda: greet(sec, slab + 1))

        @pl.when(is_lead)
        def _():
            for j in range(ingots):
                greet(melts + j, slab)

        @pl.when(is_early & jnp.logical_not(is_lead))
        def _():
            greet(sec - lead, slab)

        for m in targets:
            pl.when(sec == m)(lambda: greet(early, slab))

    @pl.when(jnp.logical_not(is_melt))
    def _():
        for offset in near:
            greet(sec, along(offset))
        for m in range(early, melts):
            greet(m, slab)

    beside = has_left.astype(jnp.int32) + has_right.astype(jnp.int32)
    heard = jnp.where(is_melt, beside + jnp.where(is_lead, 1, jnp.where(is_early, 0, ingots)), len(near) + lead)
    heard = heard + jnp.where(sec == early, len(targets), 0) if targets else heard
    for load in tables + loads:
        load.start()
    pl.semaphore_wait(barrier, heard)

    def halo(index, src, dst, to_left, to_right):
        (left_src, left_dst), (right_src, right_dst) = to_left, to_right
        send, recv = halo_send.at[index], halo_recv.at[index]
        return (
            pltpu.make_async_remote_copy(
                src_ref=src.at[left_src], dst_ref=dst.at[left_dst], send_sem=send.at[0], recv_sem=recv.at[1],
                device_id=(sec, slab - 1), device_id_type=MESH,
            ),
            pltpu.make_async_remote_copy(
                src_ref=src.at[right_src], dst_ref=dst.at[right_dst], send_sem=send.at[1], recv_sem=recv.at[0],
                device_id=(sec, slab + 1), device_id_type=MESH,
            ),
        )

    def start(pair):
        pl.when(has_left)(lambda: pair[0].start())
        pl.when(has_right)(lambda: pair[1].start())

    def wait_recv(pair):
        pl.when(has_right)(lambda: pair[0].wait_recv())
        pl.when(has_left)(lambda: pair[1].wait_recv())

    def wait_send(pair):
        pl.when(has_left)(lambda: pair[0].wait_send())
        pl.when(has_right)(lambda: pair[1].wait_send())

    def lower(planes, offset=0):
        return pl.ds(offset, planes), pl.ds(last + offset, planes)

    def upper(planes, offset=0):
        at = depth - planes - offset
        return pl.ds(at, planes), pl.ds(at, planes)

    def pass_on(buf, rows, index):
        here = buf.at[pl.ds(first, depth), rows]
        pair = []
        for side, there, to in ((0, last, slab - 1), (1, 0, slab + 1)):
            pair.append(
                pltpu.make_async_remote_copy(
                    src_ref=here, dst_ref=buf.at[pl.ds(there, depth), rows], send_sem=side_send.at[side, index],
                    recv_sem=side_recv.at[1 - side], device_id=(sec, to), device_id_type=MESH,
                )
            )
        start(pair)
        return pair

    def take(buf, side):
        region = buf.at[pl.ds(2 * depth * side, depth)]
        pltpu.make_async_copy(region, region, side_recv.at[side]).wait()

    zero = jnp.zeros((height, width), jnp.float32)

    def clear(*bufs):
        @pl.when(jnp.logical_not(has_left))
        def _():
            for buf in bufs:
                buf[first - 1] = zero

        @pl.when(jnp.logical_not(has_right))
        def _():
            for buf in bufs:
                buf[last] = zero

    row_i = lax.broadcasted_iota(jnp.int32, (contact, contact), 0)
    lane_i = lax.broadcasted_iota(jnp.int32, (contact, contact), 1)

    def column(row):
        return jnp.sum(jnp.where(row_i == lane_i, row, 0.0), axis=1, keepdims=True)

    def slot_rows(index):
        return pl.ds(index * PAIRCAP, PAIRCAP)

    @pl.when(is_melt)
    def _():
        heat_halo = halo(0, heat_ref, heat, lower(depth), upper(depth))
        coef_halo = halo(1, factor_ref, coef, lower(depth - 1), upper(depth - 1))
        edge_halo = halo(2, factor_ref, coef, lower(1, depth - 1), upper(1, depth - 1))
        dual_halo = halo(3, dual_ref, dual, lower(depth), upper(depth))
        start(heat_halo)
        start(coef_halo)

        @pl.when(jnp.logical_not(is_early))
        def _():
            for j in range(ingots):
                greet(melts + j, slab, ready)

        clear(heat, dual, w4)
        for load in tables:
            load.wait()

        for j in range(ingots):
            named = part_ref[j : j + 1, :].astype(jnp.float32) == sec.astype(jnp.float32)
            lines = line_ref[j : j + 1, :].astype(jnp.float32)
            before = column(jnp.where(named, 1.0, 0.0))
            rank = jnp.sum(jnp.where(row_i < lane_i, before, 0.0), axis=0, keepdims=True)
            slot = lax.broadcasted_iota(jnp.int32, (PAIRCAP, contact), 0).astype(jnp.float32)
            chosen = jnp.where(named, 1.0, 0.0) * jnp.where(rank == slot, 1.0, 0.0)
            slot_line = jnp.sum(chosen * lines, axis=1, keepdims=True)
            live = jnp.sum(chosen, axis=1, keepdims=True)
            q = lax.broadcasted_iota(jnp.int32, (PAIRCAP, height), 1).astype(jnp.float32)
            pick[slot_rows(j), :] = jnp.where(q == slot_line, live, 0.0)
        eye = jnp.where(
            lax.broadcasted_iota(jnp.int32, (height, height), 0) == lax.broadcasted_iota(jnp.int32, (height, height), 1),
            1.0, 0.0,
        )
        pick_t[...] = lax.dot_general(
            eye, pick[...], (((1,), (1,)), ((), ())), precision=HIGHEST, preferred_element_type=jnp.float32
        )

        archived = instant_ref[0].astype(jnp.float32)
        speeds = []
        for k in range(STEPS):
            phase = jnp.full((1, width), archived + k)
            speeds.append(1.0 + 0.5 * jnp.sin(2.0 * math.pi * phase / period_steps))

        for load in loads:
            load.wait()
        wait_recv(heat_halo)
        wait_recv(coef_halo)
        start(edge_halo)
        start(dual_halo)

        states = (heat, a1, a2, a3, state_ref)
        for k in range(STEPS):
            src, dst = states[k], states[k + 1]
            final = k == STEPS - 1
            shift = first if final else 0

            def forward(z, carry, k=k, src=src, dst=dst, shift=shift):
                c = src[z]
                below = src[z - 1]
                total = (below + src[z + 1]) + in_plane(c)
                change = coef[z] * (total - 6.0 * c) - speeds[k] * (c - below)
                bent = jnp.tanh(c)
                dst[z - shift] = c + time_step * change - time_step * sink_rate * bent
                keep[k, z] = 1.0 - time_step * sink_rate * (1.0 - bent * bent)
                return carry

            lax.fori_loop(1 + k, 3 * depth - 1 - k, forward, 0, unroll=2)
            if not final:
                clear(dst)

        for z in range(depth):
            offered[z] = jnp.dot(pick[...], state_ref[z], precision=HIGHEST, preferred_element_type=jnp.float32)
        @pl.when(is_lead)
        def _():
            pl.semaphore_wait(ready, ingots)
            greet(sec + lead, slab, ready)
            for j in range(ingots):
                greet(melts + j, slab, ready)

        @pl.when(is_early & jnp.logical_not(is_lead))
        def _():
            pl.semaphore_wait(ready, 1)

        sends = []
        for j in range(ingots):
            send = pltpu.make_async_remote_copy(
                src_ref=offered.at[:, slot_rows(j), :],
                dst_ref=slots.at[pl.ds(first, depth), pl.ds(pl.multiple_of(sec * PAIRCAP, PAIRCAP), PAIRCAP), :],
                send_sem=row_send.at[j], recv_sem=row_recv.at[sec], device_id=(melts + j, slab), device_id_type=MESH,
            )
            send.start()
            sends.append(send)
        keep3 = keep.at[3]
        keep_halo = halo(
            4, keep3, keep3, (pl.ds(first, depth - 1), pl.ds(last, depth - 1)), (pl.ds(first + 1, depth - 1), pl.ds(1, depth - 1))
        )
        start(keep_halo)

        for z in (first - 2, last + 1):
            bent = jnp.tanh(a2[z])
            keep[2, z] = 1.0 - time_step * sink_rate * (1.0 - bent * bent)
        wait_recv(edge_halo)
        wait_recv(dual_halo)
        wait_recv(keep_halo)

        def relay_on(index):
            j, m = relayed[index]
            return pltpu.make_async_remote_copy(
                src_ref=relay.at[index], dst_ref=returned.at[pl.ds(first, depth), slot_rows(j), :],
                send_sem=relay_send.at[index], recv_sem=row_recv.at[j], device_id=(m, slab), device_id_type=MESH,
            )

        if relayed:

            @pl.when(sec == early)
            def _():
                for index in range(len(relayed)):
                    pltpu.make_async_copy(relay.at[index], relay.at[index], relay_recv.at[index]).wait()
                    relay_on(index).start()

        passed = []
        for j in reversed(range(ingots)):
            rows = slot_rows(j)

            def arrive(j=j, rows=rows):
                region = returned.at[pl.ds(first, depth), rows]
                pltpu.make_async_copy(region, region, row_recv.at[j]).wait()

            def add_up(j=j, rows=rows):
                region = got.at[:, :, rows]
                pltpu.make_async_copy(region, region, ahead_recv.at[j]).wait()
                pltpu.make_async_copy(weights_in.at[j], weights_in.at[j], weight_recv.at[j]).wait()
                c = [weights_in[j, i : i + 1, :] for i in range(BASIS)]
                for z in range(depth):
                    returned[first + z, rows, :] = (c[0] * got[0, z, rows, :] + c[1] * got[1, z, rows, :]) + (
                        c[2] * got[2, z, rows, :] + c[3] * got[3, z, rows, :]
                    )

            summed = [m for m in ahead if j in ahead[m]]
            if summed:
                pl.when(any_of(sec, summed))(add_up)
                pl.when(jnp.logical_not(any_of(sec, summed)))(arrive)
            else:
                arrive()
            passed.append(pass_on(returned, rows, j))

        def add_returned(at):
            for z in range(at, at + depth):
                rows = jnp.dot(pick_t[...], returned[z], precision=HIGHEST, preferred_element_type=jnp.float32)
                value = dual[z] + rows
                dual[z] = value
                w4[z] = coef[z] * value

        add_returned(first)

        mus, ws = (adjoint_ref, mu1, mu2, mu3, dual), (None, w1, w2, w3, w4)

        def backward(k, lo, hi):
            src, dst, wsrc, wdst = mus[k + 1], mus[k], ws[k + 1], ws[k]
            shift = first if k == 0 else 0

            def plane(z, carry):
                c, w = src[z], wsrc[z]
                total = (wsrc[z - 1] + wsrc[z + 1]) + in_plane(w)
                change = total - 6.0 * w - speeds[k] * (c - src[z + 1])
                value = keep[k, z] * c + time_step * change
                dst[z - shift] = value
                if wdst is not None:
                    wdst[z] = coef[z] * value
                return carry

            lax.fori_loop(lo, hi, plane, 0, unroll=hi - lo if hi - lo == 4 else 2)
            if wdst is not None:
                clear(dst, wdst)

        right_first = (slab % 2 == 0) | ((sec == 0) & (slab == 1) & has_right)

        @pl.when(right_first)
        def _():
            take(returned, 1)
            add_returned(last)
            for k in (3, 2, 1):
                backward(k, first + STEPS - k, last + k)

            @pl.when(has_left)
            def _():
                take(returned, 0)
                add_returned(0)

            for k in (3, 2, 1, 0):
                backward(k, first - k, first + STEPS - k)

        @pl.when(jnp.logical_not(right_first))
        def _():
            take(returned, 0)
            add_returned(0)
            for k in (3, 2, 1):
                backward(k, first - k, last - STEPS + k)

            @pl.when(has_right)
            def _():
                take(returned, 1)
                add_returned(last)

            for k in (3, 2, 1, 0):
                backward(k, last - STEPS + k, last + k)

        if relayed:

            @pl.when(sec == early)
            def _():
                for index in range(len(relayed)):
                    relay_on(index).wait_send()

        for pair in [heat_halo, coef_halo, edge_halo, dual_halo, keep_halo] + passed:
            wait_send(pair)
        for send in sends:
            send.wait_send()

    @pl.when(jnp.logical_not(is_melt))
    def _():
        dual_near = halo(3, dual_ref, dual, lower(2), upper(2))
        coef_near = halo(1, factor_ref, coef, lower(1), upper(1))
        dual_far = halo(4, dual_ref, dual, lower(depth - 2, 2), upper(depth - 2, 2))
        coef_far = halo(2, factor_ref, coef, lower(depth - 2, 1), upper(depth - 2, 1))
        heat_halo = halo(0, heat_ref, heat, lower(depth), upper(depth))
        start(dual_near)
        start(coef_near)
        start(coef_far)
        start(dual_far)
        for m in range(lead):
            greet(m, slab, ready)
        rounds = []
        reach = CLOSE
        while reach < n_slab // 2:
            rounds.append(reach)
            reach *= 2

        def tell(index):
            for offset in (-rounds[index], rounds[index]):
                greet(sec, along(offset), known.at[index])

        if rounds:
            tell(0)
        clear(heat, dual)

        for load in tables:
            load.wait()
        mine = sec - melts
        names = part_ref[pl.ds(mine, 1), :].astype(jnp.float32)
        flags = flag_ref[pl.ds(mine, 1), :].astype(jnp.float32)
        names_col, flags_col = column(names), column(flags)
        same = jnp.where(names_col == names, 1.0, 0.0)
        rank_col = jnp.sum(jnp.where(lane_i < row_i, same, 0.0), axis=1, keepdims=True)
        rank_row = jnp.sum(jnp.where(row_i < lane_i, same, 0.0), axis=0, keepdims=True)
        count = melts * PAIRCAP
        slot_lane = lax.broadcasted_iota(jnp.int32, (contact, count), 1).astype(jnp.float32)
        slot_row = lax.broadcasted_iota(jnp.int32, (count, contact), 0).astype(jnp.float32)
        place = jnp.where(slot_lane == names_col * PAIRCAP + rank_col, flags_col, 0.0)
        give = jnp.where(slot_row == names * PAIRCAP + rank_row, flags, 0.0)

        for load in loads:
            load.wait()
        told = [0]

        def hear(count):
            while told[0] < min(count, len(rounds)):
                pl.semaphore_wait(known.at[told[0]], 2)
                told[0] += 1
                if told[0] < len(rounds):
                    tell(told[0])

        early_sends = []

        def pick_basis(i):
            t = (dual, a1, a2, a3)[i]
            for z in range(depth):
                basis_rows[i, z] = jnp.dot(
                    give, t[first + z, :contact, :], precision=HIGHEST, preferred_element_type=jnp.float32
                )
            for place_m, m in enumerate(ahead):
                send = pltpu.make_async_remote_copy(
                    src_ref=basis_rows.at[i, :, slot_rows(m), :],
                    dst_ref=got.at[i, :, pl.ds(pl.multiple_of(mine * PAIRCAP, PAIRCAP), PAIRCAP), :],
                    send_sem=ahead_send.at[place_m, i], recv_sem=ahead_recv.at[mine], device_id=(m, slab), device_id_type=MESH,
                )
                only(mine, ahead[m], ingots, send.start)
                early_sends.append((m, send))

        def solve(which, t0, out, arrive_near, arrive_far, meanwhile, then):
            ts = (t0, a1, a2, a3)

            def grow(k, z):
                t = ts[k - 1]
                c = t[z]
                value = (coef[z] - (CENTRE - 6.0)) * c - ((t[z - 1] + t[z + 1]) + in_plane(c))
                if k == 1:
                    ts[k][z] = value * (1.0 / RADIUS)
                else:
                    ts[k][z] = value * (2.0 / RADIUS) - ts[k - 2][z]

            def grow_all(k, lo, hi):
                lax.fori_loop(lo, hi, lambda z, carry: grow(k, z) or carry, 0, unroll=hi - lo if hi - lo == 4 else 2)

            def add_up(terms, count):
                def plane(z, sums):
                    return tuple(s + fold(term) for s, term in zip(sums, terms(z)))

                sums = lax.fori_loop(first, last, plane, (jnp.zeros((8, width), jnp.float32),) * count, unroll=2)
                return [jnp.sum(total, axis=0, keepdims=True) for total in sums]

            def near_terms(z):
                x0, x1, x2 = (ref[z] for ref in ts[:3])
                return x0 * x0, x0 * x1, x1 * x1, x1 * x2, x2 * x2

            def far_terms(z):
                x2, x3 = a2[z], a3[z]
                image = (coef[z] - (CENTRE - 6.0)) * x3 - 2.0 * a3[z + 1] - in_plane(x3)
                return x2 * x3, x3 * x3, x3 * image * (1.0 / RADIUS)

            arrive_near()
            grow_all(1, first - 1, last + 1)
            clear(a1)
            grow_all(2, first, last)
            sums = add_up(near_terms, 5)
            arrive_far()
            for z in (first - 3, first - 2, last + 1, last + 2):
                grow(1, z)
            for z in (first - 2, first - 1, last, last + 1):
                grow(2, z)
            clear(a2)
            grow_all(3, first, last)
            grow(3, first - 1)
            grow(3, last)
            clear(a3)
            sums += add_up(far_terms, 3)
            hear(len(rounds))

            def everywhere(slot, sums, meanwhile):
                for k in range(8):
                    sums_ref[pl.ds(k, 1), :] = sums[k]
                packed = pack(sums_ref[...])
                packed_ref[slot] = packed
                for index, (_, shift) in enumerate(partners):
                    pltpu.make_async_remote_copy(
                        src_ref=packed_ref.at[slot], dst_ref=gather.at[slot, pl.ds(index, 1)],
                        send_sem=sum_send.at[slot], recv_sem=sum_recv.at[slot],
                        device_id=(sec, partner(shift)), device_id_type=MESH,
                    ).start()
                meanwhile()
                others = gather.at[slot, pl.ds(0, n_slab - 1)]
                pltpu.make_async_copy(others, others, sum_recv.at[slot]).wait()
                return packed + jnp.sum(gather[slot, : n_slab - 1, :], axis=0, keepdims=True)

            c, again = coefficients(everywhere(2 * which, sums, meanwhile))

            def left_over(z):
                x0, x1, x2, x3 = (ref[z] for ref in ts)
                image = (coef[z] - (CENTRE - 6.0)) * x3 - ((a3[z - 1] + a3[z + 1]) + in_plane(x3))
                moved = c[0] * x1 + 0.5 * (c[1] * (x2 + x0) + c[2] * (x3 + x1)) + c[3] * (image * (1.0 / RADIUS))
                at = (c[0] * x0 + c[1] * x1) + (c[2] * x2 + c[3] * x3)
                residual = x0 - CENTRE * at - RADIUS * moved
                return x0 * residual, x1 * residual, x2 * residual, x3 * residual

            rest = add_up(left_over, 4)
            change = again(unpack(everywhere(2 * which + 1, rest + rest, lambda: None))[:BASIS])
            c = [value + more for value, more in zip(c, change)]
            then(c)

            def combine(z, carry):
                out[z - first] = (c[0] * ts[0][z] + c[1] * ts[1][z]) + (c[2] * ts[2][z] + c[3] * ts[3][z])
                return carry

            lax.fori_loop(first, last, combine, 0, unroll=2)

        def arrive_near():
            pick_basis(0)
            hear(1)
            wait_recv(dual_near)
            wait_recv(coef_near)

        def arrive_far():
            pick_basis(1)
            pick_basis(2)
            hear(2)
            wait_recv(coef_far)
            wait_recv(dual_far)
            start(heat_halo)

        sends = []

        def send_back(c):
            weights[...] = jnp.concatenate(c + c, axis=0)
            for m in ahead:
                send = pltpu.make_async_remote_copy(
                    src_ref=weights, dst_ref=weights_in.at[mine], send_sem=row_send.at[m], recv_sem=weight_recv.at[mine],
                    device_id=(m, slab), device_id_type=MESH,
                )
                only(mine, ahead[m], ingots, send.start)
            for z in range(depth):
                back[z] = (c[0] * basis_rows[0, z] + c[1] * basis_rows[1, z]) + (
                    c[2] * basis_rows[2, z] + c[3] * basis_rows[3, z]
                )
            pl.semaphore_wait(ready, melts - early + lead)
            for index, (j, m) in enumerate(relayed):

                @pl.when(mine == j)
                def _():
                    pltpu.make_async_remote_copy(
                        src_ref=back.at[:, slot_rows(m), :], dst_ref=relay.at[index], send_sem=row_send.at[m],
                        recv_sem=relay_recv.at[index], device_id=(early, slab), device_id_type=MESH,
                    ).start()

            for m in range(melts):
                direct = [j for j in range(ingots) if (j, m) not in relayed and j not in ahead.get(m, [])]
                send = pltpu.make_async_remote_copy(
                    src_ref=back.at[:, slot_rows(m), :],
                    dst_ref=returned.at[pl.ds(first, depth), pl.ds(pl.multiple_of(mine * PAIRCAP, PAIRCAP), PAIRCAP), :],
                    send_sem=row_send.at[m], recv_sem=row_recv.at[mine], device_id=(m, slab), device_id_type=MESH,
                )
                only(mine, direct, ingots, send.start)
                sends.append((m, send))

        solve(0, dual, adjoint_ref, arrive_near, arrive_far, lambda: pick_basis(3), send_back)

        passed = []
        for m in range(melts):
            region = slots.at[pl.ds(first, depth), slot_rows(m)]
            pltpu.make_async_copy(region, region, row_recv.at[m]).wait()
            passed.append(pass_on(slots, slot_rows(m), m))

        def load_up(at):
            for z in range(at, at + depth):
                rows = jnp.dot(place, slots[z], precision=HIGHEST, preferred_element_type=jnp.float32)
                heat[z, pl.ds(0, contact), :] = heat[z, pl.ds(0, contact), :] + rows

        wait_recv(heat_halo)
        load_up(first)

        @pl.when(has_left)
        def _():
            take(slots, 0)
            load_up(0)

        @pl.when(has_right)
        def _():
            take(slots, 1)
            load_up(last)

        solve(1, heat, state_ref, lambda: None, lambda: None, lambda: None, lambda c: None)

        for pair in [dual_near, coef_near, dual_far, coef_far, heat_halo] + passed:
            wait_send(pair)
        for m, send in early_sends:
            only(mine, ahead[m], ingots, send.wait_send)
        for m, send in sends:
            summed = ahead.get(m, [])
            only(mine, summed, ingots, lambda m=m: pltpu.make_async_copy(weights, weights, row_send.at[m]).wait())
            only(mine, [j for j in range(ingots) if j not in summed], ingots, send.wait_send)
        for which in range(4):
            others = gather.at[which, pl.ds(0, n_slab - 1)]
            pltpu.make_async_copy(others, others, sum_send.at[which]).wait()


def body(n_sec, n_slab, heat_level, material_factor, dual_sensitivity, part, line, flag, instant):
    ingots, contact = line.shape
    melts = n_sec - ingots
    _, depth, height, width = heat_level.shape
    f32 = jnp.float32
    wide = pltpu.VMEM((3 * depth, height, width), f32)
    table = pltpu.VMEM((ingots, contact), jnp.int32)
    dma = pltpu.SemaphoreType.DMA
    most = max(melts, ingots)
    scratch = [
        table, table, table,
        wide, wide, wide, wide, wide, wide,
        pltpu.VMEM((STEPS, 3 * depth, height, width), f32),
        wide, wide, wide, wide, wide, wide, wide,
        pltpu.VMEM((ingots * PAIRCAP, height), f32),
        pltpu.VMEM((height, ingots * PAIRCAP), f32),
        pltpu.VMEM((depth, ingots * PAIRCAP, width), f32),
        pltpu.VMEM((3 * depth, melts * PAIRCAP, width), f32),
        pltpu.VMEM((depth, melts * PAIRCAP, width), f32),
        pltpu.VMEM((BASIS, depth, melts * PAIRCAP, width), f32),
        pltpu.VMEM((max(len(relays(n_sec, ingots)), 1), depth, PAIRCAP, width), f32),
        pltpu.VMEM((BASIS, depth, ingots * PAIRCAP, width), f32),
        pltpu.VMEM((8, width), f32),
        pltpu.VMEM((ingots, 8, width), f32),
        pltpu.VMEM((3 * depth, ingots * PAIRCAP, width), f32),
        pltpu.VMEM((8, width), f32),
        pltpu.VMEM((4, 1, width), f32),
        pltpu.VMEM((4, n_slab, width), f32),
        dma((6,)), dma((5, 2)), dma((5, 2)),
        dma((most,)), dma((most,)), dma((2, most)), dma((2,)),
        dma((4,)), dma((4,)), pltpu.SemaphoreType.REGULAR, pltpu.SemaphoreType.REGULAR((4,)),
        dma((8,)), dma((8,)), dma((4, BASIS)), dma((ingots,)), dma((ingots,)),
    ]
    hbm, vmem, smem = (pl.BlockSpec(memory_space=s) for s in (pltpu.HBM, pltpu.VMEM, pltpu.SMEM))
    fields = (part[:, :, 0], line, flag, heat_level[0], material_factor[0], dual_sensitivity[0])
    fields = [pltpu.with_memory_space_constraint(field, pltpu.HBM) for field in fields]
    both = pl.pallas_call(
        functools.partial(kernel, n_sec, n_slab),
        out_shape=jax.ShapeDtypeStruct((2, depth, height, width), f32),
        in_specs=[hbm, hbm, hbm, smem, hbm, hbm, hbm],
        out_specs=vmem,
        scratch_shapes=scratch,
        compiler_params=pltpu.CompilerParams(
            collective_id=0, has_side_effects=True, vmem_limit_bytes=32 * 1024 * 1024
        ),
    )(*fields[:3], instant, *fields[3:])
    return both[0:1], both[1:2]


def solution(mesh):
    n_sec, n_slab = mesh.shape["sec"], mesh.shape["slab"]
    fields = P("sec", "slab", None, None)
    return jax.shard_map(
        functools.partial(body, n_sec, n_slab),
        mesh=mesh,
        in_specs=(fields, fields, fields, P(), P(), P(), P()),
        out_specs=(fields, fields),
        check_vma=False,
    )
```

```python
import functools
import math

import jax
import jax.numpy as jnp
from jax import lax
from jax.experimental import pallas as pl
from jax.experimental.pallas import tpu as pltpu
from jax.sharding import PartitionSpec as P

STEPS = 4
PAIRCAP = 8
BASIS = 4
CLOSE = 4

time_step = 0.1
sink_rate = 0.5
period_steps = 16.0

CENTRE = 6.8
RADIUS = 6.4

MESH = pl.DeviceIdType.MESH
HIGHEST = lax.Precision.HIGHEST


def in_plane(c):
    rows, cols = c.shape
    row = lax.broadcasted_iota(jnp.int32, c.shape, 0)
    col = lax.broadcasted_iota(jnp.int32, c.shape, 1)
    up = jnp.where(row == 0, 0.0, pltpu.roll(c, 1, 0))
    down = jnp.where(row == rows - 1, 0.0, pltpu.roll(c, rows - 1, 0))
    left = jnp.where(col == 0, 0.0, pltpu.roll(c, 1, 1))
    right = jnp.where(col == cols - 1, 0.0, pltpu.roll(c, cols - 1, 1))
    return (up + down) + (left + right)


def fold(values):
    rows, cols = values.shape
    return jnp.sum(values.reshape(rows // 8, 8, cols), axis=0)


def own_lanes(values):
    row = lax.broadcasted_iota(jnp.int32, values.shape, 0)
    lane = lax.broadcasted_iota(jnp.int32, values.shape, 1)
    each = values.shape[1] // values.shape[0]
    return jnp.where((lane >= row * each) & (lane < (row + 1) * each), values, 0.0)


def pack(values):
    lanes = values.shape[1]
    for distance in (lanes // 2, lanes // 4, lanes // 8):
        values = values + pltpu.roll(values, distance, 1)
    return jnp.sum(own_lanes(values), axis=0, keepdims=True)


def unpack(packed):
    spread = own_lanes(jnp.broadcast_to(packed, (8, packed.shape[1])))
    total = jnp.broadcast_to(jnp.sum(spread, axis=1, keepdims=True), spread.shape)
    return [total[k : k + 1, :] for k in range(8)]


def coefficients(packed):
    s = unpack(packed)
    nu = [s[0], s[1], 2.0 * s[2] - s[0], 2.0 * s[3] - s[1], 2.0 * s[4] - s[0], 2.0 * s[5] - s[1], 2.0 * s[6] - s[0]]
    nu.append(4.0 * s[7] - 2.0 * s[5] - s[1])
    shift = 2.0 * CENTRE / RADIUS
    u = [shift * nu[k] + nu[k + 1] + nu[abs(k - 1)] for k in range(7)]
    mat = [[u[i + j] + u[abs(i - j)] for j in range(BASIS)] for i in range(BASIS)]
    diag = [mat[i][i] for i in range(BASIS)]
    inverse, factors = [], {}
    for k in range(BASIS):
        good = mat[k][k] > 1e-8 * diag[k]
        inv = jnp.where(good, 1.0 / jnp.where(good, mat[k][k], 1.0), 0.0)
        inverse.append(inv)
        for i in range(k + 1, BASIS):
            factor = mat[k][i] * inv
            for j in range(i, BASIS):
                mat[i][j] = mat[i][j] - factor * mat[k][j]
            factors[i, k] = factor

    def solve(right):
        rhs = [(4.0 / RADIUS) * value for value in right]
        for k in range(BASIS):
            for i in range(k + 1, BASIS):
                rhs[i] = rhs[i] - factors[i, k] * rhs[k]
        out = [None] * BASIS
        for i in reversed(range(BASIS)):
            value = rhs[i]
            for j in range(i + 1, BASIS):
                value = value - mat[i][j] * out[j]
            out[i] = value * inverse[i]
        return out

    return solve(nu[:BASIS]), solve


def relays(n_sec, ingots):
    if (n_sec, ingots) != (16, 4):
        return []
    return [(2, 6), (3, 6)]


def ahead_of(ingots, lead):
    return {m: list(range(ingots)) for m in range(min(3, lead))}


def kernel(
    n_sec,
    n_slab,
    part_hbm,
    line_hbm,
    flag_hbm,
    instant_ref,
    heat_ref,
    factor_ref,
    dual_ref,
    both_ref,
    part_ref,
    line_ref,
    flag_ref,
    heat,
    coef,
    dual,
    a1,
    a2,
    a3,
    keep,
    mu3,
    mu2,
    mu1,
    w4,
    w3,
    w2,
    w1,
    pick,
    pick_t,
    offered,
    slots,
    back,
    basis_rows,
    relay,
    got,
    weights,
    weights_in,
    returned,
    sums_ref,
    packed_ref,
    gather,
    local_sem,
    halo_send,
    halo_recv,
    row_send,
    row_recv,
    side_send,
    side_recv,
    sum_send,
    sum_recv,
    ready,
    known,
    relay_send,
    relay_recv,
    ahead_send,
    ahead_recv,
    weight_recv,
):
    ingots, contact = part_hbm.shape
    melts = n_sec - ingots
    lead = melts // 3
    early = 2 * lead
    depth, height, width = heat_ref.shape
    first, last = depth, 2 * depth
    sec, slab = lax.axis_index("sec"), lax.axis_index("slab")
    is_melt = sec < melts
    is_early = sec < early
    is_lead = sec < lead
    relayed = relays(n_sec, ingots)
    targets = sorted({m for _, m in relayed})
    ahead = ahead_of(ingots, lead)

    def any_of(value, choices):
        return functools.reduce(jnp.logical_or, [value == choice for choice in choices])

    def only(value, choices, count, action):
        if len(choices) == count:
            action()
        elif choices:
            pl.when(any_of(value, choices))(action)

    has_left, has_right = slab > 0, slab < n_slab - 1
    state_ref, adjoint_ref = both_ref.at[0], both_ref.at[1]

    loads = [
        pltpu.make_async_copy(src, dst.at[pl.ds(first, depth)], local_sem.at[i])
        for i, (src, dst) in enumerate(((heat_ref, heat), (factor_ref, coef), (dual_ref, dual)))
    ]
    tables = [
        pltpu.make_async_copy(src, dst, local_sem.at[3 + i])
        for i, (src, dst) in enumerate(((part_hbm, part_ref), (line_hbm, line_ref), (flag_hbm, flag_ref)))
    ]
    barrier = pltpu.get_barrier_semaphore()

    def greet(to_sec, to_slab, sem=barrier):
        pl.semaphore_signal(sem, inc=1, device_id=(to_sec, to_slab), device_id_type=MESH)

    def along(offset):
        return lax.rem(slab + offset % n_slab, n_slab)

    sizes = (4, 4, 2) if n_slab == 32 else (n_slab,)
    partners = []
    for flat in range(1, n_slab):
        shift, rest = [], flat
        for size in reversed(sizes):
            shift.insert(0, rest % size)
            rest //= size
        partners.append((sum(min(step, size - step) for step, size in zip(shift, sizes)), tuple(shift)))
    partners.sort(key=lambda entry: (-entry[0], entry[1]))

    digits, rest = [], slab
    for size in reversed(sizes):
        digits.insert(0, lax.rem(rest, size))
        rest = lax.div(rest, size)
    strides = [math.prod(sizes[place + 1 :]) for place in range(len(sizes))]
    moved = [
        [lax.rem(digit + step, size) * stride for step in range(size)]
        for digit, size, stride in zip(digits, sizes, strides)
    ]

    def partner(shift):
        return sum(moved[place][step] for place, step in enumerate(shift))

    near = sorted({offset % n_slab for offset in range(-CLOSE, CLOSE + 1)} - {0})

    @pl.when(is_melt)
    def _():
        pl.when(has_left)(lambda: greet(sec, slab - 1))
        pl.when(has_right)(lambda: greet(sec, slab + 1))

        @pl.when(is_lead)
        def _():
            for j in range(ingots):
                greet(melts + j, slab)

        @pl.when(is_early & jnp.logical_not(is_lead))
        def _():
            greet(sec - lead, slab)

        for m in targets:
            pl.when(sec == m)(lambda: greet(early, slab))

    @pl.when(jnp.logical_not(is_melt))
    def _():
        for offset in near:
            greet(sec, along(offset))
        for m in range(early, melts):
            greet(m, slab)

    beside = has_left.astype(jnp.int32) + has_right.astype(jnp.int32)
    heard = jnp.where(is_melt, beside + jnp.where(is_lead, 1, jnp.where(is_early, 0, ingots)), len(near) + lead)
    heard = heard + jnp.where(sec == early, len(targets), 0) if targets else heard
    for load in tables + loads:
        load.start()
    pl.semaphore_wait(barrier, heard)

    def halo(index, src, dst, to_left, to_right):
        (left_src, left_dst), (right_src, right_dst) = to_left, to_right
        send, recv = halo_send.at[index], halo_recv.at[index]
        return (
            pltpu.make_async_remote_copy(
                src_ref=src.at[left_src], dst_ref=dst.at[left_dst], send_sem=send.at[0], recv_sem=recv.at[1],
                device_id=(sec, slab - 1), device_id_type=MESH,
            ),
            pltpu.make_async_remote_copy(
                src_ref=src.at[right_src], dst_ref=dst.at[right_dst], send_sem=send.at[1], recv_sem=recv.at[0],
                device_id=(sec, slab + 1), device_id_type=MESH,
            ),
        )

    def start(pair):
        pl.when(has_left)(lambda: pair[0].start())
        pl.when(has_right)(lambda: pair[1].start())

    def wait_recv(pair):
        pl.when(has_right)(lambda: pair[0].wait_recv())
        pl.when(has_left)(lambda: pair[1].wait_recv())

    def wait_send(pair):
        pl.when(has_left)(lambda: pair[0].wait_send())
        pl.when(has_right)(lambda: pair[1].wait_send())

    def lower(planes, offset=0):
        return pl.ds(offset, planes), pl.ds(last + offset, planes)

    def upper(planes, offset=0):
        at = depth - planes - offset
        return pl.ds(at, planes), pl.ds(at, planes)

    def pass_on(buf, rows, index):
        here = buf.at[pl.ds(first, depth), rows]
        pair = []
        for side, there, to in ((0, last, slab - 1), (1, 0, slab + 1)):
            pair.append(
                pltpu.make_async_remote_copy(
                    src_ref=here, dst_ref=buf.at[pl.ds(there, depth), rows], send_sem=side_send.at[side, index],
                    recv_sem=side_recv.at[1 - side], device_id=(sec, to), device_id_type=MESH,
                )
            )
        start(pair)
        return pair

    def take(buf, side):
        region = buf.at[pl.ds(2 * depth * side, depth)]
        pltpu.make_async_copy(region, region, side_recv.at[side]).wait()

    zero = jnp.zeros((height, width), jnp.float32)

    def clear(*bufs):
        @pl.when(jnp.logical_not(has_left))
        def _():
            for buf in bufs:
                buf[first - 1] = zero

        @pl.when(jnp.logical_not(has_right))
        def _():
            for buf in bufs:
                buf[last] = zero

    row_i = lax.broadcasted_iota(jnp.int32, (contact, contact), 0)
    lane_i = lax.broadcasted_iota(jnp.int32, (contact, contact), 1)

    def column(row):
        return jnp.sum(jnp.where(row_i == lane_i, row, 0.0), axis=1, keepdims=True)

    def slot_rows(index):
        return pl.ds(index * PAIRCAP, PAIRCAP)

    @pl.when(is_melt)
    def _():
        heat_halo = halo(0, heat_ref, heat, lower(depth), upper(depth))
        coef_halo = halo(1, factor_ref, coef, lower(depth - 1), upper(depth - 1))
        edge_halo = halo(2, factor_ref, coef, lower(1, depth - 1), upper(1, depth - 1))
        dual_halo = halo(3, dual_ref, dual, lower(depth), upper(depth))
        start(heat_halo)
        start(coef_halo)

        @pl.when(jnp.logical_not(is_early))
        def _():
            for j in range(ingots):
                greet(melts + j, slab, ready)

        clear(heat, dual, w4)
        for load in tables:
            load.wait()

        for j in range(ingots):
            named = part_ref[j : j + 1, :].astype(jnp.float32) == sec.astype(jnp.float32)
            lines = line_ref[j : j + 1, :].astype(jnp.float32)
            before = column(jnp.where(named, 1.0, 0.0))
            rank = jnp.sum(jnp.where(row_i < lane_i, before, 0.0), axis=0, keepdims=True)
            slot = lax.broadcasted_iota(jnp.int32, (PAIRCAP, contact), 0).astype(jnp.float32)
            chosen = jnp.where(named, 1.0, 0.0) * jnp.where(rank == slot, 1.0, 0.0)
            slot_line = jnp.sum(chosen * lines, axis=1, keepdims=True)
            live = jnp.sum(chosen, axis=1, keepdims=True)
            q = lax.broadcasted_iota(jnp.int32, (PAIRCAP, height), 1).astype(jnp.float32)
            pick[slot_rows(j), :] = jnp.where(q == slot_line, live, 0.0)
        eye = jnp.where(
            lax.broadcasted_iota(jnp.int32, (height, height), 0) == lax.broadcasted_iota(jnp.int32, (height, height), 1),
            1.0, 0.0,
        )
        pick_t[...] = lax.dot_general(
            eye, pick[...], (((1,), (1,)), ((), ())), precision=HIGHEST, preferred_element_type=jnp.float32
        )

        archived = instant_ref[0].astype(jnp.float32)
        speeds = []
        for k in range(STEPS):
            phase = jnp.full((1, width), archived + k)
            speeds.append(1.0 + 0.5 * jnp.sin(2.0 * math.pi * phase / period_steps))

        for load in loads:
            load.wait()
        wait_recv(heat_halo)
        wait_recv(coef_halo)
        start(edge_halo)
        start(dual_halo)

        states = (heat, a1, a2, a3, state_ref)
        for k in range(STEPS):
            src, dst = states[k], states[k + 1]
            final = k == STEPS - 1
            shift = first if final else 0

            def forward(z, carry, k=k, src=src, dst=dst, shift=shift):
                c = src[z]
                below = src[z - 1]
                total = (below + src[z + 1]) + in_plane(c)
                change = coef[z] * (total - 6.0 * c) - speeds[k] * (c - below)
                bent = jnp.tanh(c)
                dst[z - shift] = c + time_step * change - time_step * sink_rate * bent
                keep[k, z] = 1.0 - time_step * sink_rate * (1.0 - bent * bent)
                return carry

            lax.fori_loop(1 + k, 3 * depth - 1 - k, forward, 0, unroll=2)
            if not final:
                clear(dst)

        for z in range(depth):
            offered[z] = jnp.dot(pick[...], state_ref[z], precision=HIGHEST, preferred_element_type=jnp.float32)
        @pl.when(is_lead)
        def _():
            pl.semaphore_wait(ready, ingots)
            greet(sec + lead, slab, ready)
            for j in range(ingots):
                greet(melts + j, slab, ready)

        @pl.when(is_early & jnp.logical_not(is_lead))
        def _():
            pl.semaphore_wait(ready, 1)

        sends = []
        for j in range(ingots):
            send = pltpu.make_async_remote_copy(
                src_ref=offered.at[:, slot_rows(j), :],
                dst_ref=slots.at[pl.ds(first, depth), pl.ds(pl.multiple_of(sec * PAIRCAP, PAIRCAP), PAIRCAP), :],
                send_sem=row_send.at[j], recv_sem=row_recv.at[sec], device_id=(melts + j, slab), device_id_type=MESH,
            )
            send.start()
            sends.append(send)
        keep3 = keep.at[3]
        keep_halo = halo(
            4, keep3, keep3, (pl.ds(first, depth - 1), pl.ds(last, depth - 1)), (pl.ds(first + 1, depth - 1), pl.ds(1, depth - 1))
        )
        start(keep_halo)

        for z in (first - 2, last + 1):
            bent = jnp.tanh(a2[z])
            keep[2, z] = 1.0 - time_step * sink_rate * (1.0 - bent * bent)
        wait_recv(edge_halo)
        wait_recv(dual_halo)
        wait_recv(keep_halo)

        def relay_on(index):
            j, m = relayed[index]
            return pltpu.make_async_remote_copy(
                src_ref=relay.at[index], dst_ref=returned.at[pl.ds(first, depth), slot_rows(j), :],
                send_sem=relay_send.at[index], recv_sem=row_recv.at[j], device_id=(m, slab), device_id_type=MESH,
            )

        if relayed:

            @pl.when(sec == early)
            def _():
                for index in range(len(relayed)):
                    pltpu.make_async_copy(relay.at[index], relay.at[index], relay_recv.at[index]).wait()
                    relay_on(index).start()

        passed = []
        for j in reversed(range(ingots)):
            rows = slot_rows(j)

            def arrive(j=j, rows=rows):
                region = returned.at[pl.ds(first, depth), rows]
                pltpu.make_async_copy(region, region, row_recv.at[j]).wait()

            def add_up(j=j, rows=rows):
                region = got.at[:, :, rows]
                pltpu.make_async_copy(region, region, ahead_recv.at[j]).wait()
                pltpu.make_async_copy(weights_in.at[j], weights_in.at[j], weight_recv.at[j]).wait()
                c = [weights_in[j, i : i + 1, :] for i in range(BASIS)]
                for z in range(depth):
                    returned[first + z, rows, :] = (c[0] * got[0, z, rows, :] + c[1] * got[1, z, rows, :]) + (
                        c[2] * got[2, z, rows, :] + c[3] * got[3, z, rows, :]
                    )

            summed = [m for m in ahead if j in ahead[m]]
            if summed:
                pl.when(any_of(sec, summed))(add_up)
                pl.when(jnp.logical_not(any_of(sec, summed)))(arrive)
            else:
                arrive()
            passed.append(pass_on(returned, rows, j))

        def add_returned(at):
            for z in range(at, at + depth):
                rows = jnp.dot(pick_t[...], returned[z], precision=HIGHEST, preferred_element_type=jnp.float32)
                value = dual[z] + rows
                dual[z] = value
                w4[z] = coef[z] * value

        add_returned(first)

        mus, ws = (adjoint_ref, mu1, mu2, mu3, dual), (None, w1, w2, w3, w4)

        def backward(k, lo, hi):
            src, dst, wsrc, wdst = mus[k + 1], mus[k], ws[k + 1], ws[k]
            shift = first if k == 0 else 0

            def plane(z, carry):
                c, w = src[z], wsrc[z]
                total = (wsrc[z - 1] + wsrc[z + 1]) + in_plane(w)
                change = total - 6.0 * w - speeds[k] * (c - src[z + 1])
                value = keep[k, z] * c + time_step * change
                dst[z - shift] = value
                if wdst is not None:
                    wdst[z] = coef[z] * value
                return carry

            lax.fori_loop(lo, hi, plane, 0, unroll=hi - lo if hi - lo == 4 else 2)
            if wdst is not None:
                clear(dst, wdst)

        right_first = (slab % 2 == 0) | ((sec == 0) & (slab == 1) & has_right)

        @pl.when(right_first)
        def _():
            take(returned, 1)
            add_returned(last)
            for k in (3, 2, 1):
                backward(k, first + STEPS - k, last + k)

            @pl.when(has_left)
            def _():
                take(returned, 0)
                add_returned(0)

            for k in (3, 2, 1, 0):
                backward(k, first - k, first + STEPS - k)

        @pl.when(jnp.logical_not(right_first))
        def _():
            take(returned, 0)
            add_returned(0)
            for k in (3, 2, 1):
                backward(k, first - k, last - STEPS + k)

            @pl.when(has_right)
            def _():
                take(returned, 1)
                add_returned(last)

            for k in (3, 2, 1, 0):
                backward(k, last - STEPS + k, last + k)

        if relayed:

            @pl.when(sec == early)
            def _():
                for index in range(len(relayed)):
                    relay_on(index).wait_send()

        for pair in [heat_halo, coef_halo, edge_halo, dual_halo, keep_halo] + passed:
            wait_send(pair)
        for send in sends:
            send.wait_send()

    @pl.when(jnp.logical_not(is_melt))
    def _():
        dual_near = halo(3, dual_ref, dual, lower(2), upper(2))
        coef_near = halo(1, factor_ref, coef, lower(1), upper(1))
        dual_far = halo(4, dual_ref, dual, lower(depth - 2, 2), upper(depth - 2, 2))
        coef_far = halo(2, factor_ref, coef, lower(depth - 2, 1), upper(depth - 2, 1))
        heat_halo = halo(0, heat_ref, heat, lower(depth), upper(depth))
        start(dual_near)
        start(coef_near)
        start(coef_far)
        start(dual_far)
        for m in range(lead):
            greet(m, slab, ready)
        rounds = []
        reach = CLOSE
        while reach < n_slab // 2:
            rounds.append(reach)
            reach *= 2

        def tell(index):
            for offset in (-rounds[index], rounds[index]):
                greet(sec, along(offset), known.at[index])

        if rounds:
            tell(0)
        clear(heat, dual)

        for load in tables:
            load.wait()
        mine = sec - melts
        names = part_ref[pl.ds(mine, 1), :].astype(jnp.float32)
        flags = flag_ref[pl.ds(mine, 1), :].astype(jnp.float32)
        names_col, flags_col = column(names), column(flags)
        same = jnp.where(names_col == names, 1.0, 0.0)
        rank_col = jnp.sum(jnp.where(lane_i < row_i, same, 0.0), axis=1, keepdims=True)
        rank_row = jnp.sum(jnp.where(row_i < lane_i, same, 0.0), axis=0, keepdims=True)
        count = melts * PAIRCAP
        slot_lane = lax.broadcasted_iota(jnp.int32, (contact, count), 1).astype(jnp.float32)
        slot_row = lax.broadcasted_iota(jnp.int32, (count, contact), 0).astype(jnp.float32)
        place = jnp.where(slot_lane == names_col * PAIRCAP + rank_col, flags_col, 0.0)
        give = jnp.where(slot_row == names * PAIRCAP + rank_row, flags, 0.0)

        for load in loads:
            load.wait()
        told = [0]

        def hear(count):
            while told[0] < min(count, len(rounds)):
                pl.semaphore_wait(known.at[told[0]], 2)
                told[0] += 1
                if told[0] < len(rounds):
                    tell(told[0])

        early_sends = []

        def pick_basis(i):
            t = (dual, a1, a2, a3)[i]
            for z in range(depth):
                basis_rows[i, z] = jnp.dot(
                    give, t[first + z, :contact, :], precision=HIGHEST, preferred_element_type=jnp.float32
                )
            for place_m, m in enumerate(ahead):
                send = pltpu.make_async_remote_copy(
                    src_ref=basis_rows.at[i, :, slot_rows(m), :],
                    dst_ref=got.at[i, :, pl.ds(pl.multiple_of(mine * PAIRCAP, PAIRCAP), PAIRCAP), :],
                    send_sem=ahead_send.at[place_m, i], recv_sem=ahead_recv.at[mine], device_id=(m, slab), device_id_type=MESH,
                )
                only(mine, ahead[m], ingots, send.start)
                early_sends.append((m, send))

        def solve(which, t0, out, arrive_near, arrive_far, meanwhile, then):
            ts = (t0, a1, a2, a3)

            def grow(k, z):
                t = ts[k - 1]
                c = t[z]
                value = (coef[z] - (CENTRE - 6.0)) * c - ((t[z - 1] + t[z + 1]) + in_plane(c))
                if k == 1:
                    ts[k][z] = value * (1.0 / RADIUS)
                else:
                    ts[k][z] = value * (2.0 / RADIUS) - ts[k - 2][z]

            def grow_all(k, lo, hi):
                lax.fori_loop(lo, hi, lambda z, carry: grow(k, z) or carry, 0, unroll=hi - lo if hi - lo == 4 else 2)

            def add_up(terms, count):
                def plane(z, sums):
                    return tuple(s + fold(term) for s, term in zip(sums, terms(z)))

                sums = lax.fori_loop(first, last, plane, (jnp.zeros((8, width), jnp.float32),) * count, unroll=2)
                return [jnp.sum(total, axis=0, keepdims=True) for total in sums]

            def near_terms(z):
                x0, x1, x2 = (ref[z] for ref in ts[:3])
                return x0 * x0, x0 * x1, x1 * x1, x1 * x2, x2 * x2

            def far_terms(z):
                x2, x3 = a2[z], a3[z]
                image = (coef[z] - (CENTRE - 6.0)) * x3 - 2.0 * a3[z + 1] - in_plane(x3)
                return x2 * x3, x3 * x3, x3 * image * (1.0 / RADIUS)

            arrive_near()
            grow_all(1, first - 1, last + 1)
            clear(a1)
            grow_all(2, first, last)
            sums = add_up(near_terms, 5)
            arrive_far()
            for z in (first - 3, first - 2, last + 1, last + 2):
                grow(1, z)
            for z in (first - 2, first - 1, last, last + 1):
                grow(2, z)
            clear(a2)
            grow_all(3, first, last)
            grow(3, first - 1)
            grow(3, last)
            clear(a3)
            sums += add_up(far_terms, 3)
            hear(len(rounds))

            def everywhere(slot, sums, meanwhile):
                for k in range(8):
                    sums_ref[pl.ds(k, 1), :] = sums[k]
                packed = pack(sums_ref[...])
                packed_ref[slot] = packed
                for index, (_, shift) in enumerate(partners):
                    pltpu.make_async_remote_copy(
                        src_ref=packed_ref.at[slot], dst_ref=gather.at[slot, pl.ds(index, 1)],
                        send_sem=sum_send.at[slot], recv_sem=sum_recv.at[slot],
                        device_id=(sec, partner(shift)), device_id_type=MESH,
                    ).start()
                meanwhile()
                others = gather.at[slot, pl.ds(0, n_slab - 1)]
                pltpu.make_async_copy(others, others, sum_recv.at[slot]).wait()
                return packed + jnp.sum(gather[slot, : n_slab - 1, :], axis=0, keepdims=True)

            c, again = coefficients(everywhere(2 * which, sums, meanwhile))

            def left_over(z):
                x0, x1, x2, x3 = (ref[z] for ref in ts)
                image = (coef[z] - (CENTRE - 6.0)) * x3 - ((a3[z - 1] + a3[z + 1]) + in_plane(x3))
                moved = c[0] * x1 + 0.5 * (c[1] * (x2 + x0) + c[2] * (x3 + x1)) + c[3] * (image * (1.0 / RADIUS))
                at = (c[0] * x0 + c[1] * x1) + (c[2] * x2 + c[3] * x3)
                residual = x0 - CENTRE * at - RADIUS * moved
                return x0 * residual, x1 * residual, x2 * residual, x3 * residual

            rest = add_up(left_over, 4)
            change = again(unpack(everywhere(2 * which + 1, rest + rest, lambda: None))[:BASIS])
            c = [value + more for value, more in zip(c, change)]
            then(c)

            def combine(z, carry):
                out[z - first] = (c[0] * ts[0][z] + c[1] * ts[1][z]) + (c[2] * ts[2][z] + c[3] * ts[3][z])
                return carry

            lax.fori_loop(first, last, combine, 0, unroll=2)

        def arrive_near():
            pick_basis(0)
            hear(1)
            wait_recv(dual_near)
            wait_recv(coef_near)

        def arrive_far():
            pick_basis(1)
            pick_basis(2)
            hear(2)
            wait_recv(coef_far)
            wait_recv(dual_far)
            start(heat_halo)

        sends = []

        def send_back(c):
            weights[...] = jnp.concatenate(c + c, axis=0)
            for m in ahead:
                send = pltpu.make_async_remote_copy(
                    src_ref=weights, dst_ref=weights_in.at[mine], send_sem=row_send.at[m], recv_sem=weight_recv.at[mine],
                    device_id=(m, slab), device_id_type=MESH,
                )
                only(mine, ahead[m], ingots, send.start)
            for z in range(depth):
                back[z] = (c[0] * basis_rows[0, z] + c[1] * basis_rows[1, z]) + (
                    c[2] * basis_rows[2, z] + c[3] * basis_rows[3, z]
                )
            pl.semaphore_wait(ready, melts - early + lead)
            for index, (j, m) in enumerate(relayed):

                @pl.when(mine == j)
                def _():
                    pltpu.make_async_remote_copy(
                        src_ref=back.at[:, slot_rows(m), :], dst_ref=relay.at[index], send_sem=row_send.at[m],
                        recv_sem=relay_recv.at[index], device_id=(early, slab), device_id_type=MESH,
                    ).start()

            for m in range(melts):
                direct = [j for j in range(ingots) if (j, m) not in relayed and j not in ahead.get(m, [])]
                send = pltpu.make_async_remote_copy(
                    src_ref=back.at[:, slot_rows(m), :],
                    dst_ref=returned.at[pl.ds(first, depth), pl.ds(pl.multiple_of(mine * PAIRCAP, PAIRCAP), PAIRCAP), :],
                    send_sem=row_send.at[m], recv_sem=row_recv.at[mine], device_id=(m, slab), device_id_type=MESH,
                )
                only(mine, direct, ingots, send.start)
                sends.append((m, send))

        solve(0, dual, adjoint_ref, arrive_near, arrive_far, lambda: pick_basis(3), send_back)

        passed = []
        for m in range(melts):
            region = slots.at[pl.ds(first, depth), slot_rows(m)]
            pltpu.make_async_copy(region, region, row_recv.at[m]).wait()
            passed.append(pass_on(slots, slot_rows(m), m))

        def load_up(at):
            for z in range(at, at + depth):
                rows = jnp.dot(place, slots[z], precision=HIGHEST, preferred_element_type=jnp.float32)
                heat[z, pl.ds(0, contact), :] = heat[z, pl.ds(0, contact), :] + rows

        wait_recv(heat_halo)
        load_up(first)

        @pl.when(has_left)
        def _():
            take(slots, 0)
            load_up(0)

        @pl.when(has_right)
        def _():
            take(slots, 1)
            load_up(last)

        solve(1, heat, state_ref, lambda: None, lambda: None, lambda: None, lambda c: None)

        for pair in [dual_near, coef_near, dual_far, coef_far, heat_halo] + passed:
            wait_send(pair)
        for m, send in early_sends:
            only(mine, ahead[m], ingots, send.wait_send)
        for m, send in sends:
            summed = ahead.get(m, [])
            only(mine, summed, ingots, lambda m=m: pltpu.make_async_copy(weights, weights, row_send.at[m]).wait())
            only(mine, [j for j in range(ingots) if j not in summed], ingots, send.wait_send)
        for which in range(4):
            others = gather.at[which, pl.ds(0, n_slab - 1)]
            pltpu.make_async_copy(others, others, sum_send.at[which]).wait()


def body(n_sec, n_slab, heat_level, material_factor, dual_sensitivity, part, line, flag, instant):
    ingots, contact = line.shape
    melts = n_sec - ingots
    _, depth, height, width = heat_level.shape
    f32 = jnp.float32
    wide = pltpu.VMEM((3 * depth, height, width), f32)
    table = pltpu.VMEM((ingots, contact), jnp.int32)
    dma = pltpu.SemaphoreType.DMA
    most = max(melts, ingots)
    scratch = [
        table, table, table,
        wide, wide, wide, wide, wide, wide,
        pltpu.VMEM((STEPS, 3 * depth, height, width), f32),
        wide, wide, wide, wide, wide, wide, wide,
        pltpu.VMEM((ingots * PAIRCAP, height), f32),
        pltpu.VMEM((height, ingots * PAIRCAP), f32),
        pltpu.VMEM((depth, ingots * PAIRCAP, width), f32),
        pltpu.VMEM((3 * depth, melts * PAIRCAP, width), f32),
        pltpu.VMEM((depth, melts * PAIRCAP, width), f32),
        pltpu.VMEM((BASIS, depth, melts * PAIRCAP, width), f32),
        pltpu.VMEM((max(len(relays(n_sec, ingots)), 1), depth, PAIRCAP, width), f32),
        pltpu.VMEM((BASIS, depth, ingots * PAIRCAP, width), f32),
        pltpu.VMEM((8, width), f32),
        pltpu.VMEM((ingots, 8, width), f32),
        pltpu.VMEM((3 * depth, ingots * PAIRCAP, width), f32),
        pltpu.VMEM((8, width), f32),
        pltpu.VMEM((4, 1, width), f32),
        pltpu.VMEM((4, n_slab, width), f32),
        dma((6,)), dma((5, 2)), dma((5, 2)),
        dma((most,)), dma((most,)), dma((2, most)), dma((2,)),
        dma((4,)), dma((4,)), pltpu.SemaphoreType.REGULAR, pltpu.SemaphoreType.REGULAR((4,)),
        dma((8,)), dma((8,)), dma((4, BASIS)), dma((ingots,)), dma((ingots,)),
    ]
    hbm, vmem, smem = (pl.BlockSpec(memory_space=s) for s in (pltpu.HBM, pltpu.VMEM, pltpu.SMEM))
    fields = (part[:, :, 0], line, flag, heat_level[0], material_factor[0], dual_sensitivity[0])
    fields = [pltpu.with_memory_space_constraint(field, pltpu.HBM) for field in fields]
    both = pl.pallas_call(
        functools.partial(kernel, n_sec, n_slab),
        out_shape=jax.ShapeDtypeStruct((2, depth, height, width), f32),
        in_specs=[hbm, hbm, hbm, smem, hbm, hbm, hbm],
        out_specs=vmem,
        scratch_shapes=scratch,
        compiler_params=pltpu.CompilerParams(
            collective_id=0, has_side_effects=True, vmem_limit_bytes=32 * 1024 * 1024
        ),
    )(*fields[:3], instant, *fields[3:])
    return both[0:1], both[1:2]


def solution(mesh):
    n_sec, n_slab = mesh.shape["sec"], mesh.shape["slab"]
    fields = P("sec", "slab", None, None)
    return jax.shard_map(
        functools.partial(body, n_sec, n_slab),
        mesh=mesh,
        in_specs=(fields, fields, fields, P(), P(), P(), P()),
        out_specs=(fields, fields),
        check_vma=False,
    )
```
